32 devices in a mesh: wide: 8 (over z, x), narrow: 4 (over y, core).
Axes of the slice: x: 2, y: 2, z: 4, core: 2. Of those that a mesh axis runs over, the one named last changes fastest.
Arguments:
- images: bfloat16 [32, 16, 16, 2048], P(('wide', 'narrow')), may hold values from -18 to 18
- image_sizes: int32 [32, 2], P(('wide', 'narrow')), may hold values from 8 to 16
- offset_shift: int32 [18], replicated, may hold values from -24 to 24, as said below
- squeeze_one: bfloat16 [2048, 512], replicated, may hold values from -0.125 to 0.125
- offsets_one: bfloat16 [9, 512, 18], replicated, may hold values from -0.09375 to 0.09375
- spatial_one: bfloat16 [9, 512, 512], replicated, may hold values from -0.09375 to 0.09375
- expand_one: bfloat16 [512, 2048], replicated, may hold values from -0.25 to 0.25
- squeeze_two: bfloat16 [2048, 512], replicated, may hold values from -0.125 to 0.125
- spatial_two: bfloat16 [9, 512, 512], replicated, may hold values from -0.09375 to 0.09375
- expand_two: bfloat16 [512, 2048], replicated, may hold values from -0.25 to 0.25
- norm_gain_one: float32 [3072], replicated, may hold values from 0.5 to 1.5
- norm_bias_one: float32 [3072], replicated, may hold values from -1.5 to 1.5
- norm_gain_two: float32 [3072], replicated, may hold values from 0.5 to 1.5
- norm_bias_two: float32 [3072], replicated, may hold values from -1.5 to 1.5
- run_mean_one: float32 [3072], replicated, may hold values from -3 to 3
- run_var_one: float32 [3072], replicated, may hold values from 0.5 to 2
- run_mean_two: float32 [3072], replicated, may hold values from -3 to 3
- run_var_two: float32 [3072], replicated, may hold values from 0.5 to 2
- grad_output: bfloat16 [32, 16, 16, 2048], P(('wide', 'narrow')), may hold values from -6 to 6
Outputs:
- output_images: bfloat16 [32, 16, 16, 2048], P(('wide', 'narrow'))
- grad_images: bfloat16 [32, 16, 16, 2048], P(('wide', 'narrow'))
- grad_squeeze_one: float32 [2048, 512], P(None, 'wide')
- grad_offsets_one: float32 [9, 512, 18], replicated
- grad_spatial_one: float32 [9, 512, 512], P(None, 'wide')
- grad_expand_one: float32 [512, 2048], P('wide')
- grad_squeeze_two: float32 [2048, 512], P(None, 'wide')
- grad_spatial_two: float32 [9, 512, 512], P(None, 'wide')
- grad_expand_two: float32 [512, 2048], P('wide')
- grad_gain_one: float32 [3072], replicated
- grad_bias_one: float32 [3072], replicated
- grad_gain_two: float32 [3072], replicated
- grad_bias_two: float32 [3072], replicated
- new_mean_one: float32 [3072], replicated
- new_var_one: float32 [3072], replicated
- new_mean_two: float32 [3072], replicated
- new_var_two: float32 [3072], replicated
The draws below stay inside these ranges and needn't reach their ends.
Inputs may be any that keep to these rules, and one draw needn't show every extreme that they name: `offset_shift`: every entry is -2 to 2 except the vertical shifts of two different taps, one 24 and the other -24.
All inputs are finite; a program needn't handle non-finite values.
Results may differ from the reference program's by a relative error of at most 0.024.
Values sent between devices are 32-bit elements; how exact they have to be, the bound alone decides.
No kernel may reach another device: no remote copies, remote signals or barrier semaphores. Data moves between devices by JAX's collectives and lax.ppermute only.
A program may use at most 192 MiB of HBM per device.

```python
import math
import jax
import jax.numpy as jnp
from jax import lax

D = 2048
MID = 512
OFFS = 18
SIDE = 16
IMAGES = 32


def draw_images(key, part):
    key = jax.random.fold_in(key, 11)
    base_key, jitter_key, shift_key = jax.random.split(key, 3)
    position = jnp.arange(IMAGES, dtype=jnp.float32)
    rising = jnp.exp(jnp.log(3.0) * position / max(IMAGES - 1, 1))
    jitter = jnp.exp(jax.random.uniform(jitter_key, (IMAGES,), minval=-0.2, maxval=0.2))
    scaling = (rising * jitter)[:, None, None, None]
    base_values = jnp.clip(jax.random.normal(base_key, (IMAGES, SIDE, SIDE, D)), -4.0, 4.0)
    common = 0.2 * jnp.clip(jax.random.normal(shift_key, (IMAGES, 1, 1, D)), -4.0, 4.0)
    return ((base_values + common) * scaling).astype(jnp.bfloat16)


def draw_offset_shift(key, part):
    key = jax.random.fold_in(key, 23)
    near_key, tap_key = jax.random.split(key, 2)
    nearby = jax.random.randint(near_key, (18,), -2, 3)
    order = jax.random.permutation(tap_key, 9)
    channel = jnp.arange(18, dtype=jnp.int32)
    shifted = jnp.where(channel == 2 * order[0], 24, nearby)
    shifted = jnp.where(channel == 2 * order[1], -24, shifted)
    return shifted.astype(jnp.int32)


def touch_ends(values, own_key, smallest, top_value):
    longest = values.shape.index(max(values.shape))
    spots = []
    for shift in (0, 1):
        where = [jax.random.randint(jax.random.fold_in(own_key, axis), (), 0, length) for axis, length in enumerate(values.shape)]
        where[longest] = (where[longest] + shift) % values.shape[longest]
        spots.append(tuple(where))
    return values.at[spots[0]].set(smallest).at[spots[1]].set(top_value)


def levels(own_key, extent, cuts, smallest, high):
    def one(axis_at, blocks):
        heights = jax.random.uniform(jax.random.fold_in(jax.random.fold_in(own_key, 6), axis_at), (blocks,), jnp.float32, smallest / len(cuts), high / len(cuts))
        return jnp.repeat(jnp.exp(heights), extent[axis_at] // blocks).reshape((-1,) + (1,) * (len(extent) - axis_at - 1))

    factor_of = one(*cuts[0])
    for cut in cuts[1:]:
        factor_of = factor_of * one(*cut)
    return factor_of


def scatter_about(rng, extent, scale, bound, cuts=(), kind=jnp.bfloat16):
    values = scale * jax.random.normal(rng, extent, jnp.float32)
    if cuts:
        values = values * levels(rng, extent, cuts, -0.22, 0.18)
    return jnp.clip(values, -bound, bound).astype(kind)


def setup_inputs(seed: int = 0) -> dict:
    splits = jax.random.split(jax.random.key(seed), 20)
    return {
        "images": draw_images(jax.random.fold_in(splits[19], 71), 0),
        "image_sizes": touch_ends(jax.random.randint(splits[1], (IMAGES, 2), SIDE // 2, SIDE + 1), jax.random.fold_in(splits[1], 1), SIDE // 2, SIDE).astype(jnp.int32),
        "offset_shift": draw_offset_shift(jax.random.fold_in(splits[19], 71), 0),
        "squeeze_one": scatter_about(splits[3], (D, MID), D ** -0.5, 0.125),
        "offsets_one": scatter_about(splits[4], (9, MID, OFFS), (9 * MID) ** -0.5, 0.09375),
        "spatial_one": scatter_about(splits[5], (9, MID, MID), (9 * MID) ** -0.5, 0.09375),
        "expand_one": scatter_about(splits[6], (MID, D), MID ** -0.5, 0.25),
        "squeeze_two": scatter_about(splits[7], (D, MID), D ** -0.5, 0.125),
        "spatial_two": scatter_about(splits[8], (9, MID, MID), (9 * MID) ** -0.5, 0.09375),
        "expand_two": scatter_about(splits[9], (MID, D), MID ** -0.5, 0.25),
        "norm_gain_one": jnp.clip(1.0 + 0.1 * jax.random.normal(splits[10], (2 * MID + D,), jnp.float32), 0.5, 1.5),
        "norm_bias_one": scatter_about(splits[11], (2 * MID + D,), 0.3, 1.5, (), jnp.float32),
        "norm_gain_two": jnp.clip(1.0 + 0.1 * jax.random.normal(splits[12], (2 * MID + D,), jnp.float32), 0.5, 1.5),
        "norm_bias_two": scatter_about(splits[13], (2 * MID + D,), 0.3, 1.5, (), jnp.float32),
        "run_mean_one": scatter_about(splits[14], (2 * MID + D,), 0.5, 3.0, (), jnp.float32),
        "run_var_one": jnp.clip(jnp.exp(jax.random.uniform(splits[15], (2 * MID + D,), jnp.float32, math.log(0.5), math.log(2.0))), 0.5, 2.0),
        "run_mean_two": scatter_about(splits[16], (2 * MID + D,), 0.5, 3.0, (), jnp.float32),
        "run_var_two": jnp.clip(jnp.exp(jax.random.uniform(splits[17], (2 * MID + D,), jnp.float32, math.log(0.5), math.log(2.0))), 0.5, 2.0),
        "grad_output": scatter_about(splits[18], (IMAGES, SIDE, SIDE, D), 1.0, 6.0, ((0, 32),)),
    }


@jax.custom_vjp
def low(v):
    return lax.optimization_barrier(v.astype(jnp.bfloat16)).astype(jnp.float32)

@jax.custom_vjp
def low_back(v):
    return v

def low_keep(v):
    return (low(v), None)

def low_pass(kept, grad):
    return (grad,)

def back_keep(v):
    return (v, None)

def back_low(kept, grad):
    return (low(grad),)
low.defvjp(low_keep, low_pass)
low_back.defvjp(back_keep, back_low)
exact_dots = lax.Precision.HIGHEST
eps_norm = 1e-05
keep_rate = 0.6

def expand_taps(values):
    side_rows, side_cols = (values.shape[0], values.shape[1])
    padded = jnp.pad(values, ((2, 2), (2, 2), (0, 0)))
    pieces = [padded[2 * tap_row:2 * tap_row + side_rows, 2 * tap_col:2 * tap_col + side_cols, :] for tap_row in range(3) for tap_col in range(3)]
    return jnp.concatenate(pieces, axis=2).reshape(side_rows * side_cols, -1)

def tap_distances(offsets, tap_index, side_rows, side_cols):
    tap_row, tap_col = (tap_index // 3, tap_index % 3)
    position = jnp.arange(side_rows * side_cols, dtype=jnp.int32)
    row_base = (position // side_cols).astype(jnp.float32) + 2.0 * (tap_row - 1)
    col_base = (position % side_cols).astype(jnp.float32) + 2.0 * (tap_col - 1)
    dist_y = (row_base + offsets[:, 2 * tap_index])[:, None] - jnp.arange(side_rows, dtype=jnp.float32)[None, :]
    dist_x = (col_base + offsets[:, 2 * tap_index + 1])[:, None] - jnp.arange(side_cols, dtype=jnp.float32)[None, :]
    return (dist_y, dist_x)

def smooth_kernel(dist):
    bump = jax.nn.relu(1.0 - dist * dist)
    return bump * bump

def plain_image(one_image, spatial):
    middle = one_image.shape[2]
    return jnp.dot(expand_taps(one_image), spatial.reshape(9 * middle, middle), precision=exact_dots)

def deform_image(one_image, offset_weights, spatial, shift_float):
    side_rows, side_cols, middle = one_image.shape
    taps_all = expand_taps(one_image)
    offsets = low_back(jnp.dot(taps_all, offset_weights.reshape(9 * middle, -1), precision=exact_dots)) + shift_float
    flat_values = one_image.reshape(side_rows * side_cols, middle)
    samples = []
    for tap_index in range(9):
        dist_y, dist_x = tap_distances(offsets, tap_index, side_rows, side_cols)
        weight_y = smooth_kernel(dist_y)
        weight_x = smooth_kernel(dist_x)
        sampling = (weight_y[:, :, None] * weight_x[:, None, :]).reshape(side_rows * side_cols, -1)
        samples.append(jnp.dot(sampling, flat_values, precision=exact_dots))
    columns = low(jnp.concatenate(samples, axis=1))
    return jnp.dot(columns, spatial.reshape(9 * middle, middle), precision=exact_dots)

def norm_apply(pre_norm, valid_mask, pixel_count, gain_part, bias_part):
    sum_values = lax.optimization_barrier(jnp.sum(valid_mask * pre_norm, axis=(0, 1)))
    squares = lax.optimization_barrier(jnp.sum(valid_mask * pre_norm * pre_norm, axis=(0, 1)))
    mean_value = sum_values / pixel_count
    var_value = squares / pixel_count - mean_value * mean_value
    normed = (pre_norm - mean_value) * lax.rsqrt(var_value + eps_norm)
    return (gain_part * normed + bias_part, mean_value, var_value)

def block(inputs, squeeze, spatial, expand, gain_all, bias_all, valid_mask, pixel_count, offset_weights, shift_float):
    image_count = inputs.shape[0]
    middle = squeeze.shape[1]
    pre_first = low_back(jnp.einsum('bpd,de->bpe', low(inputs), squeeze, precision=exact_dots))
    out_first, mean_first, var_first = norm_apply(pre_first, valid_mask, pixel_count, gain_all[:middle], bias_all[:middle])
    act_first = low(jax.nn.silu(out_first) * valid_mask)
    grid_act = act_first.reshape(image_count, SIDE, SIDE, middle)
    if offset_weights is None:
        plain_fn = jax.checkpoint(plain_image)
        pre_second = lax.map(lambda one_image: plain_fn(one_image, spatial), grid_act)
    else:
        deform_fn = jax.checkpoint(deform_image)
        pre_second = lax.map(lambda one_image: deform_fn(one_image, offset_weights, spatial, shift_float), grid_act)
    pre_second = low_back(pre_second)
    out_second, mean_second, var_second = norm_apply(pre_second, valid_mask, pixel_count, gain_all[middle:2 * middle], bias_all[middle:2 * middle])
    act_second = low(jax.nn.silu(out_second) * valid_mask)
    pre_third = low_back(jnp.einsum('bpe,ed->bpd', act_second, expand, precision=exact_dots))
    out_third, mean_third, var_third = norm_apply(pre_third, valid_mask, pixel_count, gain_all[2 * middle:], bias_all[2 * middle:])
    result = jax.nn.silu(out_third + inputs) * valid_mask
    means = jnp.concatenate([mean_first, mean_second, mean_third])
    variances = jnp.concatenate([var_first, var_second, var_third])
    return (result, means, variances)

def reference(images, image_sizes, offset_shift, squeeze_one, offsets_one, spatial_one, expand_one, squeeze_two, spatial_two, expand_two, norm_gain_one, norm_bias_one, norm_gain_two, norm_bias_two, run_mean_one, run_var_one, run_mean_two, run_var_two, grad_output):
    pixels = SIDE * SIDE
    position = jnp.arange(pixels, dtype=jnp.int32)
    inside = (position[None, :] // SIDE < image_sizes[:, 0:1]) & (position[None, :] % SIDE < image_sizes[:, 1:2])
    valid_mask = inside.astype(jnp.float32)[:, :, None]
    pixel_count = jnp.sum(valid_mask)
    shift_float = offset_shift.astype(jnp.float32)
    images_flat = images.astype(jnp.float32).reshape(IMAGES, pixels, D)
    grad_flat = grad_output.astype(jnp.float32).reshape(IMAGES, pixels, D)

    def forward(images_in, sq_one, off_one, sp_one, ex_one, sq_two, sp_two, ex_two, gain_one, bias_one, gain_two, bias_two):
        first, means_one, vars_one = block(images_in, sq_one, sp_one, ex_one, gain_one, bias_one, valid_mask, pixel_count, off_one, shift_float)
        second, means_two, vars_two = block(first, sq_two, sp_two, ex_two, gain_two, bias_two, valid_mask, pixel_count, None, shift_float)
        return (second, (means_one, vars_one, means_two, vars_two))
    params = (images_flat, squeeze_one.astype(jnp.float32), offsets_one.astype(jnp.float32), spatial_one.astype(jnp.float32), expand_one.astype(jnp.float32), squeeze_two.astype(jnp.float32), spatial_two.astype(jnp.float32), expand_two.astype(jnp.float32), norm_gain_one, norm_bias_one, norm_gain_two, norm_bias_two)
    block_output, pullback, aux_stats = jax.vjp(forward, *params, has_aux=True)
    grads = pullback(grad_flat)
    means_one, vars_one, means_two, vars_two = aux_stats
    unbias = pixel_count / (pixel_count - 1.0)
    new_mean_one = keep_rate * run_mean_one + (1.0 - keep_rate) * means_one
    new_var_one = keep_rate * run_var_one + (1.0 - keep_rate) * vars_one * unbias
    new_mean_two = keep_rate * run_mean_two + (1.0 - keep_rate) * means_two
    new_var_two = keep_rate * run_var_two + (1.0 - keep_rate) * vars_two * unbias
    output_images = block_output.astype(jnp.bfloat16).reshape(IMAGES, SIDE, SIDE, D)
    grad_images = grads[0].astype(jnp.bfloat16).reshape(IMAGES, SIDE, SIDE, D)
    return (output_images, grad_images, grads[1], grads[2], grads[3], grads[4], grads[5], grads[6], grads[7], grads[8], grads[9], grads[10], grads[11], new_mean_one, new_var_one, new_mean_two, new_var_two)
```

```python
import functools

import jax
import jax.numpy as jnp
from jax import lax
from jax.experimental import pallas as pl
from jax.experimental.pallas import tpu as pltpu
from jax.sharding import PartitionSpec as P

eps_norm = 1e-05
keep_rate = 0.6
vmem_bytes = 60 * 1024 * 1024
lane = 128
tile_rows = 16
axes = ("wide", "narrow")
f32 = jnp.float32
bf16 = jnp.bfloat16


def shape_of(shape, kind=f32):
    return jax.ShapeDtypeStruct(shape, kind)


copies_of = {}


def need(ref):
    entry = copies_of.get(id(ref))
    if entry is not None and entry[1]:
        entry[1] = False
        entry[0].wait()
    return ref


def flush(ref):
    entry = copies_of.get(id(ref))
    if entry is not None and entry[1]:
        entry[1] = False
        entry[0].start()


def call(body, outs, args, smem=(), scratch=(), after=(), late=(), stay=None, stay_out=()):
    stay = () if stay is None else stay
    hbm = pl.BlockSpec(memory_space=pltpu.HBM)
    vmem = pl.BlockSpec(memory_space=pltpu.VMEM)
    specs = [
        pl.BlockSpec(memory_space=pltpu.SMEM) if place in smem else vmem if place in stay else hbm
        for place in range(len(args))
    ] + [pl.BlockSpec(memory_space=pl.ANY)] * len(after)
    moved = [place for place in range(len(args)) if place not in smem and place not in stay]
    used, extra, made = (len(args), len(after), len(outs))
    sent = [slot for slot in range(made) if slot not in stay_out]

    def kernel(*refs):
        given = list(refs[:used])
        results = list(refs[used + extra : used + extra + made])
        rest = refs[used + extra + made :]
        in_slots, out_slots = (rest[: len(moved)], rest[len(moved) : len(moved) + len(sent)])
        in_flags, out_flags = rest[len(moved) + len(sent) : len(moved) + len(sent) + 2]
        copies_of.clear()
        for slot, place in enumerate(moved):
            copy = pltpu.make_async_copy(given[place], in_slots[slot], in_flags.at[slot])
            copy.start()
            copies_of[id(in_slots[slot])] = [copy, True]
            given[place] = in_slots[slot]
        for place in moved:
            if place not in late:
                need(given[place])
        for slot, place in enumerate(sent):
            copies_of[id(out_slots[slot])] = [
                pltpu.make_async_copy(out_slots[slot], results[place], out_flags.at[slot]), True
            ]
            results[place] = out_slots[slot]
        body(*given, *results, *rest[len(moved) + len(sent) + 2 :])
        for place in moved:
            need(given[place])
        for slot in out_slots:
            if copies_of[id(slot)][1]:
                flush(slot)
        for slot in out_slots:
            copies_of[id(slot)][0].wait()
        copies_of.clear()

    slots = [pltpu.VMEM(args[place].shape, args[place].dtype) for place in moved]
    slots += [pltpu.VMEM(outs[place].shape, outs[place].dtype) for place in sent]
    flags = [pltpu.SemaphoreType.DMA((max(len(moved), 1),)), pltpu.SemaphoreType.DMA((max(len(sent), 1),))]
    return pl.pallas_call(
        kernel,
        out_shape=tuple(outs),
        in_specs=specs,
        out_specs=tuple(vmem if place in stay_out else hbm for place in range(made)),
        scratch_shapes=slots + flags + list(scratch),
        compiler_params=pltpu.CompilerParams(vmem_limit_bytes=vmem_bytes),
    )(*args, *after)


def dot_nn(first_op, second_op):
    return lax.dot_general(
        first_op, second_op, (((1,), (0,)), ((), ())), preferred_element_type=f32
    )


def dot_nt(first_op, second_op):
    return lax.dot_general(
        first_op, second_op, (((1,), (1,)), ((), ())), preferred_element_type=f32
    )


def dot_tn(first_op, second_op):
    return lax.dot_general(
        first_op, second_op, (((0,), (0,)), ((), ())), preferred_element_type=f32
    )


def logistic(values):
    return 0.5 * jnp.tanh(0.5 * values) + 0.5


def silu(values):
    return values * logistic(values)


def silu_slope(values):
    gate = logistic(values)
    return gate * (1.0 + values * (1.0 - gate))


def flat_row(rows, start, width):
    first = start // lane
    return jnp.concatenate(
        [rows[first + step : first + step + 1, :] for step in range(width // lane)], axis=1
    )


def fold_row(row):
    return [row[:, step * lane : (step + 1) * lane] for step in range(row.shape[1] // lane)]


def write_copies(copies_ref, rows, extra=None):
    packed = jnp.concatenate([piece for row in rows for piece in fold_row(row)], axis=0)
    if extra is not None:
        packed = jnp.concatenate([packed, extra], axis=0)

    def one_copy(step, carry):
        copies_ref[step] = packed
        return carry

    lax.fori_loop(0, copies_ref.shape[0], one_copy, 0)


def read_copies(copies_ref):
    return jnp.sum(copies_ref[...], axis=0)


def wide_mask(mask_ref, rows, width):
    return jnp.concatenate([mask_ref[rows, :]] * (width // lane), axis=1)


def eight_rows(values):
    folded = values[:8]
    for start in range(8, values.shape[0], 8):
        folded = folded + values[start : start + 8]
    return folded


def row_loop(pixels, body, carry):
    def step(index, state):
        return body(pl.ds(pl.multiple_of(index * tile_rows, tile_rows), tile_rows), state)

    return lax.fori_loop(0, pixels // tile_rows, step, carry)


def two_sums(pixels, width, body):
    zero = jnp.zeros((8, width), f32)

    def step(rows, state):
        first, second = body(rows)
        return (state[0] + eight_rows(first), state[1] + eight_rows(second))

    first, second = row_loop(pixels, step, (zero, zero))
    return (jnp.sum(first, axis=0, keepdims=True), jnp.sum(second, axis=0, keepdims=True))


def moments(total, width, count):
    mean = flat_row(total, 0, width) / count
    var = flat_row(total, width, width) / count - mean * mean
    return (mean, var)


def scale_shift(mean, var, gain, bias):
    inverse = lax.rsqrt(var + eps_norm)
    scale = gain * inverse
    return (scale, bias - mean * scale)


def spans_of(width, block):
    return [(start, min(block, width - start)) for start in range(0, width, block)]


def grad_rows(total, stats, gain, count, width):
    mean, var = (stats[0:1], stats[1:2])
    inverse = lax.rsqrt(var + eps_norm)
    sum_grad = flat_row(total, 0, width)
    sum_prod = flat_row(total, width, width)
    return (
        gain * inverse,
        sum_grad / count,
        inverse * sum_prod / count,
        mean,
        sum_grad,
        sum_prod,
    )


def build_taps(act_ref, shifted_ref, pixels, side):
    pad = 2 * side
    width = act_ref.shape[1]
    column = lax.broadcasted_iota(jnp.int32, (pixels, lane), 0) % side
    for tap_col in range(3):
        move = 2 * (tap_col - 1)
        moved = act_ref[pl.ds(pad + move, pixels), :]
        if move:
            inside = (column + move >= 0) & (column + move < side)
            keep = jnp.concatenate([inside.astype(f32)] * (width // lane), axis=1)
            moved = moved * keep
        shifted_ref[tap_col, pl.ds(0, pad), :] = jnp.zeros((pad, width), bf16)
        shifted_ref[tap_col, pl.ds(pad + pixels, pad), :] = jnp.zeros((pad, width), bf16)
        shifted_ref[tap_col, pl.ds(pad, pixels), :] = moved.astype(bf16)


def tap_of(shifted_ref, tap_index, pixels, side):
    tap_row, tap_col = (tap_index // 3, tap_index % 3)
    return shifted_ref[tap_col, pl.ds(2 * side * tap_row, pixels), :]


def fold_columns(sums_ref, pixels, side):
    pad = 2 * side
    width = sums_ref.shape[2]
    column = lax.broadcasted_iota(jnp.int32, (pixels, lane), 0) % side
    total = sums_ref[1, pl.ds(pad, pixels), :]
    for tap_col in (0, 2):
        move = 2 * (tap_col - 1)
        inside = (column - move >= 0) & (column - move < side)
        keep = jnp.concatenate([inside.astype(f32)] * (width // lane), axis=1)
        total = total + keep * sums_ref[tap_col, pl.ds(pad - move, pixels), :]
    return total


def tap_rows_out(sums_ref, tap_index, pixels, side, values):
    tap_row, tap_col = (tap_index // 3, tap_index % 3)
    rows = pl.ds(2 * side * tap_row, pixels)
    sums_ref[tap_col, rows, :] = sums_ref[tap_col, rows, :] + values


def tap_factors(offsets, tap_index, side):
    pixels = offsets.shape[0]
    tap_row, tap_col = (tap_index // 3, tap_index % 3)
    shape = (pixels, pixels)
    position = lax.broadcasted_iota(jnp.int32, shape, 0)
    source = lax.broadcasted_iota(jnp.int32, shape, 1)
    gap_y = (position // side - source // side + 2 * (tap_row - 1)).astype(f32)
    gap_x = (position % side - source % side + 2 * (tap_col - 1)).astype(f32)
    dist_y = gap_y + offsets[:, 2 * tap_index : 2 * tap_index + 1]
    dist_x = gap_x + offsets[:, 2 * tap_index + 1 : 2 * tap_index + 2]
    bump_y = jnp.maximum(1.0 - dist_y * dist_y, 0.0)
    bump_x = jnp.maximum(1.0 - dist_x * dist_x, 0.0)
    return (dist_y, dist_x, bump_y, bump_x)


def first_body(sizes_ref, place_ref, images_ref, squeeze_ref, pre_ref, mask_ref, copies_ref, half_ref):
    pixels, width = pre_ref.shape
    side = 1 << ((pixels.bit_length() - 1) // 2)
    position = lax.broadcasted_iota(jnp.int32, (pixels, lane), 0)
    inside = (position // side < sizes_ref[0, 0]) & (position % side < sizes_ref[0, 1])
    mask = inside.astype(f32)
    mask_ref[...] = mask
    pre_ref[...] = dot_nn(images_ref[...], squeeze_ref[...])

    def both(rows):
        values = pre_ref[rows, :]
        masked = values * wide_mask(mask_ref, rows, width)
        return (masked, masked * values)

    sums = two_sums(pixels, width, both)
    amount = jnp.sum(mask, axis=0, keepdims=True)
    write_copies(copies_ref, sums, jnp.broadcast_to(amount, (8, lane)))
    half = half_ref.shape[1]
    other = pl.multiple_of((1 - place_ref[0, 0]) * half, lane)
    half_ref[...] = images_ref[:, pl.ds(other, half)].astype(f32)


def activate(pre_ref, mask_ref, scale, shift, out_ref, base=0):
    pixels, width = pre_ref.shape

    def step(rows, carry):
        out = silu(pre_ref[rows, :] * scale + shift) * wide_mask(mask_ref, rows, width)
        target = pl.ds(rows.start + base, tile_rows)
        out_ref[target, :] = out.astype(bf16).astype(out_ref.dtype)
        return carry

    row_loop(pixels, step, 0)


def masked_sums(values_ref, mask_ref):
    pixels, width = values_ref.shape

    def both(rows):
        values = values_ref[rows, :]
        masked = values * wide_mask(mask_ref, rows, width)
        return (masked, masked * values)

    return two_sums(pixels, width, both)


def deform_body(
    total_ref, pre_ref, mask_ref, gain_ref, bias_ref, weights_ref, move_ref, spatial_ref,
    act_ref, columns_ref, columns_wide_ref, offsets_ref, second_ref, copies_ref, stats_ref,
    count_ref, padded_ref, shifted_ref,
):
    pixels, width = pre_ref.shape
    side = 1 << ((pixels.bit_length() - 1) // 2)
    total = read_copies(total_ref)
    count = total[2 * width // lane : 2 * width // lane + 1, 0:1]
    count_ref[...] = jnp.broadcast_to(count, (8, lane))
    mean, var = moments(total, width, count)
    stats_ref[...] = jnp.concatenate([mean, var], axis=0)
    scale, shift = scale_shift(mean, var, gain_ref[:, :width], bias_ref[:, :width])
    padded_ref[...] = jnp.zeros_like(padded_ref)
    activate(pre_ref, mask_ref, scale, shift, padded_ref, 2 * side)
    act_ref[...] = padded_ref[pl.ds(2 * side, pixels), :].astype(bf16)
    build_taps(padded_ref, shifted_ref, pixels, side)
    flush(act_ref)
    offsets = move_ref[...]
    need(weights_ref)
    for tap_index in range(9):
        taps = tap_of(shifted_ref, tap_index, pixels, side)
        offsets = offsets + dot_nn(taps, weights_ref[tap_index])
    offsets_ref[...] = offsets
    flush(offsets_ref)
    need(spatial_ref)
    second_ref[...] = jnp.zeros_like(second_ref)
    for tap_index in range(9):
        dist_y, dist_x, bump_y, bump_x = tap_factors(offsets, tap_index, side)
        root = bump_y * bump_x
        columns = dot_nn((root * root).astype(bf16), act_ref[...]).astype(bf16)
        span = pl.ds(tap_index * width, width)
        columns_ref[:, span] = columns
        columns_wide_ref[:, span] = columns.astype(f32)
        second_ref[...] = second_ref[...] + dot_nn(columns, spatial_ref[tap_index])
    flush(columns_wide_ref)
    flush(columns_ref)
    write_copies(copies_ref, masked_sums(second_ref, mask_ref))


def plain_body(
    total_ref, pre_ref, mask_ref, count_ref, gain_ref, bias_ref, spatial_ref,
    wide_ref, second_ref, copies_ref, stats_ref,
    padded_ref, shifted_ref,
):
    pixels, width = pre_ref.shape
    side = 1 << ((pixels.bit_length() - 1) // 2)
    total = read_copies(total_ref)
    mean, var = moments(total, width, count_ref[0:1, 0:1])
    stats_ref[...] = jnp.concatenate([mean, var], axis=0)
    scale, shift = scale_shift(mean, var, gain_ref[:, :width], bias_ref[:, :width])
    padded_ref[...] = jnp.zeros_like(padded_ref)
    activate(pre_ref, mask_ref, scale, shift, padded_ref, 2 * side)
    wide_ref[...] = padded_ref[pl.ds(2 * side, pixels), :]
    flush(wide_ref)
    build_taps(padded_ref, shifted_ref, pixels, side)
    need(spatial_ref)
    second_ref[...] = jnp.zeros_like(second_ref)
    for tap_index in range(9):
        taps = tap_of(shifted_ref, tap_index, pixels, side)
        second_ref[...] = second_ref[...] + dot_nn(taps, spatial_ref[tap_index])
    write_copies(copies_ref, masked_sums(second_ref, mask_ref))


def third_body(
    total_ref, pre_ref, mask_ref, count_ref, gain_ref, bias_ref, expand_ref,
    act_ref, wide_ref, third_ref, copies_ref, stats_ref,
):
    pixels, width = pre_ref.shape
    channels = third_ref.shape[1]
    total = read_copies(total_ref)
    mean, var = moments(total, width, count_ref[0:1, 0:1])
    stats_ref[...] = jnp.concatenate([mean, var], axis=0)
    scale, shift = scale_shift(
        mean, var, gain_ref[:, width : 2 * width], bias_ref[:, width : 2 * width]
    )
    activate(pre_ref, mask_ref, scale, shift, act_ref)
    wide_ref[...] = act_ref[...].astype(f32)
    flush(act_ref)
    flush(wide_ref)
    need(expand_ref)
    sums, squares = ([], [])
    for start, size in spans_of(channels, 256):
        block = dot_nn(act_ref[...], expand_ref[:, start : start + size])
        third_ref[:, start : start + size] = block
        sums.append(jnp.sum(block, axis=0, keepdims=True))
        squares.append(jnp.sum(block * block, axis=0, keepdims=True))
    flush(third_ref)
    write_copies(copies_ref, sums + squares)


def between_body(
    total_ref, pre_ref, images_ref, mask_ref, count_ref, place_ref, gain_ref, bias_ref, squeeze_ref,
    summed_ref, low_ref, half_ref, first_ref, copies_ref, stats_ref,
):
    pixels, channels = pre_ref.shape
    total = read_copies(total_ref)
    mean, var = moments(total, channels, count_ref[0:1, 0:1])
    stats_ref[...] = jnp.concatenate([mean, var], axis=0)
    begin = gain_ref.shape[1] - channels
    scale, shift = scale_shift(mean, var, gain_ref[:, begin:], bias_ref[:, begin:])
    for start, size in spans_of(channels, 512):
        span = pl.ds(start, size)

        def step(rows, carry):
            summed = (
                pre_ref[rows, span] * scale[:, start : start + size]
                + shift[:, start : start + size]
                + images_ref[rows, span].astype(f32)
            )
            summed_ref[rows, span] = summed
            low_ref[rows, span] = (silu(summed) * wide_mask(mask_ref, rows, size)).astype(bf16)
            return carry

        row_loop(pixels, step, 0)
    flush(summed_ref)
    flush(low_ref)
    need(squeeze_ref)
    sums, squares = ([], [])
    for start, size in spans_of(first_ref.shape[1], 256):
        block = dot_nn(low_ref[...], squeeze_ref[:, start : start + size])
        first_ref[:, start : start + size] = block
        sums.append(jnp.sum(block, axis=0, keepdims=True))
        squares.append(jnp.sum(block * block, axis=0, keepdims=True))
    write_copies(copies_ref, sums + squares)
    half = half_ref.shape[1]
    other = pl.multiple_of((1 - place_ref[0, 0]) * half, lane)
    half_ref[...] = low_ref[:, pl.ds(other, half)].astype(f32)


def turn_body(
    total_ref, pre_ref, before_ref, grad_ref, mask_ref, count_ref, gain_ref, bias_ref,
    image_ref, grad_sum_ref, copies_ref, stats_ref,
):
    pixels, channels = pre_ref.shape
    total = read_copies(total_ref)
    mean, var = moments(total, channels, count_ref[0:1, 0:1])
    stats_ref[...] = jnp.concatenate([mean, var], axis=0)
    begin = gain_ref.shape[1] - channels
    scale, shift = scale_shift(mean, var, gain_ref[:, begin:], bias_ref[:, begin:])
    inverse = lax.rsqrt(var + eps_norm)
    sums, prods = ([], [])
    for start, size in spans_of(channels, 512):
        span = pl.ds(start, size)
        cut = slice(start, start + size)

        def both(rows):
            mask = wide_mask(mask_ref, rows, size)
            pre = pre_ref[rows, span]
            summed = pre * scale[:, cut] + shift[:, cut] + silu(before_ref[rows, span]) * mask
            gate = logistic(summed)
            image_ref[rows, span] = (summed * gate * mask).astype(bf16)
            slope = gate * (1.0 + summed * (1.0 - gate))
            grad = grad_ref[rows, span].astype(f32) * mask * slope
            grad_sum_ref[rows, span] = grad
            return (grad, grad * ((pre - mean[:, cut]) * inverse[:, cut]))

        total_grad, total_prod = two_sums(pixels, size, both)
        sums.append(total_grad)
        prods.append(total_prod)
    flush(image_ref)
    flush(grad_sum_ref)
    write_copies(copies_ref, sums + prods)


def low_gradient(rows, width, start, grad, pre, mask, coefs):
    cut = slice(start, start + width)
    scale, mean_grad, mean_prod, mean = (part[:, cut] for part in coefs[:4])
    return scale * (grad - mask * (mean_grad + (pre - mean) * mean_prod))


def back_third_body(
    total_ref, grad_sum_ref, pre_ref, stats_ref, second_ref, second_stats_ref, mask_ref, count_ref,
    place_ref, gain_ref, bias_ref, expand_ref,
    low_ref, half_ref, grad_ref, copies_ref, result_ref,
):
    pixels, channels = pre_ref.shape
    width = second_ref.shape[1]
    total = read_copies(total_ref)
    coefs = grad_rows(
        total, stats_ref[...], gain_ref[:, 2 * width :], count_ref[0:1, 0:1], channels
    )
    result_ref[...] = jnp.concatenate(coefs[4:6], axis=0)
    for start, size in spans_of(channels, 512):
        span = pl.ds(start, size)

        def step(rows, carry):
            mask = wide_mask(mask_ref, rows, size)
            low_ref[rows, span] = low_gradient(
                rows, size, start, grad_sum_ref[rows, span], pre_ref[rows, span], mask, coefs
            ).astype(bf16)
            return carry

        row_loop(pixels, step, 0)
    half = half_ref.shape[1]
    other = pl.multiple_of((1 - place_ref[0, 0]) * half, lane)
    half_ref[...] = low_ref[:, pl.ds(other, half)].astype(f32)
    flush(low_ref)
    flush(half_ref)
    for ref in (expand_ref, second_ref, second_stats_ref):
        need(ref)
    for start, size in spans_of(width, 256):
        grad_ref[:, start : start + size] = dot_nt(low_ref[...], expand_ref[start : start + size, :])
    norm_two_slope(grad_ref, second_ref, second_stats_ref, mask_ref, gain_ref, bias_ref, width, copies_ref)


def norm_two_slope(grad_ref, pre_ref, stats_ref, mask_ref, gain_ref, bias_ref, begin, copies_ref):
    pixels, width = pre_ref.shape
    mean, var = (stats_ref[0:1, :], stats_ref[1:2, :])
    inverse = lax.rsqrt(var + eps_norm)
    scale, shift = scale_shift(
        mean, var, gain_ref[:, begin : begin + width], bias_ref[:, begin : begin + width]
    )

    def both(rows):
        pre = pre_ref[rows, :]
        slope = silu_slope(pre * scale + shift)
        grad = grad_ref[rows, :] * slope * wide_mask(mask_ref, rows, width)
        grad_ref[rows, :] = grad
        return (grad, grad * ((pre - mean) * inverse))

    write_copies(copies_ref, two_sums(pixels, width, both))


def low_second(total_ref, grad_ref, pre_ref, stats_ref, mask_ref, count_ref, gain, low_ref, result_ref):
    pixels, width = pre_ref.shape
    total = read_copies(total_ref)
    coefs = grad_rows(total, stats_ref[...], gain, count_ref[0:1, 0:1], width)
    result_ref[...] = jnp.concatenate(coefs[4:6], axis=0)

    def step(rows, carry):
        mask = wide_mask(mask_ref, rows, width)
        low_ref[rows, :] = low_gradient(
            rows, width, 0, grad_ref[rows, :], pre_ref[rows, :], mask, coefs
        ).astype(bf16)
        return carry

    row_loop(pixels, step, 0)


def back_plain_body(
    total_ref, grad_in_ref, second_ref, second_stats_ref, first_ref, first_stats_ref, mask_ref,
    count_ref, place_ref, gain_ref, bias_ref, spatial_ref,
    low_ref, half_ref, grad_ref, copies_ref, result_ref,
    sums_ref,
):
    pixels, width = second_ref.shape
    side = 1 << ((pixels.bit_length() - 1) // 2)
    low_second(
        total_ref, grad_in_ref, second_ref, second_stats_ref, mask_ref, count_ref,
        gain_ref[:, width : 2 * width], low_ref, result_ref,
    )
    half = half_ref.shape[1]
    other = pl.multiple_of((1 - place_ref[0, 0]) * half, lane)
    half_ref[...] = low_ref[:, pl.ds(other, half)].astype(f32)
    flush(low_ref)
    flush(half_ref)
    need(spatial_ref)
    sums_ref[...] = jnp.zeros_like(sums_ref)
    for tap_index in range(9):
        tap_rows_out(
            sums_ref, tap_index, pixels, side, dot_nt(low_ref[...], spatial_ref[tap_index])
        )
    grad_ref[...] = fold_columns(sums_ref, pixels, side)
    norm_two_slope(grad_ref, first_ref, first_stats_ref, mask_ref, gain_ref, bias_ref, 0, copies_ref)


def back_deform_body(
    total_ref, grad_in_ref, second_ref, second_stats_ref, first_ref, first_stats_ref, mask_ref,
    count_ref, place_ref, gain_ref, bias_ref, spatial_ref, act_ref, offsets_ref, weights_ref,
    low_ref, half_ref, grad_ref, copies_ref, result_ref, grad_offsets_ref,
    sums_ref, padded_ref, shifted_ref,
):
    pixels, width = second_ref.shape
    side = 1 << ((pixels.bit_length() - 1) // 2)
    low_second(
        total_ref, grad_in_ref, second_ref, second_stats_ref, mask_ref, count_ref,
        gain_ref[:, width : 2 * width], low_ref, result_ref,
    )
    half = half_ref.shape[1]
    other = pl.multiple_of((1 - place_ref[0, 0]) * half, lane)
    half_ref[...] = low_ref[:, pl.ds(other, half)].astype(f32)
    flush(low_ref)
    flush(half_ref)
    for ref in (first_ref, first_stats_ref, spatial_ref, act_ref, offsets_ref, weights_ref):
        need(ref)
    offsets = offsets_ref[...]
    outs = offsets.shape[1]
    channel = lax.broadcasted_iota(jnp.int32, (pixels, outs), 1)
    moved = jnp.zeros((pixels, outs), f32)
    grad_ref[...] = jnp.zeros_like(grad_ref)
    for tap_index in range(9):
        dist_y, dist_x, bump_y, bump_x = tap_factors(offsets, tap_index, side)
        weight_y, weight_x = (bump_y * bump_y, bump_x * bump_x)
        sampling = (weight_y * weight_x).astype(bf16)
        piece = dot_nt(low_ref[...], spatial_ref[tap_index]).astype(bf16)
        grad_ref[...] = grad_ref[...] + dot_tn(sampling, piece)
        product = -4.0 * dot_nt(piece, act_ref[...])
        along_y = jnp.sum(product * (dist_y * bump_y * weight_x), axis=1, keepdims=True)
        along_x = jnp.sum(product * (dist_x * bump_x * weight_y), axis=1, keepdims=True)
        moved = moved + jnp.where(channel == 2 * tap_index, along_y, 0.0)
        moved = moved + jnp.where(channel == 2 * tap_index + 1, along_x, 0.0)
    moved_low = moved.astype(bf16)
    padded_ref[...] = jnp.zeros_like(padded_ref)
    padded_ref[pl.ds(2 * side, pixels), :] = act_ref[...].astype(f32)
    build_taps(padded_ref, shifted_ref, pixels, side)
    sums_ref[...] = jnp.zeros_like(sums_ref)
    grad_offsets_ref[...] = jnp.zeros_like(grad_offsets_ref)
    for tap_index in range(9):
        taps = tap_of(shifted_ref, tap_index, pixels, side)
        first = tap_index * outs
        grad_offsets_ref[first : first + outs, :] = dot_tn(moved_low, taps)
        tap_rows_out(
            sums_ref, tap_index, pixels, side, dot_nt(moved_low, weights_ref[tap_index])
        )
    grad_ref[...] = grad_ref[...] + fold_columns(sums_ref, pixels, side)
    norm_two_slope(grad_ref, first_ref, first_stats_ref, mask_ref, gain_ref, bias_ref, 0, copies_ref)


def back_between_body(
    total_ref, grad_ref, first_ref, first_stats_ref, grad_sum_ref, summed_ref, pre_ref, stats_ref,
    mask_ref, count_ref, gain_ref, squeeze_ref,
    low_ref, wide_ref, next_ref, copies_ref, result_ref,
):
    pixels, width = first_ref.shape
    channels = pre_ref.shape[1]
    low_second(
        total_ref, grad_ref, first_ref, first_stats_ref, mask_ref, count_ref,
        gain_ref[:, :width], low_ref, result_ref,
    )
    wide_ref[...] = low_ref[...].astype(f32)
    flush(low_ref)
    flush(wide_ref)
    for ref in (grad_sum_ref, summed_ref, pre_ref, stats_ref, squeeze_ref):
        need(ref)
    mean, var = (stats_ref[0:1, :], stats_ref[1:2, :])
    inverse = lax.rsqrt(var + eps_norm)
    sums, prods = ([], [])
    for start, size in spans_of(channels, 512):
        span = pl.ds(start, size)
        cut = slice(start, start + size)
        next_ref[:, span] = dot_nt(low_ref[...], squeeze_ref[start : start + size, :])

        def both(rows):
            mask = wide_mask(mask_ref, rows, size)
            slope = silu_slope(summed_ref[rows, span])
            grad = (next_ref[rows, span] + grad_sum_ref[rows, span]) * mask * slope
            next_ref[rows, span] = grad
            return (grad, grad * ((pre_ref[rows, span] - mean[:, cut]) * inverse[:, cut]))

        total_grad, total_prod = two_sums(pixels, size, both)
        sums.append(total_grad)
        prods.append(total_prod)
    write_copies(copies_ref, sums + prods)


def last_low_body(
    total_ref, grad_ref, first_ref, first_stats_ref, mask_ref, count_ref, gain_ref,
    low_ref, wide_ref, result_ref,
):
    width = first_ref.shape[1]
    low_second(
        total_ref, grad_ref, first_ref, first_stats_ref, mask_ref, count_ref,
        gain_ref[:, :width], low_ref, result_ref,
    )
    wide_ref[...] = low_ref[...].astype(f32)


def last_body(low_ref, grad_sum_ref, squeeze_ref, image_ref, token_ref):
    token_ref[...] = jnp.zeros_like(token_ref)
    for start, size in spans_of(image_ref.shape[1], 256):
        block = dot_nt(low_ref[...], squeeze_ref[start : start + size, :])
        image_ref[:, start : start + size] = (
            block + grad_sum_ref[:, start : start + size]
        ).astype(bf16)


def sum_copies_body(copies_ref, out_ref):
    total = jnp.sum(copies_ref[...], axis=0)

    def one_copy(step, carry):
        out_ref[step] = total
        return carry

    lax.fori_loop(0, out_ref.shape[0], one_copy, 0)


block_cols = 256


def split_chunks(scratch_ref, keep_ref, send_ref, own, place, spot):
    for index in range(keep_ref.shape[0]):
        low = index & ((1 << place) - 1)
        base = ((index >> place) << (place + 1)) | low
        keep_ref[index, spot] = scratch_ref[base + own * (1 << place)]
        send_ref[index, spot] = scratch_ref[base + (1 - own) * (1 << place)]


def weights_body(kinds, firsts, spans, own_place_ref, *refs):
    groups = [refs[4 * place : 4 * place + 4] for place in range(len(kinds))]
    rest = refs[4 * len(kinds) :]
    streams = len(spans)
    outs, token_ref = (rest[: 2 * streams], rest[2 * streams])
    chunks_ref, scratch = (rest[2 * streams + 1], list(rest[2 * streams + 2 :]))
    token_ref[...] = jnp.zeros_like(token_ref)
    count, depth, _ = chunks_ref.shape
    makers = []
    for kind, (rows_ref, rows_other_ref, cols_ref, cols_other_ref) in zip(kinds, groups):
        for ref in (rows_ref, rows_other_ref, cols_ref, cols_other_ref):
            need(ref)
        pixels, half = cols_other_ref.shape
        side = 1 << ((pixels.bit_length() - 1) // 2)
        both_cols = scratch.pop(0)
        start_own = pl.multiple_of(own_place_ref[0, 0] * half, lane)
        both_cols[pl.ds(0, pixels), :] = cols_ref[:, pl.ds(start_own, half)]
        both_cols[pl.ds(pixels, pixels), :] = cols_other_ref[...].astype(bf16)
        if kind == "rows":
            both_rows = scratch.pop(0)
            both_rows[pl.ds(0, pixels), :] = rows_ref[...]
            both_rows[pl.ds(pixels, pixels), :] = rows_other_ref[...].astype(bf16)
            for start in range(0, half, block_cols):
                makers.append(
                    lambda rows=both_rows, cols=both_cols, start=start: dot_tn(
                        rows[...], cols[:, start : start + block_cols]
                    )
                )
        elif kind == "plain":
            padded, taps = (scratch.pop(0), (scratch.pop(0), scratch.pop(0)))
            for source, shifted in zip((rows_ref, rows_other_ref), taps):
                padded[...] = jnp.zeros_like(padded)
                padded[pl.ds(2 * side, pixels), :] = source[...]
                build_taps(padded, shifted, pixels, side)
            for tap in range(9):
                makers.append(
                    lambda taps=taps, cols=both_cols, tap=tap, pixels=pixels, side=side: dot_tn(
                        tap_of(taps[0], tap, pixels, side), cols[pl.ds(0, pixels), :]
                    )
                    + dot_tn(tap_of(taps[1], tap, pixels, side), cols[pl.ds(pixels, pixels), :])
                )
        else:
            width = cols_ref.shape[1]
            for tap in range(9):
                span = slice(tap * width, (tap + 1) * width)
                makers.append(
                    lambda one=rows_ref, two=rows_other_ref, cols=both_cols, span=span, pixels=pixels: dot_tn(
                        one[:, span], cols[pl.ds(0, pixels), :]
                    )
                    + dot_tn(two[:, span].astype(bf16), cols[pl.ds(pixels, pixels), :])
                )
    for stream, (start, stop) in enumerate(spans):
        bit = firsts[stream]
        own = own_place_ref[0, bit]
        for part in range(start, stop):
            chunks_ref[...] = makers[part]().reshape(count, depth, block_cols)
            split_chunks(
                chunks_ref, outs[2 * stream], outs[2 * stream + 1], own, bit - 1, part - start
            )
        flush(outs[2 * stream + 1])
        flush(outs[2 * stream])


def step_body(spots, own_place_ref, *refs):
    streams = len(spots)
    kept, came = (refs[:streams], refs[streams : 2 * streams])
    outs = refs[2 * streams :]
    outs[-1][...] = jnp.zeros_like(outs[-1])
    for stream, (bit, place) in enumerate(spots):
        own = own_place_ref[0, bit]
        need(kept[stream])
        need(came[stream])
        keep_ref, send_ref = (outs[2 * stream], outs[2 * stream + 1])
        for index in range(keep_ref.shape[0]):
            low = index & ((1 << place) - 1)
            base = ((index >> place) << (place + 1)) | low
            theirs = base + (1 - own) * (1 << place)
            send_ref[index] = kept[stream][theirs] + came[stream][theirs]
        flush(send_ref)
        for index in range(keep_ref.shape[0]):
            low = index & ((1 << place) - 1)
            base = ((index >> place) << (place + 1)) | low
            mine = base + own * (1 << place)
            keep_ref[index] = kept[stream][mine] + came[stream][mine]
        flush(keep_ref)


def last_step_body(streams, *refs):
    kept, came, out_ref = (refs[:streams], refs[streams : 2 * streams], refs[2 * streams])
    refs[-1][...] = jnp.zeros_like(refs[-1])
    start = 0
    for stream in range(streams):
        stop = start + kept[stream].shape[1]
        out_ref[start:stop] = kept[stream][0] + came[stream][0]
        start = stop


def assemble_body(kinds, flips, own_place_ref, own_ref, pair_ref, side_ref, both_ref, *outs):
    outs[-1 - sum(flips)][...] = jnp.zeros_like(outs[-1 - sum(flips)])
    turned = list(outs[len(outs) - sum(flips) :])
    rows, cols = own_ref.shape[-2:]
    pair, line = (own_place_ref[0, 0], own_place_ref[0, 1])
    for row_at, col_at in ((0, 0), (0, 1), (1, 0), (1, 1)):
        same_row, same_col = (line == row_at, pair == col_at)
        row_span = slice(row_at * rows, (row_at + 1) * rows)

        def chosen(part):
            near = jnp.where(same_col, own_ref[part], pair_ref[part])
            far = jnp.where(same_col, side_ref[part], both_ref[part])
            return jnp.where(same_row, near, far)

        part = 0
        used = 0
        for place, kind in enumerate(kinds):
            if kind == "rows":
                target = outs[place]
                if flips[place]:
                    target = turned[used]
                    used += 1
                parts = target.shape[1] // 2 // cols
                for step in range(parts):
                    at = (col_at * parts + step) * cols
                    target[row_span, at : at + cols] = chosen(part + step)
                part += parts
            else:
                for step in range(9):
                    outs[place][step, row_span, col_at * cols : (col_at + 1) * cols] = chosen(part + step)
                part += 9
    used = 0
    for place, flip in enumerate(flips):
        if flip:
            width = turned[used].shape[1]
            for start in range(0, width, block_cols):
                outs[place][start : start + block_cols, :] = turned[used][:, start : start + block_cols].T
            used += 1


class Comm:
    def __init__(self, wide_size, narrow_size):
        self.total = wide_size * narrow_size
        self.bits = self.total.bit_length() - 1
        self.low = narrow_size.bit_length() - 1
        self.index = lax.axis_index("wide") * narrow_size + lax.axis_index("narrow")
        self.places = jnp.stack([self.bit(place) for place in range(self.bits)])[None, :]

    def bit(self, place):
        return (self.index >> place) & 1

    def swap_over(self, values, flips):
        pairs = [(source, source ^ flips) for source in range(self.total)]
        return lax.ppermute(values, axes, pairs)

    def swap(self, values, place):
        return self.swap_over(values, 1 << place)

    def sync(self, copies):
        return lax.all_to_all(copies, axes, 0, 0, tiled=True)

    def orders(self):
        outer = list(range(self.low, self.bits))
        inner = list(range(1, self.low))
        return (
            outer[:1] + inner + outer[1:],
            inner + outer[1:2] + outer[:1] + outer[2:],
            outer[1:2] + outer[:1] + inner + outer[2:],
        )


token = (8, lane)


class Chain:
    def __init__(self, comm, kinds, groups, after=()):
        self.comm = comm
        self.kinds = kinds
        self.orders = comm.orders()
        pixels, rows = groups[0][0].shape
        if kinds[0] == "given":
            rows = groups[0][2].shape[1]
        self.rows = rows
        chunks = 1 << (comm.bits - 1)
        depth = rows // chunks
        side = 1 << ((pixels.bit_length() - 1) // 2)
        total = 0
        scratch = [pltpu.VMEM((chunks, depth, block_cols), f32)]
        self.shapes = []
        for kind, (_, _, cols_op, cols_other) in zip(kinds, groups):
            half = cols_other.shape[1]
            scratch.append(pltpu.VMEM((2 * pixels, half), bf16))
            if kind == "rows":
                total += half // block_cols
                scratch.append(pltpu.VMEM((2 * pixels, rows), bf16))
                self.shapes.append((2 * depth, 2 * half))
            else:
                total += 9
                self.shapes.append((9, 2 * depth, 2 * half))
            if kind == "plain":
                scratch.append(pltpu.VMEM((pixels + 4 * side, rows), f32))
                scratch += [pltpu.VMEM((3, pixels + 4 * side, rows), bf16)] * 2
        first = -(-total // 3)
        second = first + -(-(total - first) // 2)
        spans = ((0, first), (first, second), (second, total))
        outs = []
        for start, stop in spans:
            outs += [shape_of((chunks // 2, stop - start, depth, block_cols))] * 2
        args = (comm.places,) + tuple(part for group in groups for part in group)
        pieces = call(
            functools.partial(weights_body, kinds, tuple(order[0] for order in self.orders), spans),
            outs + [shape_of(token)], args, (0,), scratch, after, tuple(range(1, len(args))),
        )
        self.left = [
            [place for place in range(1, comm.bits) if place != order[0]] for order in self.orders
        ]
        self.at = 0
        self.quarters = []
        self.token = pieces[-1]
        self.exchange(pieces)

    def exchange(self, pieces):
        self.kept = pieces[0:-1:2]
        self.came = [
            self.comm.swap(sent, order[self.at]) for sent, order in zip(pieces[1:-1:2], self.orders)
        ]
        self.at += 1

    def step(self, after=()):
        count = len(self.kept)
        if self.at < len(self.orders[0]):
            spots, outs = ([], [])
            for stream, order in enumerate(self.orders):
                bit = order[self.at]
                spots.append((bit, self.left[stream].index(bit)))
                self.left[stream].remove(bit)
                shape = self.kept[stream].shape
                outs += [shape_of((shape[0] // 2,) + shape[1:])] * 2
            pieces = call(
                functools.partial(step_body, tuple(spots)),
                outs + [shape_of(token)],
                (self.comm.places, *self.kept, *self.came), (0,), (), after,
                tuple(range(1, 1 + 2 * count)),
            )
            self.token = pieces[-1]
            self.exchange(pieces)
        else:
            shape = list(self.kept[0].shape[1:])
            shape[0] = sum(piece.shape[1] for piece in self.kept)
            joined, self.token = call(
                functools.partial(last_step_body, count),
                [shape_of(tuple(shape)), shape_of(token)],
                (*self.kept, *self.came), (), (), after,
            )
            self.quarters = [joined] + [self.comm.swap_over(joined, flips) for flips in (1, 2, 3)]
        return self

    def finish(self, flips, after=()):
        while not self.quarters:
            self.step(after)
        outs = [shape_of(shape[::-1] if flip else shape) for shape, flip in zip(self.shapes, flips)]
        scratch = [pltpu.VMEM(shape, f32) for shape, flip in zip(self.shapes, flips) if flip]
        *results, self.token = call(
            functools.partial(assemble_body, self.kinds, flips),
            outs + [shape_of(token)], (self.comm.places, *self.quarters), (0,), scratch, after,
        )
        return results


def per_device(
    wide_size, narrow_size, images, image_sizes, offset_shift, squeeze_one, offsets_one, spatial_one,
    expand_one, squeeze_two, spatial_two, expand_two, norm_gain_one, norm_bias_one, norm_gain_two,
    norm_bias_two, run_mean_one, run_var_one, run_mean_two, run_var_two, grad_output,
):
    comm = Comm(wide_size, narrow_size)
    side, channels = (images.shape[1], images.shape[3])
    pixels = side * side
    width = squeeze_one.shape[1]
    outs = offsets_one.shape[2]
    total = comm.total
    small = (total, 2 * width // lane, lane)
    large = (total, 2 * channels // lane, lane)
    flat = images.reshape(pixels, channels)
    grad_out = grad_output.reshape(pixels, channels)
    gain_one, bias_one = (norm_gain_one[None, :], norm_bias_one[None, :])
    gain_two, bias_two = (norm_gain_two[None, :], norm_bias_two[None, :])
    field = shape_of((pixels, width))
    field_low = shape_of((pixels, width), bf16)
    plane = shape_of((pixels, channels))
    plane_low = shape_of((pixels, channels), bf16)
    half_plane = shape_of((pixels, channels // 2))
    half_field = shape_of((pixels, width // 2))
    stats_small, stats_large = (shape_of((2, width)), shape_of((2, channels)))
    padded = pltpu.VMEM((pixels + 4 * side, width), f32)
    shifted = pltpu.VMEM((3, pixels + 4 * side, width), bf16)
    tap_sums = pltpu.VMEM((3, pixels + 4 * side, width), f32)

    first_one, mask, copies, images_half = call(
        first_body,
        (field, shape_of((pixels, lane)), shape_of((total, 2 * width // lane + 8, lane)), half_plane),
        (image_sizes, comm.places, flat, squeeze_one),
        (0, 1),
    )
    images_half = comm.swap(images_half, 0)
    copies = comm.sync(copies)
    (act_one, columns, columns_wide, offsets, second_one, copies, first_stats_one, count) = call(
        deform_body,
        (
            field_low, shape_of((pixels, 9 * width), bf16), shape_of((pixels, 9 * width)),
            shape_of((pixels, outs)), field, shape_of(small), stats_small, shape_of((8, lane)),
        ),
        (
            copies, first_one, mask, gain_one, bias_one, offsets_one,
            offset_shift.astype(f32)[None, :], spatial_one,
        ),
        (),
        (padded, shifted),
        (),
        (5, 7),
    )
    columns_wide = comm.swap(columns_wide, 0)
    copies = comm.sync(copies)
    act_second_one, act_second_wide_one, third_one, copies, second_stats_one = call(
        third_body,
        (field_low, field, plane, shape_of(large), stats_small),
        (copies, second_one, mask, count, gain_one, bias_one, expand_one), late=(6,),
    )
    act_second_wide_one = comm.swap(act_second_wide_one, 0)
    copies = comm.sync(copies)
    summed_one, low_two, low_half, first_two, copies, third_stats_one = call(
        between_body,
        (plane, plane_low, half_plane, field, shape_of(small), stats_large),
        (copies, third_one, flat, mask, count, comm.places, gain_one, bias_one, squeeze_two),
        (5,), late=(8,),
    )
    low_half = comm.swap(low_half, 0)
    copies = comm.sync(copies)
    act_wide_two, second_two, copies, first_stats_two = call(
        plain_body,
        (field, field, shape_of(small), stats_small),
        (copies, first_two, mask, count, gain_two, bias_two, spatial_two),
        (),
        (padded, shifted), late=(6,),
    )
    act_wide_two_other = comm.swap(act_wide_two, 0)
    copies = comm.sync(copies)
    act_second_two, act_second_wide_two, third_two, copies, second_stats_two = call(
        third_body,
        (field_low, field, plane, shape_of(large), stats_small),
        (copies, second_two, mask, count, gain_two, bias_two, expand_two), late=(6,),
    )
    act_second_wide_two = comm.swap(act_second_wide_two, 0)
    copies = comm.sync(copies)
    output_images, grad_sum_two, copies, third_stats_two = call(
        turn_body,
        (plane_low, plane, shape_of(large), stats_large),
        (copies, third_two, summed_one, grad_out, mask, count, gain_two, bias_two),
    )
    copies = comm.sync(copies)
    low_third_two, third_half, grad_second_two, copies, third_result_two = call(
        back_third_body,
        (plane_low, half_plane, field, shape_of(small), stats_large),
        (
            copies, grad_sum_two, third_two, third_stats_two, second_two, second_stats_two, mask, count,
            comm.places, gain_two, bias_two, expand_two,
        ),
        (8,), late=(4, 5, 11),
    )
    third_half = comm.swap(third_half, 0)
    copies = comm.sync(copies)
    low_second_two, second_half, grad_first_two, copies, second_result_two = call(
        back_plain_body,
        (field_low, half_field, field, shape_of(small), stats_small),
        (
            copies, grad_second_two, second_two, second_stats_two, first_two, first_stats_two, mask,
            count, comm.places, gain_two, bias_two, spatial_two,
        ),
        (8,),
        (tap_sums,),
        (),
        (11,),
    )
    second_half = comm.swap(second_half, 0)
    copies = comm.sync(copies)
    chain_one = Chain(
        comm, ("rows", "plain"),
        (
            (act_second_two, act_second_wide_two, low_third_two, third_half),
            (act_wide_two, act_wide_two_other, low_second_two, second_half),
        ),
    )
    low_first_two, low_first_wide, grad_sum_one, copies, first_result_two = call(
        back_between_body,
        (field_low, field, plane, shape_of(large), stats_small),
        (
            copies, grad_first_two, first_two, first_stats_two, grad_sum_two, summed_one, third_one,
            third_stats_one, mask, count, gain_two, squeeze_two,
        ),
        (),
        (),
        (chain_one.token,),
        (4, 5, 6, 7, 11),
    )
    low_first_wide = comm.swap(low_first_wide, 0)
    copies = comm.sync(copies)
    low_third_one, third_half, grad_second_one, copies, third_result_one = call(
        back_third_body,
        (plane_low, half_plane, field, shape_of(small), stats_large),
        (
            copies, grad_sum_one, third_one, third_stats_one, second_one, second_stats_one, mask, count,
            comm.places, gain_one, bias_one, expand_one,
        ),
        (8,),
        (),
        (),
        (4, 5, 11),
    )
    third_half = comm.swap(third_half, 0)
    copies = comm.sync(copies)
    chain_one.step((third_result_one,))
    slots = -(-9 * outs // total)
    slots = -(-slots // 8) * 8
    low_second_one, second_half, grad_first_one, copies, second_result_one, grad_offsets = call(
        back_deform_body,
        (
            field_low, half_field, field, shape_of(small), stats_small, shape_of((total * slots, width)),
        ),
        (
            copies, grad_second_one, second_one, second_stats_one, first_one, first_stats_one, mask,
            count, comm.places, gain_one, bias_one, spatial_one, act_one, offsets, offsets_one,
        ),
        (8,),
        (tap_sums, padded, shifted),
        (chain_one.token,),
        (4, 5, 11, 12, 13, 14),
    )
    second_half = comm.swap(second_half, 0)
    copies = comm.sync(copies)
    chain_one.step((second_result_one,))
    chain_two = Chain(
        comm, ("rows", "rows", "given"),
        (
            (low_first_two, low_first_wide, low_two, low_half),
            (act_second_one, act_second_wide_one, low_third_one, third_half),
            (columns, columns_wide, low_second_one, second_half),
        ),
        (chain_one.token,),
    )
    low_first_one, low_first_wide, first_result_one = call(
        last_low_body,
        (field_low, field, stats_small),
        (copies, grad_first_one, first_one, first_stats_one, mask, count, gain_one),
        (),
        (),
        (chain_two.token,),
    )
    low_first_wide = comm.swap(low_first_wide, 0)
    grad_offsets = comm.sync(grad_offsets.reshape(total, slots, width))
    grad_images, last_token = call(
        last_body,
        (plane_low, shape_of(token)),
        (low_first_one, grad_sum_one, squeeze_one),
    )
    chain_three = Chain(
        comm, ("rows",), ((low_first_one, low_first_wide, flat, images_half),), (last_token,)
    )
    (grad_offsets,) = call(
        sum_copies_body, (shape_of((total, slots, width)),), (grad_offsets,), (), (),
        (chain_three.token,),
    )
    grad_offsets = comm.sync(grad_offsets)
    last = chain_three.token
    for chain in (
        chain_one, chain_one, chain_three, chain_two, chain_three, chain_two, chain_three, chain_two,
        chain_three, chain_two,
    ):
        last = chain.step((last,)).token
    grad_expand_two, grad_spatial_two = chain_one.finish((False, False), (last,))
    (grad_squeeze_one,) = chain_three.finish((True,), (last,))
    grad_squeeze_two, grad_expand_one, grad_spatial_one = chain_two.finish((True, False, False), (last,))

    def laid(parts, row):
        return jnp.concatenate([part[row] for part in parts])

    results_one = (first_result_one, second_result_one, third_result_one)
    results_two = (first_result_two, second_result_two, third_result_two)
    stats_one = (first_stats_one, second_stats_one, third_stats_one)
    stats_two = (first_stats_two, second_stats_two, third_stats_two)
    pixel_count = count[0, 0]
    unbias = pixel_count / (pixel_count - 1.0)
    fresh = 1.0 - keep_rate
    return (
        output_images.reshape(images.shape),
        grad_images.reshape(images.shape),
        grad_squeeze_one,
        grad_offsets.reshape(total * slots, width)[: 9 * outs].reshape(9, outs, width).transpose(0, 2, 1),
        grad_spatial_one,
        grad_expand_one,
        grad_squeeze_two,
        grad_spatial_two,
        grad_expand_two,
        laid(results_one, 1),
        laid(results_one, 0),
        laid(results_two, 1),
        laid(results_two, 0),
        keep_rate * run_mean_one + fresh * laid(stats_one, 0),
        keep_rate * run_var_one + fresh * laid(stats_one, 1) * unbias,
        keep_rate * run_mean_two + fresh * laid(stats_two, 0),
        keep_rate * run_var_two + fresh * laid(stats_two, 1) * unbias,
    )


def solution(mesh):
    images_spec = P(axes, None, None, None)
    whole = P()
    return jax.shard_map(
        functools.partial(per_device, mesh.shape["wide"], mesh.shape["narrow"]),
        mesh=mesh,
        in_specs=(images_spec, P(axes, None)) + (whole,) * 16 + (images_spec,),
        out_specs=(
            images_spec,
            images_spec,
            P(None, "wide"),
            whole,
            P(None, "wide", None),
            P("wide", None),
            P(None, "wide"),
            P(None, "wide", None),
            P("wide", None),
        )
        + (whole,) * 8,
        check_vma=False,
    )
```

```python
import functools

import jax
import jax.numpy as jnp
from jax import lax
from jax.experimental import pallas as pl
from jax.experimental.pallas import tpu as pltpu
from jax.sharding import PartitionSpec as P

eps_norm = 1e-05
keep_rate = 0.6
vmem_bytes = 52 * 1024 * 1024
lane = 128
tile_rows = 16
axes = ("wide", "narrow")
f32 = jnp.float32
bf16 = jnp.bfloat16


def shape_of(shape, kind=f32):
    return jax.ShapeDtypeStruct(shape, kind)


copies_of = {}


def need(ref):
    entry = copies_of.get(id(ref))
    if entry is not None and entry[1]:
        entry[1] = False
        entry[0].wait()
    return ref


def flush(ref):
    entry = copies_of.get(id(ref))
    if entry is not None and entry[1]:
        entry[1] = False
        entry[0].start()


class Near:
    def __init__(self, value):
        self.value = value


def call(body, outs, args, smem=(), scratch=(), after=(), late=(), stay_out=(), pieces=None, begun=None):
    stay = tuple(place for place, arg in enumerate(args) if isinstance(arg, Near))
    args = tuple(arg.value if isinstance(arg, Near) else arg for arg in args)
    pieces = pieces or {}
    begun = begun or {}
    hbm = pl.BlockSpec(memory_space=pltpu.HBM)
    vmem = pl.BlockSpec(memory_space=pltpu.VMEM)
    specs = [
        pl.BlockSpec(memory_space=pltpu.SMEM) if place in smem else vmem if place in stay else hbm
        for place in range(len(args))
    ] + [pl.BlockSpec(memory_space=pl.ANY)] * len(after) + [hbm] * len(begun)
    moved = [place for place in range(len(args)) if place not in smem and place not in stay]
    used, extra, made = (len(args), len(after) + len(begun), len(outs))
    sent = [slot for slot in range(made) if slot not in stay_out]

    def kernel(*refs):
        given = list(refs[:used])
        results = list(refs[used + extra : used + extra + made])
        rest = refs[used + extra + made :]
        in_slots, out_slots = (rest[: len(moved)], rest[len(moved) : len(moved) + len(sent)])
        in_flags, out_flags = rest[len(moved) + len(sent) : len(moved) + len(sent) + 2]
        copies_of.clear()
        for slot, place in enumerate(moved):
            copy = pltpu.make_async_copy(given[place], in_slots[slot], in_flags.at[slot])
            copy.start()
            copies_of[id(in_slots[slot])] = [copy, True]
            given[place] = in_slots[slot]
        for place in moved:
            if place not in late:
                need(given[place])
        for slot, place in enumerate(sent):
            copies_of[id(out_slots[slot])] = [
                pltpu.make_async_copy(
                    out_slots[slot],
                    results[place].at[:, pl.ds(*pieces[place])] if place in pieces else results[place],
                    out_flags.at[slot],
                ),
                True,
            ]
            results[place] = out_slots[slot]
        body(*given, *results, *rest[len(moved) + len(sent) + 2 :])
        for place in moved:
            need(given[place])
        for slot in out_slots:
            if copies_of[id(slot)][1]:
                flush(slot)
        for slot in out_slots:
            copies_of[id(slot)][0].wait()
        copies_of.clear()

    slots = [pltpu.VMEM(args[place].shape, args[place].dtype) for place in moved]
    for place in sent:
        shape = outs[place].shape
        if place in pieces:
            shape = (shape[0], pieces[place][1]) + shape[2:]
        slots.append(pltpu.VMEM(shape, outs[place].dtype))
    flags = [pltpu.SemaphoreType.DMA((max(len(moved), 1),)), pltpu.SemaphoreType.DMA((max(len(sent), 1),))]
    return pl.pallas_call(
        kernel,
        input_output_aliases={used + len(after) + at: place for at, place in enumerate(begun)},
        out_shape=tuple(outs),
        in_specs=specs,
        out_specs=tuple(vmem if place in stay_out else hbm for place in range(made)),
        scratch_shapes=slots + flags + list(scratch),
        compiler_params=pltpu.CompilerParams(vmem_limit_bytes=vmem_bytes),
    )(*args, *after, *begun.values())


def dot_nn(first_op, second_op):
    return lax.dot_general(
        first_op, second_op, (((1,), (0,)), ((), ())), preferred_element_type=f32
    )


def dot_nt(first_op, second_op):
    return lax.dot_general(
        first_op, second_op, (((1,), (1,)), ((), ())), preferred_element_type=f32
    )


def dot_tn(first_op, second_op):
    return lax.dot_general(
        first_op, second_op, (((0,), (0,)), ((), ())), preferred_element_type=f32
    )


def logistic(values):
    return 0.5 * jnp.tanh(0.5 * values) + 0.5


def silu(values):
    return values * logistic(values)


def silu_slope(values):
    gate = logistic(values)
    return gate * (1.0 + values * (1.0 - gate))


def flat_row(rows, start, width):
    first = start // lane
    return jnp.concatenate(
        [rows[first + step : first + step + 1, :] for step in range(width // lane)], axis=1
    )


def fold_row(row):
    return [row[:, step * lane : (step + 1) * lane] for step in range(row.shape[1] // lane)]


def write_copies(copies_ref, rows, extra=None):
    packed = jnp.concatenate([piece for row in rows for piece in fold_row(row)], axis=0)
    if extra is not None:
        packed = jnp.concatenate([packed, extra], axis=0)

    def one_copy(step, carry):
        copies_ref[step] = packed
        return carry

    lax.fori_loop(0, copies_ref.shape[0], one_copy, 0)


def read_copies(copies_ref):
    return jnp.sum(copies_ref[...], axis=0)


def wide_mask(mask_ref, rows, width):
    return jnp.concatenate([mask_ref[rows, :]] * (width // lane), axis=1)


def eight_rows(values):
    folded = values[:8]
    for start in range(8, values.shape[0], 8):
        folded = folded + values[start : start + 8]
    return folded


def row_loop(pixels, body, carry):
    def step(index, state):
        return body(pl.ds(pl.multiple_of(index * tile_rows, tile_rows), tile_rows), state)

    return lax.fori_loop(0, pixels // tile_rows, step, carry)


def two_sums(pixels, width, body):
    zero = jnp.zeros((8, width), f32)

    def step(rows, state):
        first, second = body(rows)
        return (state[0] + eight_rows(first), state[1] + eight_rows(second))

    first, second = row_loop(pixels, step, (zero, zero))
    return (jnp.sum(first, axis=0, keepdims=True), jnp.sum(second, axis=0, keepdims=True))


def moments(total, width, count):
    mean = flat_row(total, 0, width) / count
    var = flat_row(total, width, width) / count - mean * mean
    return (mean, var)


def scale_shift(mean, var, gain, bias):
    inverse = lax.rsqrt(var + eps_norm)
    scale = gain * inverse
    return (scale, bias - mean * scale)


def spans_of(width, block):
    return [(start, min(block, width - start)) for start in range(0, width, block)]


def grad_rows(total, stats, gain, count, width):
    mean, var = (stats[0:1], stats[1:2])
    inverse = lax.rsqrt(var + eps_norm)
    sum_grad = flat_row(total, 0, width)
    sum_prod = flat_row(total, width, width)
    return (
        gain * inverse,
        sum_grad / count,
        inverse * sum_prod / count,
        mean,
        sum_grad,
        sum_prod,
    )


def build_taps(act_ref, shifted_ref, pixels, side):
    pad = 2 * side
    width = act_ref.shape[1]
    column = lax.broadcasted_iota(jnp.int32, (pixels, lane), 0) % side
    for tap_col in range(3):
        move = 2 * (tap_col - 1)
        moved = act_ref[pl.ds(pad + move, pixels), :]
        if move:
            inside = (column + move >= 0) & (column + move < side)
            keep = jnp.concatenate([inside.astype(f32)] * (width // lane), axis=1)
            moved = moved * keep
        shifted_ref[tap_col, pl.ds(0, pad), :] = jnp.zeros((pad, width), bf16)
        shifted_ref[tap_col, pl.ds(pad + pixels, pad), :] = jnp.zeros((pad, width), bf16)
        shifted_ref[tap_col, pl.ds(pad, pixels), :] = moved.astype(bf16)


def tap_of(shifted_ref, tap_index, pixels, side):
    tap_row, tap_col = (tap_index // 3, tap_index % 3)
    return shifted_ref[tap_col, pl.ds(2 * side * tap_row, pixels), :]


def fold_columns(sums_ref, pixels, side):
    pad = 2 * side
    width = sums_ref.shape[2]
    column = lax.broadcasted_iota(jnp.int32, (pixels, lane), 0) % side
    total = sums_ref[1, pl.ds(pad, pixels), :]
    for tap_col in (0, 2):
        move = 2 * (tap_col - 1)
        inside = (column - move >= 0) & (column - move < side)
        keep = jnp.concatenate([inside.astype(f32)] * (width // lane), axis=1)
        total = total + keep * sums_ref[tap_col, pl.ds(pad - move, pixels), :]
    return total


def tap_rows_out(sums_ref, tap_index, pixels, side, values):
    tap_row, tap_col = (tap_index // 3, tap_index % 3)
    rows = pl.ds(2 * side * tap_row, pixels)
    sums_ref[tap_col, rows, :] = sums_ref[tap_col, rows, :] + values


def tap_factors(offsets, tap_index, side):
    pixels = offsets.shape[0]
    tap_row, tap_col = (tap_index // 3, tap_index % 3)
    shape = (pixels, pixels)
    position = lax.broadcasted_iota(jnp.int32, shape, 0)
    source = lax.broadcasted_iota(jnp.int32, shape, 1)
    gap_y = (position // side - source // side + 2 * (tap_row - 1)).astype(f32)
    gap_x = (position % side - source % side + 2 * (tap_col - 1)).astype(f32)
    dist_y = gap_y + offsets[:, 2 * tap_index : 2 * tap_index + 1]
    dist_x = gap_x + offsets[:, 2 * tap_index + 1 : 2 * tap_index + 2]
    bump_y = jnp.maximum(1.0 - dist_y * dist_y, 0.0)
    bump_x = jnp.maximum(1.0 - dist_x * dist_x, 0.0)
    return (dist_y, dist_x, bump_y, bump_x)


def first_body(sizes_ref, place_ref, images_ref, squeeze_ref, pre_ref, mask_ref, copies_ref, half_ref):
    pixels, width = pre_ref.shape
    side = 1 << ((pixels.bit_length() - 1) // 2)
    position = lax.broadcasted_iota(jnp.int32, (pixels, lane), 0)
    inside = (position // side < sizes_ref[0, 0]) & (position % side < sizes_ref[0, 1])
    mask = inside.astype(f32)
    mask_ref[...] = mask
    pre_ref[...] = dot_nn(images_ref[...], squeeze_ref[...])

    def both(rows):
        values = pre_ref[rows, :]
        masked = values * wide_mask(mask_ref, rows, width)
        return (masked, masked * values)

    sums = two_sums(pixels, width, both)
    amount = jnp.sum(mask, axis=0, keepdims=True)
    write_copies(copies_ref, sums, jnp.broadcast_to(amount, (8, lane)))
    half = half_ref.shape[1]
    other = pl.multiple_of((1 - place_ref[0, 0]) * half, lane)
    half_ref[...] = images_ref[:, pl.ds(other, half)].astype(f32)


def activate(pre_ref, mask_ref, scale, shift, out_ref, base=0):
    pixels, width = pre_ref.shape

    def step(rows, carry):
        out = silu(pre_ref[rows, :] * scale + shift) * wide_mask(mask_ref, rows, width)
        target = pl.ds(rows.start + base, tile_rows)
        out_ref[target, :] = out.astype(bf16).astype(out_ref.dtype)
        return carry

    row_loop(pixels, step, 0)


def masked_sums(values_ref, mask_ref):
    pixels, width = values_ref.shape

    def both(rows):
        values = values_ref[rows, :]
        masked = values * wide_mask(mask_ref, rows, width)
        return (masked, masked * values)

    return two_sums(pixels, width, both)


def deform_body(
    total_ref, pre_ref, mask_ref, gain_ref, bias_ref, weights_ref, move_ref, spatial_ref,
    act_ref, columns_ref, columns_wide_ref, offsets_ref, second_ref, copies_ref, stats_ref,
    count_ref, padded_ref, shifted_ref,
):
    pixels, width = pre_ref.shape
    side = 1 << ((pixels.bit_length() - 1) // 2)
    total = read_copies(total_ref)
    count = total[2 * width // lane : 2 * width // lane + 1, 0:1]
    count_ref[...] = jnp.broadcast_to(count, (8, lane))
    mean, var = moments(total, width, count)
    stats_ref[...] = jnp.concatenate([mean, var], axis=0)
    scale, shift = scale_shift(mean, var, gain_ref[:, :width], bias_ref[:, :width])
    padded_ref[...] = jnp.zeros_like(padded_ref)
    activate(pre_ref, mask_ref, scale, shift, padded_ref, 2 * side)
    act_ref[...] = padded_ref[pl.ds(2 * side, pixels), :].astype(bf16)
    build_taps(padded_ref, shifted_ref, pixels, side)
    flush(act_ref)
    offsets = move_ref[...]
    need(weights_ref)
    for tap_index in range(9):
        taps = tap_of(shifted_ref, tap_index, pixels, side)
        offsets = offsets + dot_nn(taps, weights_ref[tap_index])
    offsets_ref[...] = offsets
    flush(offsets_ref)
    need(spatial_ref)
    second_ref[...] = jnp.zeros_like(second_ref)
    for tap_index in range(9):
        dist_y, dist_x, bump_y, bump_x = tap_factors(offsets, tap_index, side)
        root = bump_y * bump_x
        columns = dot_nn((root * root).astype(bf16), act_ref[...]).astype(bf16)
        span = pl.ds(tap_index * width, width)
        columns_ref[:, span] = columns
        columns_wide_ref[:, span] = columns.astype(f32)
        second_ref[...] = second_ref[...] + dot_nn(columns, spatial_ref[tap_index])
    flush(columns_wide_ref)
    flush(columns_ref)
    write_copies(copies_ref, masked_sums(second_ref, mask_ref))


def plain_body(
    total_ref, pre_ref, mask_ref, count_ref, gain_ref, bias_ref, spatial_ref,
    wide_ref, second_ref, copies_ref, stats_ref,
    padded_ref, shifted_ref,
):
    pixels, width = pre_ref.shape
    side = 1 << ((pixels.bit_length() - 1) // 2)
    total = read_copies(total_ref)
    mean, var = moments(total, width, count_ref[0:1, 0:1])
    stats_ref[...] = jnp.concatenate([mean, var], axis=0)
    scale, shift = scale_shift(mean, var, gain_ref[:, :width], bias_ref[:, :width])
    padded_ref[...] = jnp.zeros_like(padded_ref)
    activate(pre_ref, mask_ref, scale, shift, padded_ref, 2 * side)
    wide_ref[...] = padded_ref[pl.ds(2 * side, pixels), :]
    flush(wide_ref)
    build_taps(padded_ref, shifted_ref, pixels, side)
    need(spatial_ref)
    second_ref[...] = jnp.zeros_like(second_ref)
    for tap_index in range(9):
        taps = tap_of(shifted_ref, tap_index, pixels, side)
        second_ref[...] = second_ref[...] + dot_nn(taps, spatial_ref[tap_index])
    write_copies(copies_ref, masked_sums(second_ref, mask_ref))


def third_body(
    total_ref, pre_ref, mask_ref, count_ref, gain_ref, bias_ref, expand_ref,
    act_ref, wide_ref, third_ref, copies_ref, stats_ref,
):
    pixels, width = pre_ref.shape
    channels = third_ref.shape[1]
    total = read_copies(total_ref)
    mean, var = moments(total, width, count_ref[0:1, 0:1])
    stats_ref[...] = jnp.concatenate([mean, var], axis=0)
    scale, shift = scale_shift(
        mean, var, gain_ref[:, width : 2 * width], bias_ref[:, width : 2 * width]
    )
    activate(pre_ref, mask_ref, scale, shift, act_ref)
    wide_ref[...] = act_ref[...].astype(f32)
    flush(act_ref)
    flush(wide_ref)
    need(expand_ref)
    sums, squares = ([], [])
    for start, size in spans_of(channels, 256):
        block = dot_nn(act_ref[...], expand_ref[:, start : start + size])
        third_ref[:, start : start + size] = block
        sums.append(jnp.sum(block, axis=0, keepdims=True))
        squares.append(jnp.sum(block * block, axis=0, keepdims=True))
    flush(third_ref)
    write_copies(copies_ref, sums + squares)


def between_body(
    total_ref, pre_ref, images_ref, mask_ref, count_ref, place_ref, gain_ref, bias_ref, squeeze_ref,
    summed_ref, low_ref, half_ref, first_ref, copies_ref, stats_ref,
):
    pixels, channels = pre_ref.shape
    total = read_copies(total_ref)
    mean, var = moments(total, channels, count_ref[0:1, 0:1])
    stats_ref[...] = jnp.concatenate([mean, var], axis=0)
    begin = gain_ref.shape[1] - channels
    scale, shift = scale_shift(mean, var, gain_ref[:, begin:], bias_ref[:, begin:])
    for start, size in spans_of(channels, 512):
        span = pl.ds(start, size)

        def step(rows, carry):
            summed = (
                pre_ref[rows, span] * scale[:, start : start + size]
                + shift[:, start : start + size]
                + images_ref[rows, span].astype(f32)
            )
            summed_ref[rows, span] = summed
            low_ref[rows, span] = (silu(summed) * wide_mask(mask_ref, rows, size)).astype(bf16)
            return carry

        row_loop(pixels, step, 0)
    flush(summed_ref)
    flush(low_ref)
    need(squeeze_ref)
    sums, squares = ([], [])
    for start, size in spans_of(first_ref.shape[1], 256):
        block = dot_nn(low_ref[...], squeeze_ref[:, start : start + size])
        first_ref[:, start : start + size] = block
        sums.append(jnp.sum(block, axis=0, keepdims=True))
        squares.append(jnp.sum(block * block, axis=0, keepdims=True))
    write_copies(copies_ref, sums + squares)
    half = half_ref.shape[1]
    other = pl.multiple_of((1 - place_ref[0, 0]) * half, lane)
    half_ref[...] = low_ref[:, pl.ds(other, half)].astype(f32)


def turn_body(
    total_ref, pre_ref, before_ref, grad_ref, mask_ref, count_ref, gain_ref, bias_ref,
    image_ref, grad_sum_ref, copies_ref, stats_ref,
):
    pixels, channels = pre_ref.shape
    total = read_copies(total_ref)
    mean, var = moments(total, channels, count_ref[0:1, 0:1])
    stats_ref[...] = jnp.concatenate([mean, var], axis=0)
    begin = gain_ref.shape[1] - channels
    scale, shift = scale_shift(mean, var, gain_ref[:, begin:], bias_ref[:, begin:])
    inverse = lax.rsqrt(var + eps_norm)
    sums, prods = ([], [])
    for start, size in spans_of(channels, 512):
        span = pl.ds(start, size)
        cut = slice(start, start + size)

        def both(rows):
            mask = wide_mask(mask_ref, rows, size)
            pre = pre_ref[rows, span]
            summed = pre * scale[:, cut] + shift[:, cut] + silu(before_ref[rows, span]) * mask
            gate = logistic(summed)
            image_ref[rows, span] = (summed * gate * mask).astype(bf16)
            slope = gate * (1.0 + summed * (1.0 - gate))
            grad = grad_ref[rows, span].astype(f32) * mask * slope
            grad_sum_ref[rows, span] = grad
            return (grad, grad * ((pre - mean[:, cut]) * inverse[:, cut]))

        total_grad, total_prod = two_sums(pixels, size, both)
        sums.append(total_grad)
        prods.append(total_prod)
    flush(image_ref)
    flush(grad_sum_ref)
    write_copies(copies_ref, sums + prods)


def low_gradient(rows, width, start, grad, pre, mask, coefs):
    cut = slice(start, start + width)
    scale, mean_grad, mean_prod, mean = (part[:, cut] for part in coefs[:4])
    return scale * (grad - mask * (mean_grad + (pre - mean) * mean_prod))


def back_third_body(
    total_ref, grad_sum_ref, pre_ref, stats_ref, second_ref, second_stats_ref, mask_ref, count_ref,
    place_ref, gain_ref, bias_ref, expand_ref,
    low_ref, half_ref, grad_ref, copies_ref, result_ref,
):
    pixels, channels = pre_ref.shape
    width = second_ref.shape[1]
    total = read_copies(total_ref)
    coefs = grad_rows(
        total, stats_ref[...], gain_ref[:, 2 * width :], count_ref[0:1, 0:1], channels
    )
    result_ref[...] = jnp.concatenate(coefs[4:6], axis=0)
    for start, size in spans_of(channels, 512):
        span = pl.ds(start, size)

        def step(rows, carry):
            mask = wide_mask(mask_ref, rows, size)
            low_ref[rows, span] = low_gradient(
                rows, size, start, grad_sum_ref[rows, span], pre_ref[rows, span], mask, coefs
            ).astype(bf16)
            return carry

        row_loop(pixels, step, 0)
    half = half_ref.shape[1]
    other = pl.multiple_of((1 - place_ref[0, 0]) * half, lane)
    half_ref[...] = low_ref[:, pl.ds(other, half)].astype(f32)
    flush(low_ref)
    flush(half_ref)
    for ref in (expand_ref, second_ref, second_stats_ref):
        need(ref)
    for start, size in spans_of(width, 256):
        grad_ref[:, start : start + size] = dot_nt(low_ref[...], expand_ref[start : start + size, :])
    norm_two_slope(grad_ref, second_ref, second_stats_ref, mask_ref, gain_ref, bias_ref, width, copies_ref)


def norm_two_slope(grad_ref, pre_ref, stats_ref, mask_ref, gain_ref, bias_ref, begin, copies_ref):
    pixels, width = pre_ref.shape
    mean, var = (stats_ref[0:1, :], stats_ref[1:2, :])
    inverse = lax.rsqrt(var + eps_norm)
    scale, shift = scale_shift(
        mean, var, gain_ref[:, begin : begin + width], bias_ref[:, begin : begin + width]
    )

    def both(rows):
        pre = pre_ref[rows, :]
        slope = silu_slope(pre * scale + shift)
        grad = grad_ref[rows, :] * slope * wide_mask(mask_ref, rows, width)
        grad_ref[rows, :] = grad
        return (grad, grad * ((pre - mean) * inverse))

    write_copies(copies_ref, two_sums(pixels, width, both))


def low_second(total_ref, grad_ref, pre_ref, stats_ref, mask_ref, count_ref, gain, low_ref, result_ref):
    pixels, width = pre_ref.shape
    total = read_copies(total_ref)
    coefs = grad_rows(total, stats_ref[...], gain, count_ref[0:1, 0:1], width)
    result_ref[...] = jnp.concatenate(coefs[4:6], axis=0)

    def step(rows, carry):
        mask = wide_mask(mask_ref, rows, width)
        low_ref[rows, :] = low_gradient(
            rows, width, 0, grad_ref[rows, :], pre_ref[rows, :], mask, coefs
        ).astype(bf16)
        return carry

    row_loop(pixels, step, 0)


def back_plain_body(
    total_ref, grad_in_ref, second_ref, second_stats_ref, first_ref, first_stats_ref, mask_ref,
    count_ref, place_ref, gain_ref, bias_ref, spatial_ref,
    low_ref, half_ref, grad_ref, copies_ref, result_ref,
    sums_ref,
):
    pixels, width = second_ref.shape
    side = 1 << ((pixels.bit_length() - 1) // 2)
    low_second(
        total_ref, grad_in_ref, second_ref, second_stats_ref, mask_ref, count_ref,
        gain_ref[:, width : 2 * width], low_ref, result_ref,
    )
    half = half_ref.shape[1]
    other = pl.multiple_of((1 - place_ref[0, 0]) * half, lane)
    half_ref[...] = low_ref[:, pl.ds(other, half)].astype(f32)
    flush(low_ref)
    flush(half_ref)
    need(spatial_ref)
    sums_ref[...] = jnp.zeros_like(sums_ref)
    for tap_index in range(9):
        tap_rows_out(
            sums_ref, tap_index, pixels, side, dot_nt(low_ref[...], spatial_ref[tap_index])
        )
    grad_ref[...] = fold_columns(sums_ref, pixels, side)
    norm_two_slope(grad_ref, first_ref, first_stats_ref, mask_ref, gain_ref, bias_ref, 0, copies_ref)


def back_deform_body(
    total_ref, grad_in_ref, second_ref, second_stats_ref, first_ref, first_stats_ref, mask_ref,
    count_ref, place_ref, gain_ref, bias_ref, spatial_ref, act_ref, offsets_ref, weights_ref,
    low_ref, half_ref, grad_ref, copies_ref, result_ref, grad_offsets_ref,
    sums_ref, padded_ref, shifted_ref,
):
    pixels, width = second_ref.shape
    side = 1 << ((pixels.bit_length() - 1) // 2)
    low_second(
        total_ref, grad_in_ref, second_ref, second_stats_ref, mask_ref, count_ref,
        gain_ref[:, width : 2 * width], low_ref, result_ref,
    )
    half = half_ref.shape[1]
    other = pl.multiple_of((1 - place_ref[0, 0]) * half, lane)
    half_ref[...] = low_ref[:, pl.ds(other, half)].astype(f32)
    flush(low_ref)
    flush(half_ref)
    for ref in (first_ref, first_stats_ref, spatial_ref, act_ref, offsets_ref, weights_ref):
        need(ref)
    offsets = offsets_ref[...]
    outs = offsets.shape[1]
    channel = lax.broadcasted_iota(jnp.int32, (pixels, outs), 1)
    moved = jnp.zeros((pixels, outs), f32)
    grad_ref[...] = jnp.zeros_like(grad_ref)
    for tap_index in range(9):
        dist_y, dist_x, bump_y, bump_x = tap_factors(offsets, tap_index, side)
        weight_y, weight_x = (bump_y * bump_y, bump_x * bump_x)
        sampling = (weight_y * weight_x).astype(bf16)
        piece = dot_nt(low_ref[...], spatial_ref[tap_index]).astype(bf16)
        grad_ref[...] = grad_ref[...] + dot_tn(sampling, piece)
        product = -4.0 * dot_nt(piece, act_ref[...])
        along_y = jnp.sum(product * (dist_y * bump_y * weight_x), axis=1, keepdims=True)
        along_x = jnp.sum(product * (dist_x * bump_x * weight_y), axis=1, keepdims=True)
        moved = moved + jnp.where(channel == 2 * tap_index, along_y, 0.0)
        moved = moved + jnp.where(channel == 2 * tap_index + 1, along_x, 0.0)
    moved_low = moved.astype(bf16)
    padded_ref[...] = jnp.zeros_like(padded_ref)
    padded_ref[pl.ds(2 * side, pixels), :] = act_ref[...].astype(f32)
    build_taps(padded_ref, shifted_ref, pixels, side)
    sums_ref[...] = jnp.zeros_like(sums_ref)
    grad_offsets_ref[...] = jnp.zeros_like(grad_offsets_ref)
    for tap_index in range(9):
        taps = tap_of(shifted_ref, tap_index, pixels, side)
        first = tap_index * outs
        grad_offsets_ref[first : first + outs, :] = dot_tn(moved_low, taps)
        tap_rows_out(
            sums_ref, tap_index, pixels, side, dot_nt(moved_low, weights_ref[tap_index])
        )
    grad_ref[...] = grad_ref[...] + fold_columns(sums_ref, pixels, side)
    norm_two_slope(grad_ref, first_ref, first_stats_ref, mask_ref, gain_ref, bias_ref, 0, copies_ref)


def back_between_body(
    total_ref, grad_ref, first_ref, first_stats_ref, grad_sum_ref, summed_ref, pre_ref, stats_ref,
    mask_ref, count_ref, gain_ref, squeeze_ref,
    low_ref, wide_ref, next_ref, copies_ref, result_ref,
):
    pixels, width = first_ref.shape
    channels = pre_ref.shape[1]
    low_second(
        total_ref, grad_ref, first_ref, first_stats_ref, mask_ref, count_ref,
        gain_ref[:, :width], low_ref, result_ref,
    )
    wide_ref[...] = low_ref[...].astype(f32)
    flush(low_ref)
    flush(wide_ref)
    for ref in (grad_sum_ref, summed_ref, pre_ref, stats_ref, squeeze_ref):
        need(ref)
    mean, var = (stats_ref[0:1, :], stats_ref[1:2, :])
    inverse = lax.rsqrt(var + eps_norm)
    sums, prods = ([], [])
    for start, size in spans_of(channels, 512):
        span = pl.ds(start, size)
        cut = slice(start, start + size)
        next_ref[:, span] = dot_nt(low_ref[...], squeeze_ref[start : start + size, :])

        def both(rows):
            mask = wide_mask(mask_ref, rows, size)
            slope = silu_slope(summed_ref[rows, span])
            grad = (next_ref[rows, span] + grad_sum_ref[rows, span]) * mask * slope
            next_ref[rows, span] = grad
            return (grad, grad * ((pre_ref[rows, span] - mean[:, cut]) * inverse[:, cut]))

        total_grad, total_prod = two_sums(pixels, size, both)
        sums.append(total_grad)
        prods.append(total_prod)
    write_copies(copies_ref, sums + prods)


def last_low_body(
    total_ref, grad_ref, first_ref, first_stats_ref, mask_ref, count_ref, gain_ref,
    low_ref, wide_ref, result_ref,
):
    width = first_ref.shape[1]
    low_second(
        total_ref, grad_ref, first_ref, first_stats_ref, mask_ref, count_ref,
        gain_ref[:, :width], low_ref, result_ref,
    )
    wide_ref[...] = low_ref[...].astype(f32)


def last_body(low_ref, grad_sum_ref, squeeze_ref, image_ref, token_ref):
    token_ref[...] = jnp.zeros_like(token_ref)
    for start, size in spans_of(image_ref.shape[1], 256):
        block = dot_nt(low_ref[...], squeeze_ref[start : start + size, :])
        image_ref[:, start : start + size] = (
            block + grad_sum_ref[:, start : start + size]
        ).astype(bf16)


def sum_copies_body(copies_ref, out_ref):
    total = jnp.sum(copies_ref[...], axis=0)

    def one_copy(step, carry):
        out_ref[step] = total
        return carry

    lax.fori_loop(0, out_ref.shape[0], one_copy, 0)


block_cols = 256


def split_chunks(scratch_ref, keep_ref, send_ref, own, place, spot):
    for index in range(keep_ref.shape[0]):
        low = index & ((1 << place) - 1)
        base = ((index >> place) << (place + 1)) | low
        keep_ref[index, spot] = scratch_ref[base + own * (1 << place)]
        send_ref[index, spot] = scratch_ref[base + (1 - own) * (1 << place)]


def weights_body(kinds, firsts, spans, own_place_ref, *refs):
    groups = [refs[4 * place : 4 * place + 4] for place in range(len(kinds))]
    rest = refs[4 * len(kinds) :]
    streams = len(spans)
    outs, token_ref = (rest[: 2 * streams], rest[2 * streams])
    chunks_ref, scratch = (rest[2 * streams + 1], list(rest[2 * streams + 2 :]))
    token_ref[...] = jnp.zeros_like(token_ref)
    count, depth, _ = chunks_ref.shape
    makers = []
    for kind, (rows_ref, rows_other_ref, cols_ref, cols_other_ref) in zip(kinds, groups):
        for ref in (rows_ref, rows_other_ref, cols_ref, cols_other_ref):
            need(ref)
        pixels, half = cols_other_ref.shape
        side = 1 << ((pixels.bit_length() - 1) // 2)
        both_cols = scratch.pop(0)
        start_own = pl.multiple_of(own_place_ref[0, 0] * half, lane)
        both_cols[pl.ds(0, pixels), :] = cols_ref[:, pl.ds(start_own, half)]
        both_cols[pl.ds(pixels, pixels), :] = cols_other_ref[...].astype(bf16)
        if kind == "rows":
            both_rows = scratch.pop(0)
            both_rows[pl.ds(0, pixels), :] = rows_ref[...]
            both_rows[pl.ds(pixels, pixels), :] = rows_other_ref[...].astype(bf16)
            for start in range(0, half, block_cols):
                makers.append(
                    lambda rows=both_rows, cols=both_cols, start=start: dot_tn(
                        rows[...], cols[:, start : start + block_cols]
                    )
                )
        elif kind == "plain":
            padded, taps = (scratch.pop(0), (scratch.pop(0), scratch.pop(0)))
            for source, shifted in zip((rows_ref, rows_other_ref), taps):
                padded[...] = jnp.zeros_like(padded)
                padded[pl.ds(2 * side, pixels), :] = source[...]
                build_taps(padded, shifted, pixels, side)
            for tap in range(9):
                makers.append(
                    lambda taps=taps, cols=both_cols, tap=tap, pixels=pixels, side=side: dot_tn(
                        tap_of(taps[0], tap, pixels, side), cols[pl.ds(0, pixels), :]
                    )
                    + dot_tn(tap_of(taps[1], tap, pixels, side), cols[pl.ds(pixels, pixels), :])
                )
        else:
            width = cols_ref.shape[1]
            for tap in range(9):
                span = slice(tap * width, (tap + 1) * width)
                makers.append(
                    lambda one=rows_ref, two=rows_other_ref, cols=both_cols, span=span, pixels=pixels: dot_tn(
                        one[:, span], cols[pl.ds(0, pixels), :]
                    )
                    + dot_tn(two[:, span].astype(bf16), cols[pl.ds(pixels, pixels), :])
                )
    for stream, (start, stop) in enumerate(spans):
        bit = firsts[stream]
        own = own_place_ref[0, bit]
        for part in range(start, stop):
            chunks_ref[...] = makers[part]().reshape(count, depth, block_cols)
            split_chunks(
                chunks_ref, outs[2 * stream], outs[2 * stream + 1], own, bit - 1, part - start
            )
        flush(outs[2 * stream + 1])
        flush(outs[2 * stream])


def advance_body(groups, own_place_ref, *refs):
    streams = sum(count for count, _ in groups)
    kept, came = (refs[:streams], refs[streams : 2 * streams])
    outs = list(refs[2 * streams :])
    token_ref = outs.pop()
    token_ref[...] = jnp.zeros_like(token_ref)
    at, used, start = (0, 0, 0)
    for count, spot in groups:
        members = list(range(at, at + count))
        at += count
        for stream in members:
            need(kept[stream])
            need(came[stream])
        if spot is None:
            for stream in members:
                stop = start + kept[stream].shape[1]
                outs[-1][start:stop] = kept[stream][0] + came[stream][0]
                start = stop
            continue
        bit, place = spot
        own = own_place_ref[0, bit]
        for target_ref, side in ((outs[used + 1], 1 - own), (outs[used], own)):
            first = 0
            for stream in members:
                stop = first + kept[stream].shape[1]
                for index in range(target_ref.shape[0]):
                    low = index & ((1 << place) - 1)
                    base = ((index >> place) << (place + 1)) | low
                    chunk = base + side * (1 << place)
                    target_ref[index, first:stop] = kept[stream][chunk] + came[stream][chunk]
                first = stop
            flush(target_ref)
        used += 2


def assemble_body(kinds, labels, own_place_ref, own_ref, pair_ref, side_ref, both_ref, *targets):
    rows, cols = own_ref.shape[-2:]
    pair, line = (own_place_ref[0, 0], own_place_ref[0, 1])
    for row_at, col_at in ((0, 0), (0, 1), (1, 0), (1, 1)):
        same_row, same_col = (line == row_at, pair == col_at)
        row_span = slice(row_at * rows, (row_at + 1) * rows)
        for part, (place, step) in enumerate(labels):
            near = jnp.where(same_col, own_ref[part], pair_ref[part])
            far = jnp.where(same_col, side_ref[part], both_ref[part])
            value = jnp.where(same_row, near, far)
            target = targets[place]
            if kinds[place] == "rows":
                parts = target.shape[1] // 2 // cols
                at = (col_at * parts + step) * cols
                target[row_span, at : at + cols] = value
            else:
                target[step, row_span, col_at * cols : (col_at + 1) * cols] = value
    for target in targets:
        flush(target)


def gate_body(*refs):
    pass


def gate(arrays, after):
    hbm = pl.BlockSpec(memory_space=pltpu.HBM)
    return pl.pallas_call(
        gate_body,
        out_shape=tuple(shape_of(part.shape) for part in arrays),
        in_specs=[hbm] * len(arrays) + [pl.BlockSpec(memory_space=pl.ANY)] * len(after),
        out_specs=(hbm,) * len(arrays),
        input_output_aliases={place: place for place in range(len(arrays))},
    )(*arrays, *after)


class Comm:
    def __init__(self, wide_size, narrow_size):
        self.total = wide_size * narrow_size
        self.bits = self.total.bit_length() - 1
        self.low = narrow_size.bit_length() - 1
        self.index = lax.axis_index("wide") * narrow_size + lax.axis_index("narrow")
        self.places = jnp.stack([self.bit(place) for place in range(self.bits)])[None, :]

    def bit(self, place):
        return (self.index >> place) & 1

    def swap_over(self, values, flips):
        pairs = [(source, source ^ flips) for source in range(self.total)]
        return lax.ppermute(values, axes, pairs)

    def swap(self, values, place):
        return self.swap_over(values, 1 << place)

    def sync(self, copies):
        return Near(lax.all_to_all(copies, axes, 0, 0, tiled=True))

    def orders(self):
        outer = list(range(self.low, self.bits))
        inner = list(range(1, self.low))
        return (
            outer[:1] + inner + outer[1:],
            inner + outer[1:2] + outer[:1] + outer[2:],
            outer[1:2] + outer[:1] + inner + outer[2:],
        )


token = (8, lane)


class Group:
    def __init__(self, comm, total):
        self.comm = comm
        self.orders = comm.orders()
        self.left = [
            [place for place in range(1, comm.bits) if place != order[0]] for order in self.orders
        ]
        first = -(-total // 3)
        second = first + -(-(total - first) // 2)
        self.bounds = ((0, first), (first, second), (second, total))
        self.arrays = {}
        self.labels = []
        self.kinds = ()
        self.shapes = []
        self.at = 1

    def add(self, kind, group, after=()):
        comm = self.comm
        pixels, rows = group[0].shape
        if kind == "given":
            rows = group[2].shape[1]
        chunks = 1 << (comm.bits - 1)
        depth = rows // chunks
        half = getattr(group[3], "value", group[3]).shape[1]
        side = 1 << ((pixels.bit_length() - 1) // 2)
        scratch = [pltpu.VMEM((chunks, depth, block_cols), f32), pltpu.VMEM((2 * pixels, half), bf16)]
        self.shapes.append((2 * depth, 2 * half) if kind == "rows" else (9, 2 * depth, 2 * half))
        if kind == "rows":
            scratch.append(pltpu.VMEM((2 * pixels, rows), bf16))
        if kind == "plain":
            scratch.append(pltpu.VMEM((pixels + 4 * side, rows), f32))
            scratch += [pltpu.VMEM((3, pixels + 4 * side, rows), bf16)] * 2
        count = half // block_cols if kind == "rows" else 9
        begin = len(self.labels)
        self.labels += [(len(self.kinds), step) for step in range(count)]
        self.kinds += (kind,)
        keys, spans, outs, pieces, begun = ([], [], [], {}, {})
        for stream, (start, stop) in enumerate(self.bounds):
            low, high = (max(start, begin), min(stop, begin + count))
            if low >= high:
                continue
            spans.append((low - begin, high - begin))
            keys.append(stream)
            for which in range(2):
                if (stream, which) in self.arrays:
                    begun[len(outs)] = self.arrays[stream, which]
                pieces[len(outs)] = (low - start, high - low)
                outs.append(shape_of((chunks // 2, stop - start, depth, block_cols)))
        args = (comm.places,) + tuple(group)
        made = call(
            functools.partial(
                weights_body, (kind,), tuple(self.orders[stream][0] for stream in keys), tuple(spans)
            ),
            outs + [shape_of(token)], args, (0,), scratch, after, tuple(range(1, len(args))),
            pieces=pieces, begun=begun,
        )
        for number, stream in enumerate(keys):
            self.arrays[stream, 0] = made[2 * number]
            self.arrays[stream, 1] = made[2 * number + 1]
        return made[-1]

    def start(self, after=()):
        sent = [self.arrays[stream, 1] for stream in range(len(self.orders))]
        sent = gate(sent, after) if after else sent
        self.streams = [
            [(self.arrays[stream, 0], self.comm.swap(sent[stream], order[0]))]
            for stream, order in enumerate(self.orders)
        ]

    def advance(self, after=()):
        comm = self.comm
        groups, outs = ([], [])
        last = self.at == len(self.orders[0])
        total = 0
        for order, left, members in zip(self.orders, self.left, self.streams):
            spot = None
            parts = sum(kept.shape[1] for kept, _ in members)
            shape = members[0][0].shape
            total += parts
            if not last:
                bit = order[self.at]
                spot = (bit, left.index(bit))
                left.remove(bit)
                outs += [shape_of((shape[0] // 2, parts) + shape[2:])] * 2
            groups.append((len(members), spot))
        if last:
            outs = [shape_of((total,) + shape[2:])]
        flat = [pair for members in self.streams for pair in members]
        *pieces, mark = call(
            functools.partial(advance_body, tuple(groups)),
            outs + [shape_of(token)],
            (comm.places, *(kept for kept, _ in flat), *(Near(came) for _, came in flat)),
            (0,), (), after, tuple(range(1, 1 + 2 * len(flat))),
        )
        if last:
            beside = comm.swap(pieces[0], 1)
            self.quarters = [pieces[0], comm.swap(pieces[0], 0), beside, comm.swap(beside, 0)]
        else:
            self.streams = [
                [(pieces[2 * place], comm.swap(pieces[2 * place + 1], order[self.at]))]
                for place, order in enumerate(self.orders)
            ]
        self.at += 1
        return mark

    def ended(self):
        return self.at > len(self.orders[0])

    def finish(self, after=()):
        while not self.ended():
            self.advance(after)
        kinds, shapes = (self.kinds, self.shapes)
        outs = [shape_of(shape) for shape in shapes]
        return call(
            functools.partial(assemble_body, kinds, tuple(self.labels)),
            outs, (self.comm.places, self.quarters[0], *(Near(part) for part in self.quarters[1:])), (0,), (), after,
        )


def per_device(
    wide_size, narrow_size, images, image_sizes, offset_shift, squeeze_one, offsets_one, spatial_one,
    expand_one, squeeze_two, spatial_two, expand_two, norm_gain_one, norm_bias_one, norm_gain_two,
    norm_bias_two, run_mean_one, run_var_one, run_mean_two, run_var_two, grad_output,
):
    comm = Comm(wide_size, narrow_size)
    side, channels = (images.shape[1], images.shape[3])
    pixels = side * side
    width = squeeze_one.shape[1]
    outs = offsets_one.shape[2]
    total = comm.total
    small = (total, 2 * width // lane, lane)
    large = (total, 2 * channels // lane, lane)
    flat = images.reshape(pixels, channels)
    grad_out = grad_output.reshape(pixels, channels)
    gain_one, bias_one = (norm_gain_one[None, :], norm_bias_one[None, :])
    gain_two, bias_two = (norm_gain_two[None, :], norm_bias_two[None, :])
    field = shape_of((pixels, width))
    field_low = shape_of((pixels, width), bf16)
    plane = shape_of((pixels, channels))
    plane_low = shape_of((pixels, channels), bf16)
    half_plane = shape_of((pixels, channels // 2))
    half_field = shape_of((pixels, width // 2))
    stats_small, stats_large = (shape_of((2, width)), shape_of((2, channels)))
    padded = pltpu.VMEM((pixels + 4 * side, width), f32)
    shifted = pltpu.VMEM((3, pixels + 4 * side, width), bf16)
    tap_sums = pltpu.VMEM((3, pixels + 4 * side, width), f32)

    first_one, mask, copies, images_half = call(
        first_body,
        (field, shape_of((pixels, lane)), shape_of((total, 2 * width // lane + 8, lane)), half_plane),
        (image_sizes, comm.places, flat, squeeze_one),
        (0, 1),
    )
    images_half = comm.swap(images_half, 0)
    copies = comm.sync(copies)
    (act_one, columns, columns_wide, offsets, second_one, copies, first_stats_one, count) = call(
        deform_body,
        (
            field_low, shape_of((pixels, 9 * width), bf16), shape_of((pixels, 9 * width)),
            shape_of((pixels, outs)), field, shape_of(small), stats_small, shape_of((8, lane)),
        ),
        (
            copies, first_one, mask, gain_one, bias_one, offsets_one,
            offset_shift.astype(f32)[None, :], spatial_one,
        ),
        (),
        (padded, shifted),
        (),
        (5, 7),
    )
    columns_wide = comm.swap(columns_wide, 0)
    copies = comm.sync(copies)
    act_second_one, act_second_wide_one, third_one, copies, second_stats_one = call(
        third_body,
        (field_low, field, plane, shape_of(large), stats_small),
        (copies, second_one, mask, count, gain_one, bias_one, expand_one), late=(6,),
    )
    act_second_wide_one = comm.swap(act_second_wide_one, 0)
    copies = comm.sync(copies)
    summed_one, low_two, low_half, first_two, copies, third_stats_one = call(
        between_body,
        (plane, plane_low, half_plane, field, shape_of(small), stats_large),
        (copies, third_one, flat, mask, count, comm.places, gain_one, bias_one, squeeze_two),
        (5,), late=(8,),
    )
    low_half = comm.swap(low_half, 0)
    copies = comm.sync(copies)
    act_wide_two, second_two, copies, first_stats_two = call(
        plain_body,
        (field, field, shape_of(small), stats_small),
        (copies, first_two, mask, count, gain_two, bias_two, spatial_two),
        (),
        (padded, shifted), late=(6,),
    )
    act_wide_two_other = comm.swap(act_wide_two, 0)
    copies = comm.sync(copies)
    act_second_two, act_second_wide_two, third_two, copies, second_stats_two = call(
        third_body,
        (field_low, field, plane, shape_of(large), stats_small),
        (copies, second_two, mask, count, gain_two, bias_two, expand_two), late=(6,),
    )
    act_second_wide_two = comm.swap(act_second_wide_two, 0)
    copies = comm.sync(copies)
    output_images, grad_sum_two, copies, third_stats_two = call(
        turn_body,
        (plane_low, plane, shape_of(large), stats_large),
        (copies, third_two, summed_one, grad_out, mask, count, gain_two, bias_two),
    )
    copies = comm.sync(copies)
    low_third_two, third_half, grad_second_two, copies, third_result_two = call(
        back_third_body,
        (plane_low, half_plane, field, shape_of(small), stats_large),
        (
            copies, grad_sum_two, third_two, third_stats_two, second_two, second_stats_two, mask, count,
            comm.places, gain_two, bias_two, expand_two,
        ),
        (8,), late=(4, 5, 11),
    )
    third_half = comm.swap(third_half, 0)
    copies = comm.sync(copies)
    blocks = channels // 2 // block_cols
    group_two = Group(comm, 2 * blocks + 9)
    group_one = Group(comm, 2 * blocks + 9)
    done = group_two.add("rows", (act_second_two, act_second_wide_two, low_third_two, Near(third_half)))
    low_second_two, second_half, grad_first_two, copies, second_result_two = call(
        back_plain_body,
        (field_low, half_field, field, shape_of(small), stats_small),
        (
            copies, grad_second_two, second_two, second_stats_two, first_two, first_stats_two, mask,
            count, comm.places, gain_two, bias_two, spatial_two,
        ),
        (8,),
        (tap_sums,),
        (done,),
        (11,),
    )
    second_half = comm.swap(second_half, 0)
    copies = comm.sync(copies)
    done = group_two.add("plain", (act_wide_two, act_wide_two_other, low_second_two, Near(second_half)))
    low_first_two, low_first_wide, grad_sum_one, copies, first_result_two = call(
        back_between_body,
        (field_low, field, plane, shape_of(large), stats_small),
        (
            copies, grad_first_two, first_two, first_stats_two, grad_sum_two, summed_one, third_one,
            third_stats_one, mask, count, gain_two, squeeze_two,
        ),
        (),
        (),
        (done,),
        (4, 5, 6, 7, 11),
    )
    low_first_wide = comm.swap(low_first_wide, 0)
    copies = comm.sync(copies)
    done = group_two.add("rows", (low_first_two, Near(low_first_wide), low_two, low_half))
    low_third_one, third_half, grad_second_one, copies, third_result_one = call(
        back_third_body,
        (plane_low, half_plane, field, shape_of(small), stats_large),
        (
            copies, grad_sum_one, third_one, third_stats_one, second_one, second_stats_one, mask, count,
            comm.places, gain_one, bias_one, expand_one,
        ),
        (8,),
        (),
        (done,),
        (4, 5, 11),
    )
    third_half = comm.swap(third_half, 0)
    copies = comm.sync(copies)
    done = group_one.add("rows", (act_second_one, act_second_wide_one, low_third_one, Near(third_half)))
    group_two.start((copies.value, done))
    slots = -(-9 * outs // total)
    slots = -(-slots // 8) * 8
    low_second_one, second_half, grad_first_one, copies, second_result_one, grad_offsets = call(
        back_deform_body,
        (
            field_low, half_field, field, shape_of(small), stats_small, shape_of((total * slots, width)),
        ),
        (
            copies, grad_second_one, second_one, second_stats_one, first_one, first_stats_one, mask,
            count, comm.places, gain_one, bias_one, spatial_one, act_one, offsets, offsets_one,
        ),
        (8,),
        (tap_sums, padded, shifted),
        (done,),
        (4, 5, 11, 12, 13, 14),
    )
    second_half = comm.swap(second_half, 0)
    copies = comm.sync(copies)
    done = group_one.add("given", (columns, columns_wide, low_second_one, Near(second_half)))
    done = group_two.advance((done,))
    low_first_one, low_first_wide, first_result_one = call(
        last_low_body,
        (field_low, field, stats_small),
        (copies, grad_first_one, first_one, first_stats_one, mask, count, gain_one),
        (),
        (),
        (done,),
    )
    low_first_wide = comm.swap(low_first_wide, 0)
    grad_offsets = comm.sync(grad_offsets.reshape(total, slots, width))
    grad_images, done = call(
        last_body,
        (plane_low, shape_of(token)),
        (low_first_one, grad_sum_one, squeeze_one),
    )
    done = group_one.add("rows", (low_first_one, Near(low_first_wide), flat, images_half), (done,))
    group_one.start()
    (grad_offsets,) = call(
        sum_copies_body, (shape_of((total, slots, width)),), (grad_offsets,), (), (),
        (done,),
    )
    grad_offsets = comm.sync(grad_offsets).value
    done = group_two.advance((done,))
    done = group_one.advance((done,))
    done = group_two.advance((done,))
    done = group_one.advance((done,))
    done = group_two.advance((done,))
    done = group_one.advance((done,))
    grad_expand_two, grad_spatial_two, grad_squeeze_two = group_two.finish((done,))
    grad_expand_one, grad_spatial_one, grad_squeeze_one = group_one.finish()

    def laid(parts, row):
        return jnp.concatenate([part[row] for part in parts])

    results_one = (first_result_one, second_result_one, third_result_one)
    results_two = (first_result_two, second_result_two, third_result_two)
    stats_one = (first_stats_one, second_stats_one, third_stats_one)
    stats_two = (first_stats_two, second_stats_two, third_stats_two)
    pixel_count = count[0, 0]
    unbias = pixel_count / (pixel_count - 1.0)
    fresh = 1.0 - keep_rate
    return (
        output_images.reshape(images.shape),
        grad_images.reshape(images.shape),
        grad_squeeze_one.T,
        grad_offsets.reshape(total * slots, width)[: 9 * outs].reshape(9, outs, width).transpose(0, 2, 1),
        grad_spatial_one,
        grad_expand_one,
        grad_squeeze_two.T,
        grad_spatial_two,
        grad_expand_two,
        laid(results_one, 1),
        laid(results_one, 0),
        laid(results_two, 1),
        laid(results_two, 0),
        keep_rate * run_mean_one + fresh * laid(stats_one, 0),
        keep_rate * run_var_one + fresh * laid(stats_one, 1) * unbias,
        keep_rate * run_mean_two + fresh * laid(stats_two, 0),
        keep_rate * run_var_two + fresh * laid(stats_two, 1) * unbias,
    )


def solution(mesh):
    images_spec = P(axes, None, None, None)
    whole = P()
    return jax.shard_map(
        functools.partial(per_device, mesh.shape["wide"], mesh.shape["narrow"]),
        mesh=mesh,
        in_specs=(images_spec, P(axes, None)) + (whole,) * 16 + (images_spec,),
        out_specs=(
            images_spec,
            images_spec,
            P(None, "wide"),
            whole,
            P(None, "wide", None),
            P("wide", None),
            P(None, "wide"),
            P(None, "wide", None),
            P("wide", None),
        )
        + (whole,) * 8,
        check_vma=False,
    )
```

```python
import functools

import jax
import jax.numpy as jnp
from jax import lax
from jax.experimental import pallas as pl
from jax.experimental.pallas import tpu as pltpu
from jax.sharding import PartitionSpec as P

eps_norm = 1e-05
keep_rate = 0.6
vmem_bytes = 52 * 1024 * 1024
lane = 128
tile_rows = 16
axes = ("wide", "narrow")
f32 = jnp.float32
bf16 = jnp.bfloat16


def shape_of(shape, kind=f32):
    return jax.ShapeDtypeStruct(shape, kind)


copies_of = {}


def need(ref):
    entry = copies_of.get(id(ref))
    if entry is not None and entry[1]:
        entry[1] = False
        entry[0].wait()
    return ref


def flush(ref):
    entry = copies_of.get(id(ref))
    if entry is not None and entry[1]:
        entry[1] = False
        entry[0].start()


class Near:
    def __init__(self, value):
        self.value = value


def call(body, outs, args, smem=(), scratch=(), after=(), late=(), stay_out=(), pieces=None, begun=None):
    stay = tuple(place for place, arg in enumerate(args) if isinstance(arg, Near))
    args = tuple(arg.value if isinstance(arg, Near) else arg for arg in args)
    pieces = pieces or {}
    begun = begun or {}
    hbm = pl.BlockSpec(memory_space=pltpu.HBM)
    vmem = pl.BlockSpec(memory_space=pltpu.VMEM)
    specs = [
        pl.BlockSpec(memory_space=pltpu.SMEM) if place in smem else vmem if place in stay else hbm
        for place in range(len(args))
    ] + [pl.BlockSpec(memory_space=pl.ANY)] * len(after) + [hbm] * len(begun)
    moved = [place for place in range(len(args)) if place not in smem and place not in stay]
    used, extra, made = (len(args), len(after) + len(begun), len(outs))
    sent = [slot for slot in range(made) if slot not in stay_out]

    def kernel(*refs):
        given = list(refs[:used])
        results = list(refs[used + extra : used + extra + made])
        rest = refs[used + extra + made :]
        in_slots, out_slots = (rest[: len(moved)], rest[len(moved) : len(moved) + len(sent)])
        in_flags, out_flags = rest[len(moved) + len(sent) : len(moved) + len(sent) + 2]
        copies_of.clear()
        for slot, place in enumerate(moved):
            copy = pltpu.make_async_copy(given[place], in_slots[slot], in_flags.at[slot])
            copy.start()
            copies_of[id(in_slots[slot])] = [copy, True]
            given[place] = in_slots[slot]
        for place in moved:
            if place not in late:
                need(given[place])
        for slot, place in enumerate(sent):
            copies_of[id(out_slots[slot])] = [
                pltpu.make_async_copy(
                    out_slots[slot],
                    results[place].at[:, pl.ds(*pieces[place])] if place in pieces else results[place],
                    out_flags.at[slot],
                ),
                True,
            ]
            results[place] = out_slots[slot]
        body(*given, *results, *rest[len(moved) + len(sent) + 2 :])
        for place in moved:
            need(given[place])
        for slot in out_slots:
            if copies_of[id(slot)][1]:
                flush(slot)
        for slot in out_slots:
            copies_of[id(slot)][0].wait()
        copies_of.clear()

    slots = [pltpu.VMEM(args[place].shape, args[place].dtype) for place in moved]
    for place in sent:
        shape = outs[place].shape
        if place in pieces:
            shape = (shape[0], pieces[place][1]) + shape[2:]
        slots.append(pltpu.VMEM(shape, outs[place].dtype))
    flags = [pltpu.SemaphoreType.DMA((max(len(moved), 1),)), pltpu.SemaphoreType.DMA((max(len(sent), 1),))]
    return pl.pallas_call(
        kernel,
        input_output_aliases={used + len(after) + at: place for at, place in enumerate(begun)},
        out_shape=tuple(outs),
        in_specs=specs,
        out_specs=tuple(vmem if place in stay_out else hbm for place in range(made)),
        scratch_shapes=slots + flags + list(scratch),
        compiler_params=pltpu.CompilerParams(vmem_limit_bytes=vmem_bytes),
    )(*args, *after, *begun.values())


def dot_nn(first_op, second_op):
    return lax.dot_general(
        first_op, second_op, (((1,), (0,)), ((), ())), preferred_element_type=f32
    )


def dot_nt(first_op, second_op):
    return lax.dot_general(
        first_op, second_op, (((1,), (1,)), ((), ())), preferred_element_type=f32
    )


def dot_tn(first_op, second_op):
    return lax.dot_general(
        first_op, second_op, (((0,), (0,)), ((), ())), preferred_element_type=f32
    )


def logistic(values):
    return 0.5 * jnp.tanh(0.5 * values) + 0.5


def silu(values):
    return values * logistic(values)


def silu_slope(values):
    gate = logistic(values)
    return gate * (1.0 + values * (1.0 - gate))


def flat_row(rows, start, width):
    first = start // lane
    return jnp.concatenate(
        [rows[first + step : first + step + 1, :] for step in range(width // lane)], axis=1
    )


def fold_row(row):
    return [row[:, step * lane : (step + 1) * lane] for step in range(row.shape[1] // lane)]


def write_copies(copies_ref, rows, extra=None):
    packed = jnp.concatenate([piece for row in rows for piece in fold_row(row)], axis=0)
    if extra is not None:
        packed = jnp.concatenate([packed, extra], axis=0)

    def one_copy(step, carry):
        copies_ref[step] = packed
        return carry

    lax.fori_loop(0, copies_ref.shape[0], one_copy, 0)


def read_copies(copies_ref):
    return jnp.sum(copies_ref[...], axis=0)


def wide_mask(mask_ref, rows, width):
    return jnp.concatenate([mask_ref[rows, :]] * (width // lane), axis=1)


def eight_rows(values):
    folded = values[:8]
    for start in range(8, values.shape[0], 8):
        folded = folded + values[start : start + 8]
    return folded


def row_loop(pixels, body, carry):
    def step(index, state):
        return body(pl.ds(pl.multiple_of(index * tile_rows, tile_rows), tile_rows), state)

    return lax.fori_loop(0, pixels // tile_rows, step, carry)


def two_sums(pixels, width, body):
    zero = jnp.zeros((8, width), f32)

    def step(rows, state):
        first, second = body(rows)
        return (state[0] + eight_rows(first), state[1] + eight_rows(second))

    first, second = row_loop(pixels, step, (zero, zero))
    return (jnp.sum(first, axis=0, keepdims=True), jnp.sum(second, axis=0, keepdims=True))


def moments(total, width, count):
    mean = flat_row(total, 0, width) / count
    var = flat_row(total, width, width) / count - mean * mean
    return (mean, var)


def scale_shift(mean, var, gain, bias):
    inverse = lax.rsqrt(var + eps_norm)
    scale = gain * inverse
    return (scale, bias - mean * scale)


def spans_of(width, block):
    return [(start, min(block, width - start)) for start in range(0, width, block)]


def grad_rows(total, stats, gain, count, width):
    mean, var = (stats[0:1], stats[1:2])
    inverse = lax.rsqrt(var + eps_norm)
    sum_grad = flat_row(total, 0, width)
    sum_prod = flat_row(total, width, width)
    return (
        gain * inverse,
        sum_grad / count,
        inverse * sum_prod / count,
        mean,
        sum_grad,
        sum_prod,
    )


def build_taps(act_ref, shifted_ref, pixels, side):
    pad = 2 * side
    width = act_ref.shape[1]
    column = lax.broadcasted_iota(jnp.int32, (pixels, lane), 0) % side
    for tap_col in range(3):
        move = 2 * (tap_col - 1)
        moved = act_ref[pl.ds(pad + move, pixels), :]
        if move:
            inside = (column + move >= 0) & (column + move < side)
            keep = jnp.concatenate([inside.astype(f32)] * (width // lane), axis=1)
            moved = moved * keep
        shifted_ref[tap_col, pl.ds(0, pad), :] = jnp.zeros((pad, width), bf16)
        shifted_ref[tap_col, pl.ds(pad + pixels, pad), :] = jnp.zeros((pad, width), bf16)
        shifted_ref[tap_col, pl.ds(pad, pixels), :] = moved.astype(bf16)


def tap_of(shifted_ref, tap_index, pixels, side):
    tap_row, tap_col = (tap_index // 3, tap_index % 3)
    return shifted_ref[tap_col, pl.ds(2 * side * tap_row, pixels), :]


def fold_columns(sums_ref, pixels, side):
    pad = 2 * side
    width = sums_ref.shape[2]
    column = lax.broadcasted_iota(jnp.int32, (pixels, lane), 0) % side
    total = sums_ref[1, pl.ds(pad, pixels), :]
    for tap_col in (0, 2):
        move = 2 * (tap_col - 1)
        inside = (column - move >= 0) & (column - move < side)
        keep = jnp.concatenate([inside.astype(f32)] * (width // lane), axis=1)
        total = total + keep * sums_ref[tap_col, pl.ds(pad - move, pixels), :]
    return total


def tap_rows_out(sums_ref, tap_index, pixels, side, values):
    tap_row, tap_col = (tap_index // 3, tap_index % 3)
    rows = pl.ds(2 * side * tap_row, pixels)
    sums_ref[tap_col, rows, :] = sums_ref[tap_col, rows, :] + values


def tap_factors(offsets, tap_index, side):
    pixels = offsets.shape[0]
    tap_row, tap_col = (tap_index // 3, tap_index % 3)
    shape = (pixels, pixels)
    position = lax.broadcasted_iota(jnp.int32, shape, 0)
    source = lax.broadcasted_iota(jnp.int32, shape, 1)
    gap_y = (position // side - source // side + 2 * (tap_row - 1)).astype(f32)
    gap_x = (position % side - source % side + 2 * (tap_col - 1)).astype(f32)
    dist_y = gap_y + offsets[:, 2 * tap_index : 2 * tap_index + 1]
    dist_x = gap_x + offsets[:, 2 * tap_index + 1 : 2 * tap_index + 2]
    bump_y = jnp.maximum(1.0 - dist_y * dist_y, 0.0)
    bump_x = jnp.maximum(1.0 - dist_x * dist_x, 0.0)
    return (dist_y, dist_x, bump_y, bump_x)


def first_body(sizes_ref, place_ref, images_ref, squeeze_ref, pre_ref, mask_ref, copies_ref, half_ref):
    pixels, width = pre_ref.shape
    side = 1 << ((pixels.bit_length() - 1) // 2)
    position = lax.broadcasted_iota(jnp.int32, (pixels, lane), 0)
    inside = (position // side < sizes_ref[0, 0]) & (position % side < sizes_ref[0, 1])
    mask = inside.astype(f32)
    mask_ref[...] = mask
    pre_ref[...] = dot_nn(images_ref[...], squeeze_ref[...])

    def both(rows):
        values = pre_ref[rows, :]
        masked = values * wide_mask(mask_ref, rows, width)
        return (masked, masked * values)

    sums = two_sums(pixels, width, both)
    amount = jnp.sum(mask, axis=0, keepdims=True)
    write_copies(copies_ref, sums, jnp.broadcast_to(amount, (8, lane)))
    half = half_ref.shape[1]
    other = pl.multiple_of((1 - place_ref[0, 0]) * half, lane)
    half_ref[...] = images_ref[:, pl.ds(other, half)].astype(f32)


def activate(pre_ref, mask_ref, scale, shift, out_ref, base=0):
    pixels, width = pre_ref.shape

    def step(rows, carry):
        out = silu(pre_ref[rows, :] * scale + shift) * wide_mask(mask_ref, rows, width)
        target = pl.ds(rows.start + base, tile_rows)
        out_ref[target, :] = out.astype(bf16).astype(out_ref.dtype)
        return carry

    row_loop(pixels, step, 0)


def masked_sums(values_ref, mask_ref):
    pixels, width = values_ref.shape

    def both(rows):
        values = values_ref[rows, :]
        masked = values * wide_mask(mask_ref, rows, width)
        return (masked, masked * values)

    return two_sums(pixels, width, both)


def deform_body(
    total_ref, pre_ref, mask_ref, gain_ref, bias_ref, weights_ref, move_ref, spatial_ref,
    act_ref, wide_ref, columns_ref, offsets_ref, second_ref, copies_ref, stats_ref,
    count_ref, padded_ref, shifted_ref,
):
    pixels, width = pre_ref.shape
    side = 1 << ((pixels.bit_length() - 1) // 2)
    total = read_copies(total_ref)
    count = total[2 * width // lane : 2 * width // lane + 1, 0:1]
    count_ref[...] = jnp.broadcast_to(count, (8, lane))
    mean, var = moments(total, width, count)
    stats_ref[...] = jnp.concatenate([mean, var], axis=0)
    scale, shift = scale_shift(mean, var, gain_ref[:, :width], bias_ref[:, :width])
    padded_ref[...] = jnp.zeros_like(padded_ref)
    activate(pre_ref, mask_ref, scale, shift, padded_ref, 2 * side)
    wide_ref[...] = padded_ref[pl.ds(2 * side, pixels), :]
    flush(wide_ref)
    act_ref[...] = wide_ref[...].astype(bf16)
    build_taps(padded_ref, shifted_ref, pixels, side)
    flush(act_ref)
    offsets = move_ref[...]
    need(weights_ref)
    for tap_index in range(9):
        taps = tap_of(shifted_ref, tap_index, pixels, side)
        offsets = offsets + dot_nn(taps, weights_ref[tap_index])
    offsets_ref[...] = offsets
    flush(offsets_ref)
    need(spatial_ref)
    second_ref[...] = jnp.zeros_like(second_ref)
    for tap_index in range(9):
        dist_y, dist_x, bump_y, bump_x = tap_factors(offsets, tap_index, side)
        root = bump_y * bump_x
        columns = dot_nn((root * root).astype(bf16), act_ref[...]).astype(bf16)
        span = pl.ds(tap_index * width, width)
        columns_ref[:, span] = columns
        second_ref[...] = second_ref[...] + dot_nn(columns, spatial_ref[tap_index])
    flush(columns_ref)
    write_copies(copies_ref, masked_sums(second_ref, mask_ref))


def columns_body(act_ref, offsets_ref, columns_ref, low_ref):
    pixels, width = act_ref.shape
    side = 1 << ((pixels.bit_length() - 1) // 2)
    low_ref[...] = act_ref[...].astype(bf16)
    offsets = offsets_ref[...]
    for tap_index in range(9):
        _, _, bump_y, bump_x = tap_factors(offsets, tap_index, side)
        root = bump_y * bump_x
        span = pl.ds(tap_index * width, width)
        columns_ref[:, span] = dot_nn((root * root).astype(bf16), low_ref[...]).astype(bf16)


def plain_body(
    total_ref, pre_ref, mask_ref, count_ref, gain_ref, bias_ref, spatial_ref,
    wide_ref, second_ref, copies_ref, stats_ref,
    padded_ref, shifted_ref,
):
    pixels, width = pre_ref.shape
    side = 1 << ((pixels.bit_length() - 1) // 2)
    total = read_copies(total_ref)
    mean, var = moments(total, width, count_ref[0:1, 0:1])
    stats_ref[...] = jnp.concatenate([mean, var], axis=0)
    scale, shift = scale_shift(mean, var, gain_ref[:, :width], bias_ref[:, :width])
    padded_ref[...] = jnp.zeros_like(padded_ref)
    activate(pre_ref, mask_ref, scale, shift, padded_ref, 2 * side)
    wide_ref[...] = padded_ref[pl.ds(2 * side, pixels), :]
    flush(wide_ref)
    build_taps(padded_ref, shifted_ref, pixels, side)
    need(spatial_ref)
    second_ref[...] = jnp.zeros_like(second_ref)
    for tap_index in range(9):
        taps = tap_of(shifted_ref, tap_index, pixels, side)
        second_ref[...] = second_ref[...] + dot_nn(taps, spatial_ref[tap_index])
    write_copies(copies_ref, masked_sums(second_ref, mask_ref))


def third_body(
    total_ref, pre_ref, mask_ref, count_ref, gain_ref, bias_ref, expand_ref,
    act_ref, wide_ref, third_ref, copies_ref, stats_ref,
):
    pixels, width = pre_ref.shape
    channels = third_ref.shape[1]
    total = read_copies(total_ref)
    mean, var = moments(total, width, count_ref[0:1, 0:1])
    stats_ref[...] = jnp.concatenate([mean, var], axis=0)
    scale, shift = scale_shift(
        mean, var, gain_ref[:, width : 2 * width], bias_ref[:, width : 2 * width]
    )
    activate(pre_ref, mask_ref, scale, shift, act_ref)
    wide_ref[...] = act_ref[...].astype(f32)
    flush(act_ref)
    flush(wide_ref)
    need(expand_ref)
    sums, squares = ([], [])
    for start, size in spans_of(channels, 256):
        block = dot_nn(act_ref[...], expand_ref[:, start : start + size])
        third_ref[:, start : start + size] = block
        sums.append(jnp.sum(block, axis=0, keepdims=True))
        squares.append(jnp.sum(block * block, axis=0, keepdims=True))
    flush(third_ref)
    write_copies(copies_ref, sums + squares)


def between_body(
    total_ref, pre_ref, images_ref, mask_ref, count_ref, place_ref, gain_ref, bias_ref, squeeze_ref,
    summed_ref, low_ref, half_ref, first_ref, copies_ref, stats_ref,
):
    pixels, channels = pre_ref.shape
    total = read_copies(total_ref)
    mean, var = moments(total, channels, count_ref[0:1, 0:1])
    stats_ref[...] = jnp.concatenate([mean, var], axis=0)
    begin = gain_ref.shape[1] - channels
    scale, shift = scale_shift(mean, var, gain_ref[:, begin:], bias_ref[:, begin:])
    for start, size in spans_of(channels, 512):
        span = pl.ds(start, size)

        def step(rows, carry):
            summed = (
                pre_ref[rows, span] * scale[:, start : start + size]
                + shift[:, start : start + size]
                + images_ref[rows, span].astype(f32)
            )
            summed_ref[rows, span] = summed
            low_ref[rows, span] = (silu(summed) * wide_mask(mask_ref, rows, size)).astype(bf16)
            return carry

        row_loop(pixels, step, 0)
    flush(summed_ref)
    flush(low_ref)
    need(squeeze_ref)
    sums, squares = ([], [])
    for start, size in spans_of(first_ref.shape[1], 256):
        block = dot_nn(low_ref[...], squeeze_ref[:, start : start + size])
        first_ref[:, start : start + size] = block
        sums.append(jnp.sum(block, axis=0, keepdims=True))
        squares.append(jnp.sum(block * block, axis=0, keepdims=True))
    write_copies(copies_ref, sums + squares)
    half = half_ref.shape[1]
    other = pl.multiple_of((1 - place_ref[0, 0]) * half, lane)
    half_ref[...] = low_ref[:, pl.ds(other, half)].astype(f32)


def turn_body(
    total_ref, pre_ref, before_ref, grad_ref, mask_ref, count_ref, gain_ref, bias_ref,
    image_ref, grad_sum_ref, copies_ref, stats_ref,
):
    pixels, channels = pre_ref.shape
    total = read_copies(total_ref)
    mean, var = moments(total, channels, count_ref[0:1, 0:1])
    stats_ref[...] = jnp.concatenate([mean, var], axis=0)
    begin = gain_ref.shape[1] - channels
    scale, shift = scale_shift(mean, var, gain_ref[:, begin:], bias_ref[:, begin:])
    inverse = lax.rsqrt(var + eps_norm)
    sums, prods = ([], [])
    for start, size in spans_of(channels, 512):
        span = pl.ds(start, size)
        cut = slice(start, start + size)

        def both(rows):
            mask = wide_mask(mask_ref, rows, size)
            pre = pre_ref[rows, span]
            summed = pre * scale[:, cut] + shift[:, cut] + silu(before_ref[rows, span]) * mask
            gate = logistic(summed)
            image_ref[rows, span] = (summed * gate * mask).astype(bf16)
            slope = gate * (1.0 + summed * (1.0 - gate))
            grad = grad_ref[rows, span].astype(f32) * mask * slope
            grad_sum_ref[rows, span] = grad
            return (grad, grad * ((pre - mean[:, cut]) * inverse[:, cut]))

        total_grad, total_prod = two_sums(pixels, size, both)
        sums.append(total_grad)
        prods.append(total_prod)
    flush(image_ref)
    flush(grad_sum_ref)
    write_copies(copies_ref, sums + prods)


def low_gradient(rows, width, start, grad, pre, mask, coefs):
    cut = slice(start, start + width)
    scale, mean_grad, mean_prod, mean = (part[:, cut] for part in coefs[:4])
    return scale * (grad - mask * (mean_grad + (pre - mean) * mean_prod))


def back_third_body(
    total_ref, grad_sum_ref, pre_ref, stats_ref, second_ref, second_stats_ref, mask_ref, count_ref,
    place_ref, gain_ref, bias_ref, expand_ref,
    low_ref, half_ref, grad_ref, copies_ref, result_ref,
):
    pixels, channels = pre_ref.shape
    width = second_ref.shape[1]
    total = read_copies(total_ref)
    coefs = grad_rows(
        total, stats_ref[...], gain_ref[:, 2 * width :], count_ref[0:1, 0:1], channels
    )
    result_ref[...] = jnp.concatenate(coefs[4:6], axis=0)
    for start, size in spans_of(channels, 512):
        span = pl.ds(start, size)

        def step(rows, carry):
            mask = wide_mask(mask_ref, rows, size)
            low_ref[rows, span] = low_gradient(
                rows, size, start, grad_sum_ref[rows, span], pre_ref[rows, span], mask, coefs
            ).astype(bf16)
            return carry

        row_loop(pixels, step, 0)
    half = half_ref.shape[1]
    other = pl.multiple_of((1 - place_ref[0, 0]) * half, lane)
    half_ref[...] = low_ref[:, pl.ds(other, half)].astype(f32)
    flush(low_ref)
    flush(half_ref)
    for ref in (expand_ref, second_ref, second_stats_ref):
        need(ref)
    for start, size in spans_of(width, 256):
        grad_ref[:, start : start + size] = dot_nt(low_ref[...], expand_ref[start : start + size, :])
    norm_two_slope(grad_ref, second_ref, second_stats_ref, mask_ref, gain_ref, bias_ref, width, copies_ref)


def norm_two_slope(grad_ref, pre_ref, stats_ref, mask_ref, gain_ref, bias_ref, begin, copies_ref):
    pixels, width = pre_ref.shape
    mean, var = (stats_ref[0:1, :], stats_ref[1:2, :])
    inverse = lax.rsqrt(var + eps_norm)
    scale, shift = scale_shift(
        mean, var, gain_ref[:, begin : begin + width], bias_ref[:, begin : begin + width]
    )

    def both(rows):
        pre = pre_ref[rows, :]
        slope = silu_slope(pre * scale + shift)
        grad = grad_ref[rows, :] * slope * wide_mask(mask_ref, rows, width)
        grad_ref[rows, :] = grad
        return (grad, grad * ((pre - mean) * inverse))

    write_copies(copies_ref, two_sums(pixels, width, both))


def low_second(total_ref, grad_ref, pre_ref, stats_ref, mask_ref, count_ref, gain, low_ref, result_ref):
    pixels, width = pre_ref.shape
    total = read_copies(total_ref)
    coefs = grad_rows(total, stats_ref[...], gain, count_ref[0:1, 0:1], width)
    result_ref[...] = jnp.concatenate(coefs[4:6], axis=0)

    def step(rows, carry):
        mask = wide_mask(mask_ref, rows, width)
        low_ref[rows, :] = low_gradient(
            rows, width, 0, grad_ref[rows, :], pre_ref[rows, :], mask, coefs
        ).astype(bf16)
        return carry

    row_loop(pixels, step, 0)


def back_plain_body(
    total_ref, grad_in_ref, second_ref, second_stats_ref, first_ref, first_stats_ref, mask_ref,
    count_ref, place_ref, gain_ref, bias_ref, spatial_ref,
    low_ref, half_ref, grad_ref, copies_ref, result_ref,
    sums_ref,
):
    pixels, width = second_ref.shape
    side = 1 << ((pixels.bit_length() - 1) // 2)
    low_second(
        total_ref, grad_in_ref, second_ref, second_stats_ref, mask_ref, count_ref,
        gain_ref[:, width : 2 * width], low_ref, result_ref,
    )
    half = half_ref.shape[1]
    other = pl.multiple_of((1 - place_ref[0, 0]) * half, lane)
    half_ref[...] = low_ref[:, pl.ds(other, half)].astype(f32)
    flush(low_ref)
    flush(half_ref)
    need(spatial_ref)
    sums_ref[...] = jnp.zeros_like(sums_ref)
    for tap_index in range(9):
        tap_rows_out(
            sums_ref, tap_index, pixels, side, dot_nt(low_ref[...], spatial_ref[tap_index])
        )
    grad_ref[...] = fold_columns(sums_ref, pixels, side)
    norm_two_slope(grad_ref, first_ref, first_stats_ref, mask_ref, gain_ref, bias_ref, 0, copies_ref)


def back_deform_body(
    total_ref, grad_in_ref, second_ref, second_stats_ref, first_ref, first_stats_ref, mask_ref,
    count_ref, place_ref, gain_ref, bias_ref, spatial_ref, act_ref, offsets_ref, weights_ref,
    low_ref, half_ref, grad_ref, copies_ref, result_ref, grad_offsets_ref,
    sums_ref, padded_ref, shifted_ref,
):
    pixels, width = second_ref.shape
    side = 1 << ((pixels.bit_length() - 1) // 2)
    low_second(
        total_ref, grad_in_ref, second_ref, second_stats_ref, mask_ref, count_ref,
        gain_ref[:, width : 2 * width], low_ref, result_ref,
    )
    half = half_ref.shape[1]
    other = pl.multiple_of((1 - place_ref[0, 0]) * half, lane)
    half_ref[...] = low_ref[:, pl.ds(other, half)].astype(f32)
    flush(low_ref)
    flush(half_ref)
    for ref in (first_ref, first_stats_ref, spatial_ref, act_ref, offsets_ref, weights_ref):
        need(ref)
    offsets = offsets_ref[...]
    outs = offsets.shape[1]
    channel = lax.broadcasted_iota(jnp.int32, (pixels, outs), 1)
    moved = jnp.zeros((pixels, outs), f32)
    grad_ref[...] = jnp.zeros_like(grad_ref)
    for tap_index in range(9):
        dist_y, dist_x, bump_y, bump_x = tap_factors(offsets, tap_index, side)
        weight_y, weight_x = (bump_y * bump_y, bump_x * bump_x)
        sampling = (weight_y * weight_x).astype(bf16)
        piece = dot_nt(low_ref[...], spatial_ref[tap_index]).astype(bf16)
        grad_ref[...] = grad_ref[...] + dot_tn(sampling, piece)
        product = -4.0 * dot_nt(piece, act_ref[...])
        along_y = jnp.sum(product * (dist_y * bump_y * weight_x), axis=1, keepdims=True)
        along_x = jnp.sum(product * (dist_x * bump_x * weight_y), axis=1, keepdims=True)
        moved = moved + jnp.where(channel == 2 * tap_index, along_y, 0.0)
        moved = moved + jnp.where(channel == 2 * tap_index + 1, along_x, 0.0)
    moved_low = moved.astype(bf16)
    padded_ref[...] = jnp.zeros_like(padded_ref)
    padded_ref[pl.ds(2 * side, pixels), :] = act_ref[...].astype(f32)
    build_taps(padded_ref, shifted_ref, pixels, side)
    sums_ref[...] = jnp.zeros_like(sums_ref)
    grad_offsets_ref[...] = jnp.zeros_like(grad_offsets_ref)
    for tap_index in range(9):
        taps = tap_of(shifted_ref, tap_index, pixels, side)
        first = tap_index * outs
        grad_offsets_ref[first : first + outs, :] = dot_tn(moved_low, taps)
        tap_rows_out(
            sums_ref, tap_index, pixels, side, dot_nt(moved_low, weights_ref[tap_index])
        )
    grad_ref[...] = grad_ref[...] + fold_columns(sums_ref, pixels, side)
    norm_two_slope(grad_ref, first_ref, first_stats_ref, mask_ref, gain_ref, bias_ref, 0, copies_ref)


def back_between_body(
    total_ref, grad_ref, first_ref, first_stats_ref, grad_sum_ref, summed_ref, pre_ref, stats_ref,
    mask_ref, count_ref, gain_ref, squeeze_ref,
    low_ref, wide_ref, next_ref, copies_ref, result_ref,
):
    pixels, width = first_ref.shape
    channels = pre_ref.shape[1]
    low_second(
        total_ref, grad_ref, first_ref, first_stats_ref, mask_ref, count_ref,
        gain_ref[:, :width], low_ref, result_ref,
    )
    wide_ref[...] = low_ref[...].astype(f32)
    flush(low_ref)
    flush(wide_ref)
    for ref in (grad_sum_ref, summed_ref, pre_ref, stats_ref, squeeze_ref):
        need(ref)
    mean, var = (stats_ref[0:1, :], stats_ref[1:2, :])
    inverse = lax.rsqrt(var + eps_norm)
    sums, prods = ([], [])
    for start, size in spans_of(channels, 512):
        span = pl.ds(start, size)
        cut = slice(start, start + size)
        next_ref[:, span] = dot_nt(low_ref[...], squeeze_ref[start : start + size, :])

        def both(rows):
            mask = wide_mask(mask_ref, rows, size)
            slope = silu_slope(summed_ref[rows, span])
            grad = (next_ref[rows, span] + grad_sum_ref[rows, span]) * mask * slope
            next_ref[rows, span] = grad
            return (grad, grad * ((pre_ref[rows, span] - mean[:, cut]) * inverse[:, cut]))

        total_grad, total_prod = two_sums(pixels, size, both)
        sums.append(total_grad)
        prods.append(total_prod)
    write_copies(copies_ref, sums + prods)


def last_low_body(
    total_ref, grad_ref, first_ref, first_stats_ref, mask_ref, count_ref, gain_ref,
    low_ref, wide_ref, result_ref,
):
    width = first_ref.shape[1]
    low_second(
        total_ref, grad_ref, first_ref, first_stats_ref, mask_ref, count_ref,
        gain_ref[:, :width], low_ref, result_ref,
    )
    wide_ref[...] = low_ref[...].astype(f32)


def last_body(low_ref, grad_sum_ref, squeeze_ref, image_ref, token_ref):
    token_ref[...] = jnp.zeros_like(token_ref)
    for start, size in spans_of(image_ref.shape[1], 256):
        block = dot_nt(low_ref[...], squeeze_ref[start : start + size, :])
        image_ref[:, start : start + size] = (
            block + grad_sum_ref[:, start : start + size]
        ).astype(bf16)


def sum_copies_body(copies_ref, out_ref):
    total = jnp.sum(copies_ref[...], axis=0)

    def one_copy(step, carry):
        out_ref[step] = total
        return carry

    lax.fori_loop(0, out_ref.shape[0], one_copy, 0)


def offsets_body(sums_ref, out_ref):
    outs = out_ref.shape[1]
    for tap in range(out_ref.shape[0]):
        out_ref[tap] = sums_ref[tap * outs : (tap + 1) * outs, :]


block_cols = 256


def split_chunks(scratch_ref, keep_ref, send_ref, own, place, spot):
    for index in range(keep_ref.shape[0]):
        low = index & ((1 << place) - 1)
        base = ((index >> place) << (place + 1)) | low
        keep_ref[index, spot] = scratch_ref[base + own * (1 << place)]
        send_ref[index, spot] = scratch_ref[base + (1 - own) * (1 << place)]


def weights_body(kinds, firsts, spans, own_place_ref, *refs):
    groups = [refs[4 * place : 4 * place + 4] for place in range(len(kinds))]
    rest = refs[4 * len(kinds) :]
    results = 2 * len(spans) if firsts else 1
    outs, token_ref = (rest[:results], rest[results])
    chunks_ref, scratch = (rest[results + 1], list(rest[results + 2 :]))
    token_ref[...] = jnp.zeros_like(token_ref)
    count, depth, _ = chunks_ref.shape
    makers = []
    for kind, (rows_ref, rows_other_ref, cols_ref, cols_other_ref) in zip(kinds, groups):
        for ref in (rows_ref, rows_other_ref, cols_ref, cols_other_ref):
            need(ref)
        pixels, half = cols_other_ref.shape
        side = 1 << ((pixels.bit_length() - 1) // 2)
        both_cols = scratch.pop(0)
        start_own = pl.multiple_of(own_place_ref[0, 0] * half, lane)
        both_cols[pl.ds(0, pixels), :] = cols_ref[:, pl.ds(start_own, half)]
        both_cols[pl.ds(pixels, pixels), :] = cols_other_ref[...].astype(bf16)
        if kind == "rows":
            both_rows = scratch.pop(0)
            both_rows[pl.ds(0, pixels), :] = rows_ref[...]
            both_rows[pl.ds(pixels, pixels), :] = rows_other_ref[...].astype(bf16)
            for start in range(0, half, block_cols):
                makers.append(
                    lambda rows=both_rows, cols=both_cols, start=start: dot_tn(
                        rows[...], cols[:, start : start + block_cols]
                    )
                )
        elif kind == "plain":
            padded, taps = (scratch.pop(0), (scratch.pop(0), scratch.pop(0)))
            for source, shifted in zip((rows_ref, rows_other_ref), taps):
                padded[...] = jnp.zeros_like(padded)
                padded[pl.ds(2 * side, pixels), :] = source[...]
                build_taps(padded, shifted, pixels, side)
            for tap in range(9):
                makers.append(
                    lambda taps=taps, cols=both_cols, tap=tap, pixels=pixels, side=side: dot_tn(
                        tap_of(taps[0], tap, pixels, side), cols[pl.ds(0, pixels), :]
                    )
                    + dot_tn(tap_of(taps[1], tap, pixels, side), cols[pl.ds(pixels, pixels), :])
                )
        else:
            width = cols_ref.shape[1]
            for tap in range(9):
                span = slice(tap * width, (tap + 1) * width)
                makers.append(
                    lambda one=rows_ref, two=rows_other_ref, cols=both_cols, span=span, pixels=pixels: dot_tn(
                        one[:, span], cols[pl.ds(0, pixels), :]
                    )
                    + dot_tn(two[:, span], cols[pl.ds(pixels, pixels), :])
                )
    if not firsts:
        for part, maker in enumerate(makers):
            outs[0][:, part] = maker().reshape(count, depth, block_cols)
        return
    for stream, (start, stop) in enumerate(spans):
        bit = firsts[stream]
        own = own_place_ref[0, bit]
        for part in range(start, stop):
            chunks_ref[...] = makers[part]().reshape(count, depth, block_cols)
            split_chunks(
                chunks_ref, outs[2 * stream], outs[2 * stream + 1], own, bit - 1, part - start
            )
        flush(outs[2 * stream + 1])
        flush(outs[2 * stream])


def advance_body(groups, own_place_ref, *refs):
    streams = sum(count for count, _ in groups)
    kept, came = (refs[:streams], refs[streams : 2 * streams])
    outs = list(refs[2 * streams :])
    token_ref = outs.pop()
    token_ref[...] = jnp.zeros_like(token_ref)
    at, used, start = (0, 0, 0)
    for count, spot in groups:
        members = list(range(at, at + count))
        at += count
        for stream in members:
            need(kept[stream])
            need(came[stream])
        if spot is None:
            for stream in members:
                stop = start + kept[stream].shape[1]
                outs[-1][start:stop] = kept[stream][0] + came[stream][0]
                start = stop
            continue
        bit, place = spot
        own = own_place_ref[0, bit]
        for target_ref, side in ((outs[used + 1], 1 - own), (outs[used], own)):
            first = 0
            for stream in members:
                stop = first + kept[stream].shape[1]
                for index in range(target_ref.shape[0]):
                    low = index & ((1 << place) - 1)
                    base = ((index >> place) << (place + 1)) | low
                    chunk = base + side * (1 << place)
                    target_ref[index, first:stop] = kept[stream][chunk] + came[stream][chunk]
                first = stop
            flush(target_ref)
        used += 2


def assemble_body(kinds, labels, summed, own_place_ref, own_ref, pair_ref, side_ref, both_ref, *targets):
    rows, cols = own_ref.shape[-2:]
    pair, line = (own_place_ref[0, 0], own_place_ref[0, 1])
    for row_at, col_at in ((0, 0), (0, 1), (1, 0), (1, 1)):
        if summed and row_at:
            continue
        same_row, same_col = (line == row_at, pair == col_at)
        row_span = slice(row_at * rows, (row_at + 1) * rows)
        for part, (place, step) in enumerate(labels):
            near = jnp.where(same_col, own_ref[part], pair_ref[part])
            far = jnp.where(same_col, side_ref[part], both_ref[part])
            value = near + far if summed else jnp.where(same_row, near, far)
            target = targets[place]
            if kinds[place] == "rows":
                parts = target.shape[1] // 2 // cols
                at = (col_at * parts + step) * cols
                target[row_span, at : at + cols] = value
            else:
                target[step, row_span, col_at * cols : (col_at + 1) * cols] = value
    for target in targets:
        flush(target)


def gate_body(*refs):
    pass


def gate(arrays, after):
    hbm = pl.BlockSpec(memory_space=pltpu.HBM)
    return pl.pallas_call(
        gate_body,
        out_shape=tuple(shape_of(part.shape) for part in arrays),
        in_specs=[hbm] * len(arrays) + [pl.BlockSpec(memory_space=pl.ANY)] * len(after),
        out_specs=(hbm,) * len(arrays),
        input_output_aliases={place: place for place in range(len(arrays))},
    )(*arrays, *after)


class Comm:
    def __init__(self, wide_size, narrow_size):
        self.total = wide_size * narrow_size
        self.bits = self.total.bit_length() - 1
        self.low = narrow_size.bit_length() - 1
        self.index = lax.axis_index("wide") * narrow_size + lax.axis_index("narrow")
        self.places = jnp.stack([self.bit(place) for place in range(self.bits)])[None, :]

    def bit(self, place):
        return (self.index >> place) & 1

    def swap_over(self, values, flips):
        pairs = [(source, source ^ flips) for source in range(self.total)]
        return lax.ppermute(values, axes, pairs)

    def swap(self, values, place):
        return self.swap_over(values, 1 << place)

    def sync(self, copies):
        return Near(lax.all_to_all(copies, axes, 0, 0, tiled=True))

    def order(self, letters):
        named = {"y": 1, "x": self.low, "a": self.low + 1, "b": self.low + 2}
        return [named[letter] for letter in letters] + list(range(self.low + 3, self.bits))


token = (8, lane)


class Group:
    def __init__(self, comm, total, plan):
        self.comm = comm
        self.orders = [comm.order(letters) for letters, _ in plan]
        self.left = [
            [place for place in range(1, comm.bits) if place != order[0]] for order in self.orders
        ]
        shares = [share for _, share in plan]
        ends = [total * sum(shares[: at + 1]) // sum(shares) for at in range(len(plan))]
        self.bounds = tuple(zip([0] + ends[:-1], ends))
        self.total = total
        self.arrays = {}
        self.labels = []
        self.kinds = ()
        self.shapes = []
        self.at = 1

    def add(self, kind, group, after=()):
        comm = self.comm
        pixels, rows = group[0].shape
        if kind == "given":
            rows = group[2].shape[1]
        chunks = 1 << (comm.bits - 1 if self.orders else comm.bits - comm.low)
        depth = rows // chunks
        half = getattr(group[3], "value", group[3]).shape[1]
        side = 1 << ((pixels.bit_length() - 1) // 2)
        scratch = [pltpu.VMEM((chunks, depth, block_cols), f32), pltpu.VMEM((2 * pixels, half), bf16)]
        wide_depth = rows >> (comm.bits - comm.low)
        self.shapes.append((wide_depth, 2 * half) if kind == "rows" else (9, wide_depth, 2 * half))
        if kind == "rows":
            scratch.append(pltpu.VMEM((2 * pixels, rows), bf16))
        if kind == "plain":
            scratch.append(pltpu.VMEM((pixels + 4 * side, rows), f32))
            scratch += [pltpu.VMEM((3, pixels + 4 * side, rows), bf16)] * 2
        count = half // block_cols if kind == "rows" else 9
        begin = len(self.labels)
        self.labels += [(len(self.kinds), step) for step in range(count)]
        self.kinds += (kind,)
        keys, spans, outs, pieces, begun = ([], [], [], {}, {})
        if not self.orders:
            if self.arrays:
                begun[0] = self.arrays[0, 0]
            pieces[0] = (begin, count)
            outs.append(shape_of((chunks, self.total, depth, block_cols)))
        for stream, (start, stop) in enumerate(self.bounds):
            low, high = (max(start, begin), min(stop, begin + count))
            if low >= high:
                continue
            spans.append((low - begin, high - begin))
            keys.append(stream)
            for which in range(2):
                if (stream, which) in self.arrays:
                    begun[len(outs)] = self.arrays[stream, which]
                pieces[len(outs)] = (low - start, high - low)
                outs.append(shape_of((chunks // 2, stop - start, depth, block_cols)))
        args = (comm.places,) + tuple(group)
        made = call(
            functools.partial(
                weights_body, (kind,), tuple(self.orders[stream][0] for stream in keys), tuple(spans)
            ),
            outs + [shape_of(token)], args, (0,), scratch, after, tuple(range(1, len(args))),
            pieces=pieces, begun=begun,
        )
        if not self.orders:
            self.arrays[0, 0] = made[0]
        for number, stream in enumerate(keys):
            self.arrays[stream, 0] = made[2 * number]
            self.arrays[stream, 1] = made[2 * number + 1]
        return made[-1]

    def offload(self):
        self.share = lax.psum_scatter(self.arrays[0, 0], "wide", scatter_dimension=0, tiled=True)

    def collect(self, after):
        (share,) = gate((self.share.reshape(self.share.shape[1:]),), after)
        self.join(share)

    def join(self, share):
        beside = self.comm.swap(share, 1)
        self.quarters = [share, self.comm.swap(share, 0), beside, self.comm.swap(beside, 0)]

    def start(self, after=()):
        sent = [self.arrays[stream, 1] for stream in range(len(self.orders))]
        sent = gate(sent, after) if after else sent
        self.streams = [
            [(self.arrays[stream, 0], self.comm.swap(sent[stream], order[0]))]
            for stream, order in enumerate(self.orders)
        ]

    def advance(self, after=()):
        comm = self.comm
        if len({tuple(order[self.at :]) for order in self.orders}) == 1:
            self.orders, self.left = (self.orders[:1], self.left[:1])
            self.streams = [sum(self.streams, [])]
        groups, outs = ([], [])
        last = self.at == len(self.orders[0])
        total = 0
        for order, left, members in zip(self.orders, self.left, self.streams):
            spot = None
            parts = sum(kept.shape[1] for kept, _ in members)
            shape = members[0][0].shape
            total += parts
            if not last:
                bit = order[self.at]
                spot = (bit, left.index(bit))
                left.remove(bit)
                outs += [shape_of((shape[0] // 2, parts) + shape[2:])] * 2
            groups.append((len(members), spot))
        if last:
            outs = [shape_of((total,) + shape[2:])]
        flat = [pair for members in self.streams for pair in members]
        *pieces, mark = call(
            functools.partial(advance_body, tuple(groups)),
            outs + [shape_of(token)],
            (comm.places, *(kept for kept, _ in flat), *(Near(came) for _, came in flat)),
            (0,), (), after, tuple(range(1, 1 + 2 * len(flat))),
        )
        if last:
            self.join(pieces[0])
        else:
            self.streams = [
                [(pieces[2 * place], comm.swap(pieces[2 * place + 1], order[self.at]))]
                for place, order in enumerate(self.orders)
            ]
        self.at += 1
        return mark

    def ended(self):
        return self.at > len(self.orders[0])

    def finish(self, after=()):
        while self.orders and not self.ended():
            self.advance(after)
        kinds, shapes = (self.kinds, self.shapes)
        outs = [shape_of(shape) for shape in shapes]
        return call(
            functools.partial(assemble_body, kinds, tuple(self.labels), not self.orders),
            outs, (self.comm.places, self.quarters[0], *(Near(part) for part in self.quarters[1:])), (0,), (), after,
        )


def per_device(
    wide_size, narrow_size, images, image_sizes, offset_shift, squeeze_one, offsets_one, spatial_one,
    expand_one, squeeze_two, spatial_two, expand_two, norm_gain_one, norm_bias_one, norm_gain_two,
    norm_bias_two, run_mean_one, run_var_one, run_mean_two, run_var_two, grad_output,
):
    comm = Comm(wide_size, narrow_size)
    side, channels = (images.shape[1], images.shape[3])
    pixels = side * side
    width = squeeze_one.shape[1]
    outs = offsets_one.shape[2]
    total = comm.total
    small = (total, 2 * width // lane, lane)
    large = (total, 2 * channels // lane, lane)
    flat = images.reshape(pixels, channels)
    grad_out = grad_output.reshape(pixels, channels)
    gain_one, bias_one = (norm_gain_one[None, :], norm_bias_one[None, :])
    gain_two, bias_two = (norm_gain_two[None, :], norm_bias_two[None, :])
    field = shape_of((pixels, width))
    field_low = shape_of((pixels, width), bf16)
    plane = shape_of((pixels, channels))
    plane_low = shape_of((pixels, channels), bf16)
    half_plane = shape_of((pixels, channels // 2))
    half_field = shape_of((pixels, width // 2))
    stats_small, stats_large = (shape_of((2, width)), shape_of((2, channels)))
    padded = pltpu.VMEM((pixels + 4 * side, width), f32)
    shifted = pltpu.VMEM((3, pixels + 4 * side, width), bf16)
    tap_sums = pltpu.VMEM((3, pixels + 4 * side, width), f32)

    first_one, mask, copies, images_half = call(
        first_body,
        (field, shape_of((pixels, lane)), shape_of((total, 2 * width // lane + 8, lane)), half_plane),
        (image_sizes, comm.places, flat, squeeze_one),
        (0, 1),
    )
    images_half = comm.swap(images_half, 0)
    copies = comm.sync(copies)
    (act_one, act_wide, columns, offsets, second_one, copies, first_stats_one, count) = call(
        deform_body,
        (
            field_low, field, shape_of((pixels, 9 * width), bf16),
            shape_of((pixels, outs)), field, shape_of(small), stats_small, shape_of((8, lane)),
        ),
        (
            copies, first_one, mask, gain_one, bias_one, offsets_one,
            offset_shift.astype(f32)[None, :], spatial_one,
        ),
        (),
        (padded, shifted),
        (),
        (5, 7),
    )
    act_other, offsets_other = (comm.swap(act_wide, 0), comm.swap(offsets, 0))
    copies = comm.sync(copies)
    act_second_one, act_second_wide_one, third_one, copies, second_stats_one = call(
        third_body,
        (field_low, field, plane, shape_of(large), stats_small),
        (copies, second_one, mask, count, gain_one, bias_one, expand_one), late=(6,),
    )
    (columns_other,) = call(
        columns_body, (shape_of((pixels, 9 * width), bf16),),
        (Near(act_other), Near(offsets_other)), (), (pltpu.VMEM((pixels, width), bf16),), (second_stats_one,),
    )
    act_second_wide_one = comm.swap(act_second_wide_one, 0)
    copies = comm.sync(copies)
    summed_one, low_two, low_half, first_two, copies, third_stats_one = call(
        between_body,
        (plane, plane_low, half_plane, field, shape_of(small), stats_large),
        (copies, third_one, flat, mask, count, comm.places, gain_one, bias_one, squeeze_two),
        (5,), (), (columns_other,), (8,),
    )
    low_half = comm.swap(low_half, 0)
    copies = comm.sync(copies)
    act_wide_two, second_two, copies, first_stats_two = call(
        plain_body,
        (field, field, shape_of(small), stats_small),
        (copies, first_two, mask, count, gain_two, bias_two, spatial_two),
        (),
        (padded, shifted), late=(6,),
    )
    act_wide_two_other = comm.swap(act_wide_two, 0)
    copies = comm.sync(copies)
    act_second_two, act_second_wide_two, third_two, copies, second_stats_two = call(
        third_body,
        (field_low, field, plane, shape_of(large), stats_small),
        (copies, second_two, mask, count, gain_two, bias_two, expand_two), late=(6,),
    )
    act_second_wide_two = comm.swap(act_second_wide_two, 0)
    copies = comm.sync(copies)
    output_images, grad_sum_two, copies, third_stats_two = call(
        turn_body,
        (plane_low, plane, shape_of(large), stats_large),
        (copies, third_two, summed_one, grad_out, mask, count, gain_two, bias_two),
    )
    copies = comm.sync(copies)
    low_third_two, third_half, grad_second_two, copies, third_result_two = call(
        back_third_body,
        (plane_low, half_plane, field, shape_of(small), stats_large),
        (
            copies, grad_sum_two, third_two, third_stats_two, second_two, second_stats_two, mask, count,
            comm.places, gain_two, bias_two, expand_two,
        ),
        (8,), late=(4, 5, 11),
    )
    third_half = comm.swap(third_half, 0)
    copies = comm.sync(copies)
    blocks = channels // 2 // block_cols
    plan = (("xyab", 6), ("yaxb", 6), ("axyb", 5))
    group_two = Group(comm, 2 * blocks + 9, plan)
    group_one = Group(comm, 2 * blocks + 9, plan)
    done = group_two.add("rows", (act_second_two, act_second_wide_two, low_third_two, Near(third_half)))
    low_second_two, second_half, grad_first_two, copies, second_result_two = call(
        back_plain_body,
        (field_low, half_field, field, shape_of(small), stats_small),
        (
            copies, grad_second_two, second_two, second_stats_two, first_two, first_stats_two, mask,
            count, comm.places, gain_two, bias_two, spatial_two,
        ),
        (8,),
        (tap_sums,),
        (done,),
        (11,),
    )
    second_half = comm.swap(second_half, 0)
    copies = comm.sync(copies)
    done = group_two.add("plain", (act_wide_two, act_wide_two_other, low_second_two, Near(second_half)))
    low_first_two, low_first_wide, grad_sum_one, copies, first_result_two = call(
        back_between_body,
        (field_low, field, plane, shape_of(large), stats_small),
        (
            copies, grad_first_two, first_two, first_stats_two, grad_sum_two, summed_one, third_one,
            third_stats_one, mask, count, gain_two, squeeze_two,
        ),
        (),
        (),
        (done,),
        (4, 5, 6, 7, 11),
    )
    low_first_wide = comm.swap(low_first_wide, 0)
    copies = comm.sync(copies)
    done = group_two.add("rows", (low_first_two, Near(low_first_wide), low_two, low_half))
    group_two.start((copies.value, done))
    low_third_one, third_half, grad_second_one, copies, third_result_one = call(
        back_third_body,
        (plane_low, half_plane, field, shape_of(small), stats_large),
        (
            copies, grad_sum_one, third_one, third_stats_one, second_one, second_stats_one, mask, count,
            comm.places, gain_one, bias_one, expand_one,
        ),
        (8,),
        (),
        (done,),
        (4, 5, 11),
    )
    third_half = comm.swap(third_half, 0)
    copies = comm.sync(copies)
    done = group_one.add("rows", (act_second_one, act_second_wide_one, low_third_one, Near(third_half)))
    done = group_two.advance((copies.value, done))
    slots = -(-9 * outs // total)
    slots = -(-slots // 8) * 8
    low_second_one, second_half, grad_first_one, copies, second_result_one, grad_offsets = call(
        back_deform_body,
        (
            field_low, half_field, field, shape_of(small), stats_small, shape_of((total * slots, width)),
        ),
        (
            copies, grad_second_one, second_one, second_stats_one, first_one, first_stats_one, mask,
            count, comm.places, gain_one, bias_one, spatial_one, act_one, offsets, offsets_one,
        ),
        (8,),
        (tap_sums, padded, shifted),
        (done,),
        (4, 5, 11, 12, 13, 14),
    )
    second_half = comm.swap(second_half, 0)
    copies = comm.sync(copies)
    done = group_one.add("given", (columns, columns_other, low_second_one, Near(second_half)))
    low_first_one, low_first_wide, first_result_one = call(
        last_low_body,
        (field_low, field, stats_small),
        (copies, grad_first_one, first_one, first_stats_one, mask, count, gain_one),
    )
    low_first_wide = comm.swap(low_first_wide, 0)
    done = group_two.advance((first_result_one, done))
    grad_offsets = comm.sync(grad_offsets.reshape(total, slots, width))
    grad_images, done = call(
        last_body,
        (plane_low, shape_of(token)),
        (low_first_one, grad_sum_one, squeeze_one),
        (), (), (done,),
    )
    done = group_one.add("rows", (low_first_one, Near(low_first_wide), flat, images_half), (done,))
    done = group_two.advance((done, grad_offsets.value))
    group_one.start((done,))
    (grad_offsets,) = call(
        sum_copies_body, (shape_of((total, slots, width)),), (grad_offsets,), (), (),
        (done,),
    )
    grad_offsets = comm.sync(grad_offsets).value
    done = group_two.advance((done,))
    done = group_one.advance((done,))
    (grad_offsets,) = call(
        offsets_body, (shape_of((9, outs, width)),), (grad_offsets.reshape(total * slots, width),), (), (),
        (done,),
    )
    done = group_one.advance((grad_offsets,))
    done = group_one.advance((done,))
    grad_expand_two, grad_spatial_two, grad_squeeze_two = group_two.finish((done,))
    grad_expand_one, grad_spatial_one, grad_squeeze_one = group_one.finish((grad_squeeze_two,))

    def laid(parts, row):
        return jnp.concatenate([part[row] for part in parts])

    results_one = (first_result_one, second_result_one, third_result_one)
    results_two = (first_result_two, second_result_two, third_result_two)
    stats_one = (first_stats_one, second_stats_one, third_stats_one)
    stats_two = (first_stats_two, second_stats_two, third_stats_two)
    pixel_count = count[0, 0]
    unbias = pixel_count / (pixel_count - 1.0)
    fresh = 1.0 - keep_rate
    return (
        output_images.reshape(images.shape),
        grad_images.reshape(images.shape),
        grad_squeeze_one.T,
        grad_offsets.transpose(0, 2, 1),
        grad_spatial_one,
        grad_expand_one,
        grad_squeeze_two.T,
        grad_spatial_two,
        grad_expand_two,
        laid(results_one, 1),
        laid(results_one, 0),
        laid(results_two, 1),
        laid(results_two, 0),
        keep_rate * run_mean_one + fresh * laid(stats_one, 0),
        keep_rate * run_var_one + fresh * laid(stats_one, 1) * unbias,
        keep_rate * run_mean_two + fresh * laid(stats_two, 0),
        keep_rate * run_var_two + fresh * laid(stats_two, 1) * unbias,
    )


def solution(mesh):
    images_spec = P(axes, None, None, None)
    whole = P()
    return jax.shard_map(
        functools.partial(per_device, mesh.shape["wide"], mesh.shape["narrow"]),
        mesh=mesh,
        in_specs=(images_spec, P(axes, None)) + (whole,) * 16 + (images_spec,),
        out_specs=(
            images_spec,
            images_spec,
            P(None, "wide"),
            whole,
            P(None, "wide", None),
            P("wide", None),
            P(None, "wide"),
            P(None, "wide", None),
            P("wide", None),
        )
        + (whole,) * 8,
        check_vma=False,
    )
```

```python
import functools

import jax
import jax.numpy as jnp
from jax import lax
from jax.experimental import pallas as pl
from jax.experimental.pallas import tpu as pltpu
from jax.sharding import PartitionSpec as P

eps_norm = 1e-05
keep_rate = 0.6
vmem_bytes = 52 * 1024 * 1024
lane = 128
tile_rows = 16
row_unroll = 2
axes = ("wide", "narrow")
f32 = jnp.float32
bf16 = jnp.bfloat16


def shape_of(shape, kind=f32):
    return jax.ShapeDtypeStruct(shape, kind)


copies_of = {}


def need(ref, part=None):
    entries = copies_of.get(id(ref), [])
    for entry in entries if part is None else entries[part : part + 1]:
        if entry[1]:
            entry[1] = False
            entry[0].wait()
    return ref


def flush(ref, part=None):
    entries = copies_of.get(id(ref), [])
    for entry in entries if part is None else entries[part : part + 1]:
        if entry[1]:
            entry[1] = False
            entry[0].start()


def column_copies(source, target, flags, first, count):
    if count == 1:
        return [[pltpu.make_async_copy(source, target, flags.at[first]), True]]
    width = source.shape[1] // count
    spans = [pl.ds(width * at, width) for at in range(count)]
    return [
        [pltpu.make_async_copy(source.at[:, span], target.at[:, span], flags.at[first + at]), True]
        for at, span in enumerate(spans)
    ]


class Near:
    def __init__(self, value):
        self.value = value


def call(body, outs, args, smem=(), scratch=(), after=(), late=(), stay_out=(), pieces=None, begun=None, blocks=None, blocks_out=None):
    stay = tuple(place for place, arg in enumerate(args) if isinstance(arg, Near))
    args = tuple(arg.value if isinstance(arg, Near) else arg for arg in args)
    pieces = pieces or {}
    begun = begun or {}
    blocks = blocks or {}
    blocks_out = blocks_out or {}
    hbm = pl.BlockSpec(memory_space=pltpu.HBM)
    vmem = pl.BlockSpec(memory_space=pltpu.VMEM)
    specs = [
        pl.BlockSpec(memory_space=pltpu.SMEM) if place in smem else vmem if place in stay else hbm
        for place in range(len(args))
    ] + [pl.BlockSpec(memory_space=pl.ANY)] * len(after) + [hbm] * len(begun)
    moved = [place for place in range(len(args)) if place not in smem and place not in stay]
    used, extra, made = (len(args), len(after) + len(begun), len(outs))
    sent = [slot for slot in range(made) if slot not in stay_out]

    def kernel(*refs):
        given = list(refs[:used])
        results = list(refs[used + extra : used + extra + made])
        rest = refs[used + extra + made :]
        in_slots, out_slots = (rest[: len(moved)], rest[len(moved) : len(moved) + len(sent)])
        in_flags, out_flags = rest[len(moved) + len(sent) : len(moved) + len(sent) + 2]
        copies_of.clear()
        first = 0
        for slot, place in enumerate(moved):
            count = blocks.get(place, 1)
            entries = column_copies(given[place], in_slots[slot], in_flags, first, count)
            first += count
            for entry in entries:
                entry[0].start()
            copies_of[id(in_slots[slot])] = entries
            given[place] = in_slots[slot]
        for place in moved:
            if place not in late and place not in blocks:
                need(given[place])
        first = 0
        for slot, place in enumerate(sent):
            count = blocks_out.get(place, 1)
            target = results[place].at[:, pl.ds(*pieces[place])] if place in pieces else results[place]
            copies_of[id(out_slots[slot])] = column_copies(out_slots[slot], target, out_flags, first, count)
            first += count
            results[place] = out_slots[slot]
        body(*given, *results, *rest[len(moved) + len(sent) + 2 :])
        for place in moved:
            need(given[place])
        for slot in out_slots:
            flush(slot)
        for slot in out_slots:
            for entry in copies_of[id(slot)]:
                entry[0].wait()
        copies_of.clear()

    slots = [pltpu.VMEM(args[place].shape, args[place].dtype) for place in moved]
    for place in sent:
        shape = outs[place].shape
        if place in pieces:
            shape = (shape[0], pieces[place][1]) + shape[2:]
        slots.append(pltpu.VMEM(shape, outs[place].dtype))
    in_count = sum(blocks.get(place, 1) for place in moved)
    out_count = sum(blocks_out.get(place, 1) for place in sent)
    flags = [pltpu.SemaphoreType.DMA((max(in_count, 1),)), pltpu.SemaphoreType.DMA((max(out_count, 1),))]
    return pl.pallas_call(
        kernel,
        input_output_aliases={used + len(after) + at: place for at, place in enumerate(begun)},
        out_shape=tuple(outs),
        in_specs=specs,
        out_specs=tuple(vmem if place in stay_out else hbm for place in range(made)),
        scratch_shapes=slots + flags + list(scratch),
        compiler_params=pltpu.CompilerParams(vmem_limit_bytes=vmem_bytes),
    )(*args, *after, *begun.values())


def dot_nn(first_op, second_op):
    return lax.dot_general(
        first_op, second_op, (((1,), (0,)), ((), ())), preferred_element_type=f32
    )


def dot_nt(first_op, second_op):
    return lax.dot_general(
        first_op, second_op, (((1,), (1,)), ((), ())), preferred_element_type=f32
    )


def dot_tn(first_op, second_op):
    return lax.dot_general(
        first_op, second_op, (((0,), (0,)), ((), ())), preferred_element_type=f32
    )


def logistic(values):
    return 0.5 * jnp.tanh(0.5 * values) + 0.5


def silu(values):
    return values * logistic(values)


def silu_slope(values):
    gate = logistic(values)
    return gate * (1.0 + values * (1.0 - gate))


def flat_row(rows, start, width):
    first = start // lane
    return jnp.concatenate(
        [rows[first + step : first + step + 1, :] for step in range(width // lane)], axis=1
    )


def fold_row(row):
    return [row[:, step * lane : (step + 1) * lane] for step in range(row.shape[1] // lane)]


def write_copies(copies_ref, rows, extra=None):
    packed = jnp.concatenate([piece for row in rows for piece in fold_row(row)], axis=0)
    if extra is not None:
        packed = jnp.concatenate([packed, extra], axis=0)

    def one_copy(step, carry):
        copies_ref[step] = packed
        return carry

    lax.fori_loop(0, copies_ref.shape[0], one_copy, 0)


def read_copies(copies_ref):
    return jnp.sum(copies_ref[...], axis=0)


def wide_mask(mask_ref, rows, width):
    return jnp.concatenate([mask_ref[rows, :]] * (width // lane), axis=1)


def eight_rows(values):
    folded = values[:8]
    for start in range(8, values.shape[0], 8):
        folded = folded + values[start : start + 8]
    return folded


def row_loop(pixels, body, carry):
    def step(index, state):
        return body(pl.ds(pl.multiple_of(index * tile_rows, tile_rows), tile_rows), state)

    return lax.fori_loop(0, pixels // tile_rows, step, carry, unroll=row_unroll)


def two_sums(pixels, width, body):
    zero = jnp.zeros((8, width), f32)

    def step(rows, state):
        first, second = body(rows)
        return (state[0] + eight_rows(first), state[1] + eight_rows(second))

    first, second = row_loop(pixels, step, (zero, zero))
    return (jnp.sum(first, axis=0, keepdims=True), jnp.sum(second, axis=0, keepdims=True))


def moments(total, width, count):
    mean = flat_row(total, 0, width) / count
    var = flat_row(total, width, width) / count - mean * mean
    return (mean, var)


def scale_shift(mean, var, gain, bias):
    inverse = lax.rsqrt(var + eps_norm)
    scale = gain * inverse
    return (scale, bias - mean * scale)


def spans_of(width, block):
    return [(start, min(block, width - start)) for start in range(0, width, block)]


def grad_rows(total, stats, gain, count, width):
    mean, var = (stats[0:1], stats[1:2])
    inverse = lax.rsqrt(var + eps_norm)
    sum_grad = flat_row(total, 0, width)
    sum_prod = flat_row(total, width, width)
    return (
        gain * inverse,
        sum_grad / count,
        inverse * sum_prod / count,
        mean,
        sum_grad,
        sum_prod,
    )


def build_taps(act_ref, shifted_ref, pixels, side):
    pad = 2 * side
    width = act_ref.shape[1]
    column = lax.broadcasted_iota(jnp.int32, (pixels, lane), 0) % side
    for tap_col in range(3):
        move = 2 * (tap_col - 1)
        moved = act_ref[pl.ds(pad + move, pixels), :]
        if move:
            inside = (column + move >= 0) & (column + move < side)
            keep = jnp.concatenate([inside.astype(f32)] * (width // lane), axis=1)
            moved = moved * keep
        shifted_ref[tap_col, pl.ds(0, pad), :] = jnp.zeros((pad, width), bf16)
        shifted_ref[tap_col, pl.ds(pad + pixels, pad), :] = jnp.zeros((pad, width), bf16)
        shifted_ref[tap_col, pl.ds(pad, pixels), :] = moved.astype(bf16)


def tap_of(shifted_ref, tap_index, pixels, side):
    tap_row, tap_col = (tap_index // 3, tap_index % 3)
    return shifted_ref[tap_col, pl.ds(2 * side * tap_row, pixels), :]


def fold_columns(sums_ref, pixels, side):
    pad = 2 * side
    width = sums_ref.shape[2]
    column = lax.broadcasted_iota(jnp.int32, (pixels, lane), 0) % side
    total = sums_ref[1, pl.ds(pad, pixels), :]
    for tap_col in (0, 2):
        move = 2 * (tap_col - 1)
        inside = (column - move >= 0) & (column - move < side)
        keep = jnp.concatenate([inside.astype(f32)] * (width // lane), axis=1)
        total = total + keep * sums_ref[tap_col, pl.ds(pad - move, pixels), :]
    return total


def tap_rows_out(sums_ref, tap_index, pixels, side, values):
    tap_row, tap_col = (tap_index // 3, tap_index % 3)
    rows = pl.ds(2 * side * tap_row, pixels)
    sums_ref[tap_col, rows, :] = sums_ref[tap_col, rows, :] + values


def tap_factors(offsets, tap_index, side):
    pixels = offsets.shape[0]
    tap_row, tap_col = (tap_index // 3, tap_index % 3)
    shape = (pixels, pixels)
    position = lax.broadcasted_iota(jnp.int32, (pixels, 1), 0)
    source = lax.broadcasted_iota(jnp.int32, (1, pixels), 1)
    row_at = (position // side + 2 * (tap_row - 1)).astype(f32) + offsets[:, 2 * tap_index : 2 * tap_index + 1]
    col_at = (position % side + 2 * (tap_col - 1)).astype(f32) + offsets[:, 2 * tap_index + 1 : 2 * tap_index + 2]
    dist_y = jnp.broadcast_to(row_at, shape) - (source // side).astype(f32)
    dist_x = jnp.broadcast_to(col_at, shape) - (source % side).astype(f32)
    bump_y = jnp.maximum(1.0 - dist_y * dist_y, 0.0)
    bump_x = jnp.maximum(1.0 - dist_x * dist_x, 0.0)
    return (dist_y, dist_x, bump_y, bump_x)


def first_body(sizes_ref, place_ref, images_ref, squeeze_ref, pre_ref, mask_ref, copies_ref, half_ref):
    pixels, width = pre_ref.shape
    side = 1 << ((pixels.bit_length() - 1) // 2)
    position = lax.broadcasted_iota(jnp.int32, (pixels, lane), 0)
    inside = (position // side < sizes_ref[0, 0]) & (position % side < sizes_ref[0, 1])
    mask = inside.astype(f32)
    mask_ref[...] = mask
    pre_ref[...] = dot_nn(images_ref[...], squeeze_ref[...])
    flush(pre_ref)

    def both(rows):
        values = pre_ref[rows, :]
        masked = values * wide_mask(mask_ref, rows, width)
        return (masked, masked * values)

    sums = two_sums(pixels, width, both)
    amount = jnp.sum(mask, axis=0, keepdims=True)
    write_copies(copies_ref, sums, jnp.broadcast_to(amount, (8, lane)))
    half = half_ref.shape[1]
    other = pl.multiple_of((1 - place_ref[0, 0]) * half, lane)
    half_ref[...] = images_ref[:, pl.ds(other, half)].astype(f32)


def activate(pre_ref, mask_ref, scale, shift, out_ref, base=0):
    pixels, width = pre_ref.shape

    def step(rows, carry):
        out = silu(pre_ref[rows, :] * scale + shift) * wide_mask(mask_ref, rows, width)
        target = pl.ds(rows.start + base, tile_rows)
        out_ref[target, :] = out.astype(bf16).astype(out_ref.dtype)
        return carry

    row_loop(pixels, step, 0)


def masked_sums(values_ref, mask_ref):
    pixels, width = values_ref.shape

    def both(rows):
        values = values_ref[rows, :]
        masked = values * wide_mask(mask_ref, rows, width)
        return (masked, masked * values)

    return two_sums(pixels, width, both)


def deform_body(
    total_ref, pre_ref, mask_ref, gain_ref, bias_ref, weights_ref, move_ref, spatial_ref,
    act_ref, wide_ref, columns_ref, offsets_ref, second_ref, copies_ref, stats_ref,
    count_ref, padded_ref, shifted_ref,
):
    pixels, width = pre_ref.shape
    side = 1 << ((pixels.bit_length() - 1) // 2)
    total = read_copies(total_ref)
    count = total[2 * width // lane : 2 * width // lane + 1, 0:1]
    count_ref[...] = jnp.broadcast_to(count, (8, lane))
    mean, var = moments(total, width, count)
    stats_ref[...] = jnp.concatenate([mean, var], axis=0)
    scale, shift = scale_shift(mean, var, gain_ref[:, :width], bias_ref[:, :width])
    padded_ref[...] = jnp.zeros_like(padded_ref)
    activate(pre_ref, mask_ref, scale, shift, padded_ref, 2 * side)
    wide_ref[...] = padded_ref[pl.ds(2 * side, pixels), :]
    flush(wide_ref)
    act_ref[...] = wide_ref[...].astype(bf16)
    build_taps(padded_ref, shifted_ref, pixels, side)
    flush(act_ref)
    offsets = move_ref[...]
    need(weights_ref)
    for tap_index in range(9):
        taps = tap_of(shifted_ref, tap_index, pixels, side)
        offsets = offsets + dot_nn(taps, weights_ref[tap_index])
    offsets_ref[...] = offsets
    flush(offsets_ref)
    need(spatial_ref)
    second_ref[...] = jnp.zeros_like(second_ref)
    for tap_index in range(9):
        dist_y, dist_x, bump_y, bump_x = tap_factors(offsets, tap_index, side)
        root = bump_y * bump_x
        columns = dot_nn((root * root).astype(bf16), act_ref[...]).astype(bf16)
        span = pl.ds(tap_index * width, width)
        columns_ref[:, span] = columns
        flush(columns_ref, tap_index)
        second_ref[...] = second_ref[...] + dot_nn(columns, spatial_ref[tap_index])
    flush(second_ref)
    write_copies(copies_ref, masked_sums(second_ref, mask_ref))


def columns_body(act_ref, offsets_ref, columns_ref, low_ref):
    pixels, width = act_ref.shape
    side = 1 << ((pixels.bit_length() - 1) // 2)
    low_ref[...] = act_ref[...].astype(bf16)
    offsets = offsets_ref[...]
    for tap_index in range(9):
        _, _, bump_y, bump_x = tap_factors(offsets, tap_index, side)
        root = bump_y * bump_x
        span = pl.ds(tap_index * width, width)
        columns_ref[:, span] = dot_nn((root * root).astype(bf16), low_ref[...]).astype(bf16)


def plain_body(
    total_ref, pre_ref, mask_ref, count_ref, gain_ref, bias_ref, spatial_ref,
    wide_ref, second_ref, copies_ref, stats_ref,
    padded_ref, shifted_ref,
):
    pixels, width = pre_ref.shape
    side = 1 << ((pixels.bit_length() - 1) // 2)
    total = read_copies(total_ref)
    mean, var = moments(total, width, count_ref[0:1, 0:1])
    stats_ref[...] = jnp.concatenate([mean, var], axis=0)
    scale, shift = scale_shift(mean, var, gain_ref[:, :width], bias_ref[:, :width])
    padded_ref[...] = jnp.zeros_like(padded_ref)
    activate(pre_ref, mask_ref, scale, shift, padded_ref, 2 * side)
    wide_ref[...] = padded_ref[pl.ds(2 * side, pixels), :]
    flush(wide_ref)
    build_taps(padded_ref, shifted_ref, pixels, side)
    need(spatial_ref)
    second_ref[...] = jnp.zeros_like(second_ref)
    for tap_index in range(9):
        taps = tap_of(shifted_ref, tap_index, pixels, side)
        second_ref[...] = second_ref[...] + dot_nn(taps, spatial_ref[tap_index])
    flush(second_ref)
    write_copies(copies_ref, masked_sums(second_ref, mask_ref))


def third_body(
    total_ref, pre_ref, mask_ref, count_ref, gain_ref, bias_ref, expand_ref,
    act_ref, wide_ref, third_ref, copies_ref, stats_ref,
):
    pixels, width = pre_ref.shape
    channels = third_ref.shape[1]
    total = read_copies(total_ref)
    mean, var = moments(total, width, count_ref[0:1, 0:1])
    stats_ref[...] = jnp.concatenate([mean, var], axis=0)
    scale, shift = scale_shift(
        mean, var, gain_ref[:, width : 2 * width], bias_ref[:, width : 2 * width]
    )
    activate(pre_ref, mask_ref, scale, shift, act_ref)
    wide_ref[...] = act_ref[...].astype(f32)
    flush(act_ref)
    flush(wide_ref)
    sums, squares = ([], [])
    for part, (start, size) in enumerate(spans_of(channels, 512)):
        need(expand_ref, part)
        block = dot_nn(act_ref[...], expand_ref[:, start : start + size])
        third_ref[:, start : start + size] = block
        flush(third_ref, part)
        sums.append(jnp.sum(block, axis=0, keepdims=True))
        squares.append(jnp.sum(block * block, axis=0, keepdims=True))
    flush(third_ref)
    write_copies(copies_ref, sums + squares)


def between_body(
    total_ref, pre_ref, images_ref, mask_ref, count_ref, place_ref, gain_ref, bias_ref, squeeze_ref,
    summed_ref, low_ref, half_ref, first_ref, copies_ref, stats_ref,
):
    pixels, channels = pre_ref.shape
    total = read_copies(total_ref)
    mean, var = moments(total, channels, count_ref[0:1, 0:1])
    stats_ref[...] = jnp.concatenate([mean, var], axis=0)
    begin = gain_ref.shape[1] - channels
    scale, shift = scale_shift(mean, var, gain_ref[:, begin:], bias_ref[:, begin:])
    for part, (start, size) in enumerate(spans_of(channels, 512)):
        span = pl.ds(start, size)
        need(pre_ref, part)
        need(images_ref, part)

        def step(rows, carry):
            summed = (
                pre_ref[rows, span] * scale[:, start : start + size]
                + shift[:, start : start + size]
                + images_ref[rows, span].astype(f32)
            )
            summed_ref[rows, span] = summed
            low_ref[rows, span] = (silu(summed) * wide_mask(mask_ref, rows, size)).astype(bf16)
            return carry

        row_loop(pixels, step, 0)
        flush(summed_ref, part)
        flush(low_ref, part)
    flush(summed_ref)
    flush(low_ref)
    need(squeeze_ref)
    sums, squares = ([], [])
    for start, size in spans_of(first_ref.shape[1], 256):
        block = dot_nn(low_ref[...], squeeze_ref[:, start : start + size])
        first_ref[:, start : start + size] = block
        sums.append(jnp.sum(block, axis=0, keepdims=True))
        squares.append(jnp.sum(block * block, axis=0, keepdims=True))
    flush(first_ref)
    write_copies(copies_ref, sums + squares)
    half = half_ref.shape[1]
    other = pl.multiple_of((1 - place_ref[0, 0]) * half, lane)
    half_ref[...] = low_ref[:, pl.ds(other, half)].astype(f32)


def turn_body(
    total_ref, pre_ref, before_ref, grad_ref, mask_ref, count_ref, gain_ref, bias_ref,
    image_ref, grad_sum_ref, copies_ref, stats_ref,
):
    pixels, channels = pre_ref.shape
    total = read_copies(total_ref)
    mean, var = moments(total, channels, count_ref[0:1, 0:1])
    stats_ref[...] = jnp.concatenate([mean, var], axis=0)
    begin = gain_ref.shape[1] - channels
    scale, shift = scale_shift(mean, var, gain_ref[:, begin:], bias_ref[:, begin:])
    inverse = lax.rsqrt(var + eps_norm)
    sums, prods = ([], [])
    for part, (start, size) in enumerate(spans_of(channels, 512)):
        span = pl.ds(start, size)
        cut = slice(start, start + size)
        for ref in (pre_ref, before_ref, grad_ref):
            need(ref, part)

        def both(rows):
            mask = wide_mask(mask_ref, rows, size)
            pre = pre_ref[rows, span]
            summed = pre * scale[:, cut] + shift[:, cut] + silu(before_ref[rows, span]) * mask
            gate = logistic(summed)
            image_ref[rows, span] = (summed * gate * mask).astype(bf16)
            slope = gate * (1.0 + summed * (1.0 - gate))
            grad = grad_ref[rows, span].astype(f32) * mask * slope
            grad_sum_ref[rows, span] = grad
            return (grad, grad * ((pre - mean[:, cut]) * inverse[:, cut]))

        total_grad, total_prod = two_sums(pixels, size, both)
        sums.append(total_grad)
        prods.append(total_prod)
        flush(image_ref, part)
        flush(grad_sum_ref, part)
    write_copies(copies_ref, sums + prods)


def low_gradient(rows, width, start, grad, pre, mask, coefs):
    cut = slice(start, start + width)
    scale, mean_grad, mean_prod, mean = (part[:, cut] for part in coefs[:4])
    return scale * (grad - mask * (mean_grad + (pre - mean) * mean_prod))


def back_third_body(
    total_ref, grad_sum_ref, pre_ref, stats_ref, second_ref, second_stats_ref, mask_ref, count_ref,
    place_ref, gain_ref, bias_ref, expand_ref,
    low_ref, half_ref, grad_ref, copies_ref, result_ref,
):
    pixels, channels = pre_ref.shape
    width = second_ref.shape[1]
    total = read_copies(total_ref)
    coefs = grad_rows(
        total, stats_ref[...], gain_ref[:, 2 * width :], count_ref[0:1, 0:1], channels
    )
    result_ref[...] = jnp.concatenate(coefs[4:6], axis=0)
    for part, (start, size) in enumerate(spans_of(channels, 512)):
        span = pl.ds(start, size)
        need(grad_sum_ref, part)
        need(pre_ref, part)

        def step(rows, carry):
            mask = wide_mask(mask_ref, rows, size)
            low_ref[rows, span] = low_gradient(
                rows, size, start, grad_sum_ref[rows, span], pre_ref[rows, span], mask, coefs
            ).astype(bf16)
            return carry

        row_loop(pixels, step, 0)
        flush(low_ref, part)
    half = half_ref.shape[1]
    other = pl.multiple_of((1 - place_ref[0, 0]) * half, lane)
    half_ref[...] = low_ref[:, pl.ds(other, half)].astype(f32)
    flush(low_ref)
    flush(half_ref)
    for ref in (expand_ref, second_ref, second_stats_ref):
        need(ref)
    for start, size in spans_of(width, 256):
        grad_ref[:, start : start + size] = dot_nt(low_ref[...], expand_ref[start : start + size, :])
    norm_two_slope(grad_ref, second_ref, second_stats_ref, mask_ref, gain_ref, bias_ref, width, copies_ref)


def norm_two_slope(grad_ref, pre_ref, stats_ref, mask_ref, gain_ref, bias_ref, begin, copies_ref):
    pixels, width = pre_ref.shape
    mean, var = (stats_ref[0:1, :], stats_ref[1:2, :])
    inverse = lax.rsqrt(var + eps_norm)
    scale, shift = scale_shift(
        mean, var, gain_ref[:, begin : begin + width], bias_ref[:, begin : begin + width]
    )

    def both(rows):
        pre = pre_ref[rows, :]
        slope = silu_slope(pre * scale + shift)
        grad = grad_ref[rows, :] * slope * wide_mask(mask_ref, rows, width)
        grad_ref[rows, :] = grad
        return (grad, grad * ((pre - mean) * inverse))

    write_copies(copies_ref, two_sums(pixels, width, both))


def low_second(total_ref, grad_ref, pre_ref, stats_ref, mask_ref, count_ref, gain, low_ref, result_ref):
    pixels, width = pre_ref.shape
    total = read_copies(total_ref)
    coefs = grad_rows(total, stats_ref[...], gain, count_ref[0:1, 0:1], width)
    result_ref[...] = jnp.concatenate(coefs[4:6], axis=0)

    def step(rows, carry):
        mask = wide_mask(mask_ref, rows, width)
        low_ref[rows, :] = low_gradient(
            rows, width, 0, grad_ref[rows, :], pre_ref[rows, :], mask, coefs
        ).astype(bf16)
        return carry

    row_loop(pixels, step, 0)


def back_plain_body(
    total_ref, grad_in_ref, second_ref, second_stats_ref, first_ref, first_stats_ref, mask_ref,
    count_ref, place_ref, gain_ref, bias_ref, spatial_ref,
    low_ref, half_ref, grad_ref, copies_ref, result_ref,
    sums_ref,
):
    pixels, width = second_ref.shape
    side = 1 << ((pixels.bit_length() - 1) // 2)
    low_second(
        total_ref, grad_in_ref, second_ref, second_stats_ref, mask_ref, count_ref,
        gain_ref[:, width : 2 * width], low_ref, result_ref,
    )
    half = half_ref.shape[1]
    other = pl.multiple_of((1 - place_ref[0, 0]) * half, lane)
    half_ref[...] = low_ref[:, pl.ds(other, half)].astype(f32)
    flush(low_ref)
    flush(half_ref)
    need(spatial_ref)
    sums_ref[...] = jnp.zeros_like(sums_ref)
    for tap_index in range(9):
        tap_rows_out(
            sums_ref, tap_index, pixels, side, dot_nt(low_ref[...], spatial_ref[tap_index])
        )
    grad_ref[...] = fold_columns(sums_ref, pixels, side)
    norm_two_slope(grad_ref, first_ref, first_stats_ref, mask_ref, gain_ref, bias_ref, 0, copies_ref)


def back_deform_body(
    total_ref, grad_in_ref, second_ref, second_stats_ref, first_ref, first_stats_ref, mask_ref,
    count_ref, place_ref, gain_ref, bias_ref, spatial_ref, act_ref, offsets_ref, weights_ref,
    low_ref, half_ref, grad_ref, copies_ref, result_ref, grad_offsets_ref,
    sums_ref, padded_ref, shifted_ref,
):
    pixels, width = second_ref.shape
    side = 1 << ((pixels.bit_length() - 1) // 2)
    low_second(
        total_ref, grad_in_ref, second_ref, second_stats_ref, mask_ref, count_ref,
        gain_ref[:, width : 2 * width], low_ref, result_ref,
    )
    half = half_ref.shape[1]
    other = pl.multiple_of((1 - place_ref[0, 0]) * half, lane)
    half_ref[...] = low_ref[:, pl.ds(other, half)].astype(f32)
    flush(low_ref)
    flush(half_ref)
    for ref in (first_ref, first_stats_ref, spatial_ref, act_ref, offsets_ref, weights_ref):
        need(ref)
    offsets = offsets_ref[...]
    outs = offsets.shape[1]
    channel = lax.broadcasted_iota(jnp.int32, (pixels, outs), 1)
    moved = jnp.zeros((pixels, outs), f32)
    grad_ref[...] = jnp.zeros_like(grad_ref)
    for tap_index in range(9):
        dist_y, dist_x, bump_y, bump_x = tap_factors(offsets, tap_index, side)
        weight_y, weight_x = (bump_y * bump_y, bump_x * bump_x)
        sampling = (weight_y * weight_x).astype(bf16)
        piece = dot_nt(low_ref[...], spatial_ref[tap_index]).astype(bf16)
        grad_ref[...] = grad_ref[...] + dot_tn(sampling, piece)
        product = -4.0 * dot_nt(piece, act_ref[...])
        along_y = jnp.sum(product * (dist_y * bump_y * weight_x), axis=1, keepdims=True)
        along_x = jnp.sum(product * (dist_x * bump_x * weight_y), axis=1, keepdims=True)
        moved = moved + jnp.where(channel == 2 * tap_index, along_y, 0.0)
        moved = moved + jnp.where(channel == 2 * tap_index + 1, along_x, 0.0)
    moved_low = moved.astype(bf16)
    padded_ref[...] = jnp.zeros_like(padded_ref)
    padded_ref[pl.ds(2 * side, pixels), :] = act_ref[...].astype(f32)
    build_taps(padded_ref, shifted_ref, pixels, side)
    sums_ref[...] = jnp.zeros_like(sums_ref)
    grad_offsets_ref[...] = jnp.zeros_like(grad_offsets_ref)
    for tap_index in range(9):
        taps = tap_of(shifted_ref, tap_index, pixels, side)
        first = tap_index * outs
        grad_offsets_ref[first : first + outs, :] = dot_tn(moved_low, taps)
        tap_rows_out(
            sums_ref, tap_index, pixels, side, dot_nt(moved_low, weights_ref[tap_index])
        )
    grad_ref[...] = grad_ref[...] + fold_columns(sums_ref, pixels, side)
    norm_two_slope(grad_ref, first_ref, first_stats_ref, mask_ref, gain_ref, bias_ref, 0, copies_ref)


def back_between_body(
    total_ref, grad_ref, first_ref, first_stats_ref, grad_sum_ref, summed_ref, pre_ref, stats_ref,
    mask_ref, count_ref, gain_ref, squeeze_ref,
    low_ref, wide_ref, next_ref, copies_ref, result_ref,
):
    pixels, width = first_ref.shape
    channels = pre_ref.shape[1]
    low_second(
        total_ref, grad_ref, first_ref, first_stats_ref, mask_ref, count_ref,
        gain_ref[:, :width], low_ref, result_ref,
    )
    wide_ref[...] = low_ref[...].astype(f32)
    flush(low_ref)
    flush(wide_ref)
    need(stats_ref)
    need(squeeze_ref)
    mean, var = (stats_ref[0:1, :], stats_ref[1:2, :])
    inverse = lax.rsqrt(var + eps_norm)
    sums, prods = ([], [])
    for part, (start, size) in enumerate(spans_of(channels, 512)):
        span = pl.ds(start, size)
        cut = slice(start, start + size)
        for ref in (grad_sum_ref, summed_ref, pre_ref):
            need(ref, part)
        next_ref[:, span] = dot_nt(low_ref[...], squeeze_ref[start : start + size, :])

        def both(rows):
            mask = wide_mask(mask_ref, rows, size)
            slope = silu_slope(summed_ref[rows, span])
            grad = (next_ref[rows, span] + grad_sum_ref[rows, span]) * mask * slope
            next_ref[rows, span] = grad
            return (grad, grad * ((pre_ref[rows, span] - mean[:, cut]) * inverse[:, cut]))

        total_grad, total_prod = two_sums(pixels, size, both)
        sums.append(total_grad)
        prods.append(total_prod)
        flush(next_ref, part)
    write_copies(copies_ref, sums + prods)


def last_low_body(
    total_ref, grad_ref, first_ref, first_stats_ref, mask_ref, count_ref, gain_ref,
    low_ref, wide_ref, result_ref,
):
    width = first_ref.shape[1]
    low_second(
        total_ref, grad_ref, first_ref, first_stats_ref, mask_ref, count_ref,
        gain_ref[:, :width], low_ref, result_ref,
    )
    wide_ref[...] = low_ref[...].astype(f32)


def last_body(low_ref, grad_sum_ref, squeeze_ref, image_ref, token_ref):
    token_ref[...] = jnp.zeros_like(token_ref)
    for start, size in spans_of(image_ref.shape[1], 256):
        block = dot_nt(low_ref[...], squeeze_ref[start : start + size, :])
        image_ref[:, start : start + size] = (
            block + grad_sum_ref[:, start : start + size]
        ).astype(bf16)


def sum_copies_body(copies_ref, out_ref):
    total = jnp.sum(copies_ref[...], axis=0)

    def one_copy(step, carry):
        out_ref[step] = total
        return carry

    lax.fori_loop(0, out_ref.shape[0], one_copy, 0)


def offsets_body(sums_ref, out_ref):
    outs = out_ref.shape[1]
    for tap in range(out_ref.shape[0]):
        out_ref[tap] = sums_ref[tap * outs : (tap + 1) * outs, :]


block_cols = 256


def split_chunks(scratch_ref, keep_ref, send_ref, own, place, spot):
    for index in range(keep_ref.shape[0]):
        low = index & ((1 << place) - 1)
        base = ((index >> place) << (place + 1)) | low
        keep_ref[index, spot] = scratch_ref[base + own * (1 << place)]
        send_ref[index, spot] = scratch_ref[base + (1 - own) * (1 << place)]


def weights_body(kinds, firsts, spans, own_place_ref, *refs):
    groups = [refs[4 * place : 4 * place + 4] for place in range(len(kinds))]
    rest = refs[4 * len(kinds) :]
    results = 2 * len(spans) if firsts else 1
    outs, token_ref = (rest[:results], rest[results])
    chunks_ref, scratch = (rest[results + 1], list(rest[results + 2 :]))
    token_ref[...] = jnp.zeros_like(token_ref)
    count, depth, _ = chunks_ref.shape
    makers = []
    for kind, (rows_ref, rows_other_ref, cols_ref, cols_other_ref) in zip(kinds, groups):
        for ref in (rows_ref, rows_other_ref, cols_ref, cols_other_ref):
            need(ref)
        pixels, half = cols_other_ref.shape
        side = 1 << ((pixels.bit_length() - 1) // 2)
        both_cols = scratch.pop(0)
        start_own = pl.multiple_of(own_place_ref[0, 0] * half, lane)
        both_cols[pl.ds(0, pixels), :] = cols_ref[:, pl.ds(start_own, half)]
        both_cols[pl.ds(pixels, pixels), :] = cols_other_ref[...].astype(bf16)
        if kind == "rows":
            both_rows = scratch.pop(0)
            both_rows[pl.ds(0, pixels), :] = rows_ref[...]
            both_rows[pl.ds(pixels, pixels), :] = rows_other_ref[...].astype(bf16)
            for start in range(0, half, block_cols):
                makers.append(
                    lambda rows=both_rows, cols=both_cols, start=start: dot_tn(
                        rows[...], cols[:, start : start + block_cols]
                    )
                )
        elif kind == "plain":
            padded, taps = (scratch.pop(0), (scratch.pop(0), scratch.pop(0)))
            for source, shifted in zip((rows_ref, rows_other_ref), taps):
                padded[...] = jnp.zeros_like(padded)
                padded[pl.ds(2 * side, pixels), :] = source[...]
                build_taps(padded, shifted, pixels, side)
            for tap in range(9):
                makers.append(
                    lambda taps=taps, cols=both_cols, tap=tap, pixels=pixels, side=side: dot_tn(
                        tap_of(taps[0], tap, pixels, side), cols[pl.ds(0, pixels), :]
                    )
                    + dot_tn(tap_of(taps[1], tap, pixels, side), cols[pl.ds(pixels, pixels), :])
                )
        else:
            width = cols_ref.shape[1]
            for tap in range(9):
                span = slice(tap * width, (tap + 1) * width)
                makers.append(
                    lambda one=rows_ref, two=rows_other_ref, cols=both_cols, span=span, pixels=pixels: dot_tn(
                        one[:, span], cols[pl.ds(0, pixels), :]
                    )
                    + dot_tn(two[:, span], cols[pl.ds(pixels, pixels), :])
                )
    if not firsts:
        for part, maker in enumerate(makers):
            outs[0][:, part] = maker().reshape(count, depth, block_cols)
        return
    for stream, (start, stop) in enumerate(spans):
        bit = firsts[stream]
        own = own_place_ref[0, bit]
        for part in range(start, stop):
            chunks_ref[...] = makers[part]().reshape(count, depth, block_cols)
            split_chunks(
                chunks_ref, outs[2 * stream], outs[2 * stream + 1], own, bit - 1, part - start
            )
        flush(outs[2 * stream + 1])
        flush(outs[2 * stream])


def advance_body(groups, own_place_ref, *refs):
    streams = sum(count for count, _ in groups)
    kept, came = (refs[:streams], refs[streams : 2 * streams])
    outs = list(refs[2 * streams :])
    token_ref = outs.pop()
    token_ref[...] = jnp.zeros_like(token_ref)
    at, used, start = (0, 0, 0)
    for count, spot in groups:
        members = list(range(at, at + count))
        at += count
        for stream in members:
            need(kept[stream])
            need(came[stream])
        if spot is None:
            for stream in members:
                stop = start + kept[stream].shape[1]
                outs[-1][start:stop] = kept[stream][0] + came[stream][0]
                start = stop
            continue
        bit, place = spot
        own = own_place_ref[0, bit]
        for target_ref, side in ((outs[used + 1], 1 - own), (outs[used], own)):
            first = 0
            for stream in members:
                stop = first + kept[stream].shape[1]
                for index in range(target_ref.shape[0]):
                    low = index & ((1 << place) - 1)
                    base = ((index >> place) << (place + 1)) | low
                    chunk = base + side * (1 << place)
                    target_ref[index, first:stop] = kept[stream][chunk] + came[stream][chunk]
                first = stop
            flush(target_ref)
        used += 2


def assemble_body(kinds, labels, summed, own_place_ref, own_ref, pair_ref, side_ref, both_ref, *targets):
    rows, cols = own_ref.shape[-2:]
    pair, line = (own_place_ref[0, 0], own_place_ref[0, 1])
    for row_at, col_at in ((0, 0), (0, 1), (1, 0), (1, 1)):
        if summed and row_at:
            continue
        same_row, same_col = (line == row_at, pair == col_at)
        row_span = slice(row_at * rows, (row_at + 1) * rows)
        for part, (place, step) in enumerate(labels):
            near = jnp.where(same_col, own_ref[part], pair_ref[part])
            far = jnp.where(same_col, side_ref[part], both_ref[part])
            value = near + far if summed else jnp.where(same_row, near, far)
            target = targets[place]
            if kinds[place] == "rows":
                parts = target.shape[1] // 2 // cols
                at = (col_at * parts + step) * cols
                target[row_span, at : at + cols] = value
            else:
                target[step, row_span, col_at * cols : (col_at + 1) * cols] = value
    for target in targets:
        flush(target)


def gate_body(*refs):
    pass


def gate(arrays, after):
    hbm = pl.BlockSpec(memory_space=pltpu.HBM)
    return pl.pallas_call(
        gate_body,
        out_shape=tuple(shape_of(part.shape) for part in arrays),
        in_specs=[hbm] * len(arrays) + [pl.BlockSpec(memory_space=pl.ANY)] * len(after),
        out_specs=(hbm,) * len(arrays),
        input_output_aliases={place: place for place in range(len(arrays))},
    )(*arrays, *after)


class Comm:
    def __init__(self, wide_size, narrow_size):
        self.total = wide_size * narrow_size
        self.bits = self.total.bit_length() - 1
        self.low = narrow_size.bit_length() - 1
        self.index = lax.axis_index("wide") * narrow_size + lax.axis_index("narrow")
        self.places = jnp.stack([self.bit(place) for place in range(self.bits)])[None, :]

    def bit(self, place):
        return (self.index >> place) & 1

    def swap_over(self, values, flips):
        pairs = [(source, source ^ flips) for source in range(self.total)]
        return lax.ppermute(values, axes, pairs)

    def swap(self, values, place):
        return self.swap_over(values, 1 << place)

    def sync(self, copies):
        return Near(lax.all_to_all(copies, axes, 0, 0, tiled=True))

    def order(self, letters):
        named = {"y": 1, "x": self.low, "a": self.low + 1, "b": self.low + 2}
        return [named[letter] for letter in letters] + list(range(self.low + 3, self.bits))


token = (8, lane)


class Group:
    def __init__(self, comm, total, plan):
        self.comm = comm
        self.orders = [comm.order(letters) for letters, _ in plan]
        self.left = [
            [place for place in range(1, comm.bits) if place != order[0]] for order in self.orders
        ]
        shares = [share for _, share in plan]
        ends = [total * sum(shares[: at + 1]) // sum(shares) for at in range(len(plan))]
        self.bounds = tuple(zip([0] + ends[:-1], ends))
        self.total = total
        self.arrays = {}
        self.labels = []
        self.kinds = ()
        self.shapes = []
        self.at = 1

    def add(self, kind, group, after=()):
        comm = self.comm
        pixels, rows = group[0].shape
        if kind == "given":
            rows = group[2].shape[1]
        chunks = 1 << (comm.bits - 1 if self.orders else comm.bits - comm.low)
        depth = rows // chunks
        half = getattr(group[3], "value", group[3]).shape[1]
        side = 1 << ((pixels.bit_length() - 1) // 2)
        scratch = [pltpu.VMEM((chunks, depth, block_cols), f32), pltpu.VMEM((2 * pixels, half), bf16)]
        wide_depth = rows >> (comm.bits - comm.low)
        self.shapes.append((wide_depth, 2 * half) if kind == "rows" else (9, wide_depth, 2 * half))
        if kind == "rows":
            scratch.append(pltpu.VMEM((2 * pixels, rows), bf16))
        if kind == "plain":
            scratch.append(pltpu.VMEM((pixels + 4 * side, rows), f32))
            scratch += [pltpu.VMEM((3, pixels + 4 * side, rows), bf16)] * 2
        count = half // block_cols if kind == "rows" else 9
        begin = len(self.labels)
        self.labels += [(len(self.kinds), step) for step in range(count)]
        self.kinds += (kind,)
        keys, spans, outs, pieces, begun = ([], [], [], {}, {})
        if not self.orders:
            if self.arrays:
                begun[0] = self.arrays[0, 0]
            pieces[0] = (begin, count)
            outs.append(shape_of((chunks, self.total, depth, block_cols)))
        for stream, (start, stop) in enumerate(self.bounds):
            low, high = (max(start, begin), min(stop, begin + count))
            if low >= high:
                continue
            spans.append((low - begin, high - begin))
            keys.append(stream)
            for which in range(2):
                if (stream, which) in self.arrays:
                    begun[len(outs)] = self.arrays[stream, which]
                pieces[len(outs)] = (low - start, high - low)
                outs.append(shape_of((chunks // 2, stop - start, depth, block_cols)))
        args = (comm.places,) + tuple(group)
        made = call(
            functools.partial(
                weights_body, (kind,), tuple(self.orders[stream][0] for stream in keys), tuple(spans)
            ),
            outs + [shape_of(token)], args, (0,), scratch, after, tuple(range(1, len(args))),
            pieces=pieces, begun=begun,
        )
        if not self.orders:
            self.arrays[0, 0] = made[0]
        for number, stream in enumerate(keys):
            self.arrays[stream, 0] = made[2 * number]
            self.arrays[stream, 1] = made[2 * number + 1]
        return made[-1]

    def offload(self):
        self.share = lax.psum_scatter(self.arrays[0, 0], "wide", scatter_dimension=0, tiled=True)

    def collect(self, after):
        (share,) = gate((self.share.reshape(self.share.shape[1:]),), after)
        self.join(share)

    def join(self, share):
        beside = self.comm.swap(share, 1)
        self.quarters = [share, self.comm.swap(share, 0), beside, self.comm.swap(beside, 0)]

    def start(self, after=()):
        sent = [self.arrays[stream, 1] for stream in range(len(self.orders))]
        sent = gate(sent, after) if after else sent
        self.streams = [
            [(self.arrays[stream, 0], self.comm.swap(sent[stream], order[0]))]
            for stream, order in enumerate(self.orders)
        ]

    def advance(self, after=()):
        comm = self.comm
        if len({tuple(order[self.at :]) for order in self.orders}) == 1:
            self.orders, self.left = (self.orders[:1], self.left[:1])
            self.streams = [sum(self.streams, [])]
        groups, outs = ([], [])
        last = self.at == len(self.orders[0])
        total = 0
        for order, left, members in zip(self.orders, self.left, self.streams):
            spot = None
            parts = sum(kept.shape[1] for kept, _ in members)
            shape = members[0][0].shape
            total += parts
            if not last:
                bit = order[self.at]
                spot = (bit, left.index(bit))
                left.remove(bit)
                outs += [shape_of((shape[0] // 2, parts) + shape[2:])] * 2
            groups.append((len(members), spot))
        if last:
            outs = [shape_of((total,) + shape[2:])]
        flat = [pair for members in self.streams for pair in members]
        *pieces, mark = call(
            functools.partial(advance_body, tuple(groups)),
            outs + [shape_of(token)],
            (comm.places, *(kept for kept, _ in flat), *(Near(came) for _, came in flat)),
            (0,), (), after, tuple(range(1, 1 + 2 * len(flat))),
        )
        if last:
            self.join(pieces[0])
        else:
            self.streams = [
                [(pieces[2 * place], comm.swap(pieces[2 * place + 1], order[self.at]))]
                for place, order in enumerate(self.orders)
            ]
        self.at += 1
        return mark

    def ended(self):
        return self.at > len(self.orders[0])

    def finish(self, after=()):
        while self.orders and not self.ended():
            self.advance(after)
        kinds, shapes = (self.kinds, self.shapes)
        outs = [shape_of(shape) for shape in shapes]
        return call(
            functools.partial(assemble_body, kinds, tuple(self.labels), not self.orders),
            outs, (self.comm.places, self.quarters[0], *(Near(part) for part in self.quarters[1:])), (0,), (), after,
        )


def per_device(
    wide_size, narrow_size, images, image_sizes, offset_shift, squeeze_one, offsets_one, spatial_one,
    expand_one, squeeze_two, spatial_two, expand_two, norm_gain_one, norm_bias_one, norm_gain_two,
    norm_bias_two, run_mean_one, run_var_one, run_mean_two, run_var_two, grad_output,
):
    comm = Comm(wide_size, narrow_size)
    side, channels = (images.shape[1], images.shape[3])
    pixels = side * side
    width = squeeze_one.shape[1]
    outs = offsets_one.shape[2]
    total = comm.total
    small = (total, 2 * width // lane, lane)
    quarters = channels // 512
    large = (total, 2 * channels // lane, lane)
    flat = images.reshape(pixels, channels)
    grad_out = grad_output.reshape(pixels, channels)
    gain_one, bias_one = (norm_gain_one[None, :], norm_bias_one[None, :])
    gain_two, bias_two = (norm_gain_two[None, :], norm_bias_two[None, :])
    field = shape_of((pixels, width))
    field_low = shape_of((pixels, width), bf16)
    plane = shape_of((pixels, channels))
    plane_low = shape_of((pixels, channels), bf16)
    half_plane = shape_of((pixels, channels // 2))
    half_field = shape_of((pixels, width // 2))
    stats_small, stats_large = (shape_of((2, width)), shape_of((2, channels)))
    padded = pltpu.VMEM((pixels + 4 * side, width), f32)
    shifted = pltpu.VMEM((3, pixels + 4 * side, width), bf16)
    tap_sums = pltpu.VMEM((3, pixels + 4 * side, width), f32)

    first_one, mask, copies, images_half = call(
        first_body,
        (field, shape_of((pixels, lane)), shape_of((total, 2 * width // lane + 8, lane)), half_plane),
        (image_sizes, comm.places, flat, squeeze_one),
        (0, 1),
    )
    images_half = comm.swap(images_half, 0)
    copies = comm.sync(copies)
    (act_one, act_wide, columns, offsets, second_one, copies, first_stats_one, count) = call(
        deform_body,
        (
            field_low, field, shape_of((pixels, 9 * width), bf16),
            shape_of((pixels, outs)), field, shape_of(small), stats_small, shape_of((8, lane)),
        ),
        (
            copies, first_one, mask, gain_one, bias_one, offsets_one,
            offset_shift.astype(f32)[None, :], spatial_one,
        ),
        (),
        (padded, shifted),
        (),
        (5, 7), blocks_out={2: 9},
    )
    act_other, offsets_other = (comm.swap(act_wide, 0), comm.swap(offsets, 0))
    copies = comm.sync(copies)
    act_second_one, act_second_wide_one, third_one, copies, second_stats_one = call(
        third_body,
        (field_low, field, plane, shape_of(large), stats_small),
        (copies, second_one, mask, count, gain_one, bias_one, expand_one),
        blocks={6: quarters}, blocks_out={2: quarters},
    )
    (columns_other,) = call(
        columns_body, (shape_of((pixels, 9 * width), bf16),),
        (Near(act_other), Near(offsets_other)), (), (pltpu.VMEM((pixels, width), bf16),), (second_stats_one,),
    )
    act_second_wide_one = comm.swap(act_second_wide_one, 0)
    copies = comm.sync(copies)
    summed_one, low_two, low_half, first_two, copies, third_stats_one = call(
        between_body,
        (plane, plane_low, half_plane, field, shape_of(small), stats_large),
        (copies, third_one, flat, mask, count, comm.places, gain_one, bias_one, squeeze_two),
        (5,), (), (columns_other,), (8,),
        blocks={1: quarters, 2: quarters}, blocks_out={0: quarters, 1: quarters},
    )
    low_half = comm.swap(low_half, 0)
    copies = comm.sync(copies)
    act_wide_two, second_two, copies, first_stats_two = call(
        plain_body,
        (field, field, shape_of(small), stats_small),
        (copies, first_two, mask, count, gain_two, bias_two, spatial_two),
        (),
        (padded, shifted), late=(6,),
    )
    act_wide_two_other = comm.swap(act_wide_two, 0)
    copies = comm.sync(copies)
    act_second_two, act_second_wide_two, third_two, copies, second_stats_two = call(
        third_body,
        (field_low, field, plane, shape_of(large), stats_small),
        (copies, second_two, mask, count, gain_two, bias_two, expand_two),
        blocks={6: quarters}, blocks_out={2: quarters},
    )
    act_second_wide_two = comm.swap(act_second_wide_two, 0)
    copies = comm.sync(copies)
    output_images, grad_sum_two, copies, third_stats_two = call(
        turn_body,
        (plane_low, plane, shape_of(large), stats_large),
        (copies, third_two, summed_one, grad_out, mask, count, gain_two, bias_two),
        blocks={1: quarters, 2: quarters, 3: quarters}, blocks_out={0: quarters, 1: quarters},
    )
    copies = comm.sync(copies)
    low_third_two, third_half, grad_second_two, copies, third_result_two = call(
        back_third_body,
        (plane_low, half_plane, field, shape_of(small), stats_large),
        (
            copies, grad_sum_two, third_two, third_stats_two, second_two, second_stats_two, mask, count,
            comm.places, gain_two, bias_two, expand_two,
        ),
        (8,), late=(4, 5, 11), blocks={1: quarters, 2: quarters}, blocks_out={0: quarters},
    )
    third_half = comm.swap(third_half, 0)
    copies = comm.sync(copies)
    blocks = channels // 2 // block_cols
    plan = (("xyab", 6), ("yaxb", 6), ("axyb", 5))
    group_two = Group(comm, 2 * blocks + 9, plan)
    group_one = Group(comm, 2 * blocks + 9, (("xayb", 7), ("yxab", 7), ("ayxb", 3)))
    done = group_two.add("rows", (act_second_two, act_second_wide_two, low_third_two, Near(third_half)))
    low_second_two, second_half, grad_first_two, copies, second_result_two = call(
        back_plain_body,
        (field_low, half_field, field, shape_of(small), stats_small),
        (
            copies, grad_second_two, second_two, second_stats_two, first_two, first_stats_two, mask,
            count, comm.places, gain_two, bias_two, spatial_two,
        ),
        (8,),
        (tap_sums,),
        (done,),
        (11,),
    )
    second_half = comm.swap(second_half, 0)
    copies = comm.sync(copies)
    done = group_two.add("plain", (act_wide_two, act_wide_two_other, low_second_two, Near(second_half)))
    low_first_two, low_first_wide, grad_sum_one, copies, first_result_two = call(
        back_between_body,
        (field_low, field, plane, shape_of(large), stats_small),
        (
            copies, grad_first_two, first_two, first_stats_two, grad_sum_two, summed_one, third_one,
            third_stats_one, mask, count, gain_two, squeeze_two,
        ),
        (),
        (),
        (done,),
        (4, 5, 6, 7, 11),
        blocks={4: quarters, 5: quarters, 6: quarters}, blocks_out={2: quarters},
    )
    low_first_wide = comm.swap(low_first_wide, 0)
    copies = comm.sync(copies)
    done = group_two.add("rows", (low_first_two, Near(low_first_wide), low_two, low_half))
    low_third_one, third_half, grad_second_one, copies, third_result_one = call(
        back_third_body,
        (plane_low, half_plane, field, shape_of(small), stats_large),
        (
            copies, grad_sum_one, third_one, third_stats_one, second_one, second_stats_one, mask, count,
            comm.places, gain_one, bias_one, expand_one,
        ),
        (8,),
        (),
        (done,),
        (4, 5, 11),
        blocks={1: quarters, 2: quarters}, blocks_out={0: quarters},
    )
    third_half = comm.swap(third_half, 0)
    copies = comm.sync(copies)
    done = group_one.add("rows", (act_second_one, act_second_wide_one, low_third_one, Near(third_half)))
    group_two.start((copies.value, done))
    slots = -(-9 * outs // total)
    slots = -(-slots // 8) * 8
    low_second_one, second_half, grad_first_one, copies, second_result_one, grad_offsets = call(
        back_deform_body,
        (
            field_low, half_field, field, shape_of(small), stats_small, shape_of((total * slots, width)),
        ),
        (
            copies, grad_second_one, second_one, second_stats_one, first_one, first_stats_one, mask,
            count, comm.places, gain_one, bias_one, spatial_one, act_one, offsets, offsets_one,
        ),
        (8,),
        (tap_sums, padded, shifted),
        (done,),
        (4, 5, 11, 12, 13, 14),
    )
    second_half = comm.swap(second_half, 0)
    copies = comm.sync(copies)
    done = group_one.add("given", (columns, columns_other, low_second_one, Near(second_half)))
    done = group_two.advance((done,))
    low_first_one, low_first_wide, first_result_one = call(
        last_low_body,
        (field_low, field, stats_small),
        (copies, grad_first_one, first_one, first_stats_one, mask, count, gain_one),
        (), (), (done,),
    )
    low_first_wide = comm.swap(low_first_wide, 0)
    grad_offsets = comm.sync(grad_offsets.reshape(total, slots, width))
    done = group_one.add(
        "rows", (low_first_one, Near(low_first_wide), flat, images_half), (first_result_one, done)
    )
    done = group_two.advance((done,))
    grad_images, done = call(
        last_body,
        (plane_low, shape_of(token)),
        (low_first_one, grad_sum_one, squeeze_one),
        (), (), (done,),
    )
    done = group_two.advance((done, grad_offsets.value))
    group_one.start((done,))
    (grad_offsets,) = call(
        sum_copies_body, (shape_of((total, slots, width)),), (grad_offsets,), (), (),
        (done,),
    )
    grad_offsets = comm.sync(grad_offsets).value
    done = group_two.advance((done,))
    done = group_one.advance((done,))
    (grad_offsets,) = call(
        offsets_body, (shape_of((9, outs, width)),), (grad_offsets.reshape(total * slots, width),), (), (),
        (done,),
    )
    done = group_one.advance((grad_offsets,))
    done = group_one.advance((done,))
    grad_expand_two, grad_spatial_two, grad_squeeze_two = group_two.finish((done,))
    grad_expand_one, grad_spatial_one, grad_squeeze_one = group_one.finish((grad_squeeze_two,))

    def laid(parts, row):
        return jnp.concatenate([part[row] for part in parts])

    results_one = (first_result_one, second_result_one, third_result_one)
    results_two = (first_result_two, second_result_two, third_result_two)
    stats_one = (first_stats_one, second_stats_one, third_stats_one)
    stats_two = (first_stats_two, second_stats_two, third_stats_two)
    pixel_count = count[0, 0]
    unbias = pixel_count / (pixel_count - 1.0)
    fresh = 1.0 - keep_rate
    return (
        output_images.reshape(images.shape),
        grad_images.reshape(images.shape),
        grad_squeeze_one.T,
        grad_offsets.transpose(0, 2, 1),
        grad_spatial_one,
        grad_expand_one,
        grad_squeeze_two.T,
        grad_spatial_two,
        grad_expand_two,
        laid(results_one, 1),
        laid(results_one, 0),
        laid(results_two, 1),
        laid(results_two, 0),
        keep_rate * run_mean_one + fresh * laid(stats_one, 0),
        keep_rate * run_var_one + fresh * laid(stats_one, 1) * unbias,
        keep_rate * run_mean_two + fresh * laid(stats_two, 0),
        keep_rate * run_var_two + fresh * laid(stats_two, 1) * unbias,
    )


def solution(mesh):
    images_spec = P(axes, None, None, None)
    whole = P()
    return jax.shard_map(
        functools.partial(per_device, mesh.shape["wide"], mesh.shape["narrow"]),
        mesh=mesh,
        in_specs=(images_spec, P(axes, None)) + (whole,) * 16 + (images_spec,),
        out_specs=(
            images_spec,
            images_spec,
            P(None, "wide"),
            whole,
            P(None, "wide", None),
            P("wide", None),
            P(None, "wide"),
            P(None, "wide", None),
            P("wide", None),
        )
        + (whole,) * 8,
        check_vma=False,
    )
```

```python
import functools

import jax
import jax.numpy as jnp
from jax import lax
from jax.experimental import pallas as pl
from jax.experimental.pallas import tpu as pltpu
from jax.sharding import PartitionSpec as P

eps_norm = 1e-05
keep_rate = 0.6
vmem_bytes = 52 * 1024 * 1024
lane = 128
tile_rows = 16
row_unroll = 2
axes = ("wide", "narrow")
f32 = jnp.float32
bf16 = jnp.bfloat16


def shape_of(shape, kind=f32):
    return jax.ShapeDtypeStruct(shape, kind)


copies_of = {}


def need(ref, part=None):
    entries = copies_of.get(id(ref), [])
    for entry in entries if part is None else entries[part : part + 1]:
        if entry[1]:
            entry[1] = False
            entry[0].wait()
    return ref


def flush(ref, part=None):
    entries = copies_of.get(id(ref), [])
    for entry in entries if part is None else entries[part : part + 1]:
        if entry[1]:
            entry[1] = False
            entry[0].start()


def column_copies(source, target, flags, first, count):
    if count == 1:
        return [[pltpu.make_async_copy(source, target, flags.at[first]), True]]
    width = source.shape[1] // count
    spans = [pl.ds(width * at, width) for at in range(count)]
    return [
        [pltpu.make_async_copy(source.at[:, span], target.at[:, span], flags.at[first + at]), True]
        for at, span in enumerate(spans)
    ]


class Near:
    def __init__(self, value):
        self.value = value


def call(body, outs, args, smem=(), scratch=(), after=(), late=(), stay_out=(), pieces=None, begun=None, blocks=None, blocks_out=None):
    stay = tuple(place for place, arg in enumerate(args) if isinstance(arg, Near))
    args = tuple(arg.value if isinstance(arg, Near) else arg for arg in args)
    pieces = pieces or {}
    begun = begun or {}
    blocks = blocks or {}
    blocks_out = blocks_out or {}
    hbm = pl.BlockSpec(memory_space=pltpu.HBM)
    vmem = pl.BlockSpec(memory_space=pltpu.VMEM)
    specs = [
        pl.BlockSpec(memory_space=pltpu.SMEM) if place in smem else vmem if place in stay else hbm
        for place in range(len(args))
    ] + [pl.BlockSpec(memory_space=pl.ANY)] * len(after) + [hbm] * len(begun)
    moved = [place for place in range(len(args)) if place not in smem and place not in stay]
    used, extra, made = (len(args), len(after) + len(begun), len(outs))
    sent = [slot for slot in range(made) if slot not in stay_out]

    def kernel(*refs):
        given = list(refs[:used])
        results = list(refs[used + extra : used + extra + made])
        rest = refs[used + extra + made :]
        in_slots, out_slots = (rest[: len(moved)], rest[len(moved) : len(moved) + len(sent)])
        in_flags, out_flags = rest[len(moved) + len(sent) : len(moved) + len(sent) + 2]
        copies_of.clear()
        first = 0
        for slot, place in enumerate(moved):
            count = blocks.get(place, 1)
            entries = column_copies(given[place], in_slots[slot], in_flags, first, count)
            first += count
            for entry in entries:
                entry[0].start()
            copies_of[id(in_slots[slot])] = entries
            given[place] = in_slots[slot]
        for place in moved:
            if place not in late and place not in blocks:
                need(given[place])
        first = 0
        for slot, place in enumerate(sent):
            count = blocks_out.get(place, 1)
            target = results[place].at[:, pl.ds(*pieces[place])] if place in pieces else results[place]
            copies_of[id(out_slots[slot])] = column_copies(out_slots[slot], target, out_flags, first, count)
            first += count
            results[place] = out_slots[slot]
        body(*given, *results, *rest[len(moved) + len(sent) + 2 :])
        for place in moved:
            need(given[place])
        for slot in out_slots:
            flush(slot)
        for slot in out_slots:
            for entry in copies_of[id(slot)]:
                entry[0].wait()
        copies_of.clear()

    slots = [pltpu.VMEM(args[place].shape, args[place].dtype) for place in moved]
    for place in sent:
        shape = outs[place].shape
        if place in pieces:
            shape = (shape[0], pieces[place][1]) + shape[2:]
        slots.append(pltpu.VMEM(shape, outs[place].dtype))
    in_count = sum(blocks.get(place, 1) for place in moved)
    out_count = sum(blocks_out.get(place, 1) for place in sent)
    flags = [pltpu.SemaphoreType.DMA((max(in_count, 1),)), pltpu.SemaphoreType.DMA((max(out_count, 1),))]
    return pl.pallas_call(
        kernel,
        input_output_aliases={used + len(after) + at: place for at, place in enumerate(begun)},
        out_shape=tuple(outs),
        in_specs=specs,
        out_specs=tuple(vmem if place in stay_out else hbm for place in range(made)),
        scratch_shapes=slots + flags + list(scratch),
        compiler_params=pltpu.CompilerParams(vmem_limit_bytes=vmem_bytes),
    )(*args, *after, *begun.values())


def dot_nn(first_op, second_op):
    return lax.dot_general(
        first_op, second_op, (((1,), (0,)), ((), ())), preferred_element_type=f32
    )


def dot_nt(first_op, second_op):
    return lax.dot_general(
        first_op, second_op, (((1,), (1,)), ((), ())), preferred_element_type=f32
    )


def dot_tn(first_op, second_op):
    return lax.dot_general(
        first_op, second_op, (((0,), (0,)), ((), ())), preferred_element_type=f32
    )


def logistic(values):
    return 0.5 * jnp.tanh(0.5 * values) + 0.5


def silu(values):
    return values * logistic(values)


def silu_slope(values):
    gate = logistic(values)
    return gate * (1.0 + values * (1.0 - gate))


def flat_row(rows, start, width):
    first = start // lane
    return jnp.concatenate(
        [rows[first + step : first + step + 1, :] for step in range(width // lane)], axis=1
    )


def fold_row(row):
    return [row[:, step * lane : (step + 1) * lane] for step in range(row.shape[1] // lane)]


def write_copies(copies_ref, rows, extra=None):
    packed = jnp.concatenate([piece for row in rows for piece in fold_row(row)], axis=0)
    if extra is not None:
        packed = jnp.concatenate([packed, extra], axis=0)

    def one_copy(step, carry):
        copies_ref[step] = packed
        return carry

    lax.fori_loop(0, copies_ref.shape[0], one_copy, 0)


def read_copies(copies_ref):
    return jnp.sum(copies_ref[...], axis=0)


def wide_mask(mask_ref, rows, width):
    return jnp.concatenate([mask_ref[rows, :]] * (width // lane), axis=1)


def eight_rows(values):
    folded = values[:8]
    for start in range(8, values.shape[0], 8):
        folded = folded + values[start : start + 8]
    return folded


def row_loop(pixels, body, carry):
    def step(index, state):
        return body(pl.ds(pl.multiple_of(index * tile_rows, tile_rows), tile_rows), state)

    return lax.fori_loop(0, pixels // tile_rows, step, carry, unroll=row_unroll)


def two_sums(pixels, width, body):
    zero = jnp.zeros((8, width), f32)

    def step(rows, state):
        first, second = body(rows)
        return (state[0] + eight_rows(first), state[1] + eight_rows(second))

    first, second = row_loop(pixels, step, (zero, zero))
    return (jnp.sum(first, axis=0, keepdims=True), jnp.sum(second, axis=0, keepdims=True))


def moments(total, width, count):
    mean = flat_row(total, 0, width) / count
    var = flat_row(total, width, width) / count - mean * mean
    return (mean, var)


def scale_shift(mean, var, gain, bias):
    inverse = lax.rsqrt(var + eps_norm)
    scale = gain * inverse
    return (scale, bias - mean * scale)


def spans_of(width, block):
    return [(start, min(block, width - start)) for start in range(0, width, block)]


def grad_rows(total, stats, gain, count, width):
    mean, var = (stats[0:1], stats[1:2])
    inverse = lax.rsqrt(var + eps_norm)
    sum_grad = flat_row(total, 0, width)
    sum_prod = flat_row(total, width, width)
    return (
        gain * inverse,
        sum_grad / count,
        inverse * sum_prod / count,
        mean,
        sum_grad,
        sum_prod,
    )


def build_taps(act_ref, shifted_ref, pixels, side):
    pad = 2 * side
    width = act_ref.shape[1]
    column = lax.broadcasted_iota(jnp.int32, (pixels, lane), 0) % side
    for tap_col in range(3):
        move = 2 * (tap_col - 1)
        moved = act_ref[pl.ds(pad + move, pixels), :]
        if move:
            inside = (column + move >= 0) & (column + move < side)
            keep = jnp.concatenate([inside.astype(f32)] * (width // lane), axis=1)
            moved = moved * keep
        shifted_ref[tap_col, pl.ds(0, pad), :] = jnp.zeros((pad, width), bf16)
        shifted_ref[tap_col, pl.ds(pad + pixels, pad), :] = jnp.zeros((pad, width), bf16)
        shifted_ref[tap_col, pl.ds(pad, pixels), :] = moved.astype(bf16)


def tap_of(shifted_ref, tap_index, pixels, side):
    tap_row, tap_col = (tap_index // 3, tap_index % 3)
    return shifted_ref[tap_col, pl.ds(2 * side * tap_row, pixels), :]


def fold_columns(sums_ref, pixels, side):
    pad = 2 * side
    width = sums_ref.shape[2]
    column = lax.broadcasted_iota(jnp.int32, (pixels, lane), 0) % side
    total = sums_ref[1, pl.ds(pad, pixels), :]
    for tap_col in (0, 2):
        move = 2 * (tap_col - 1)
        inside = (column - move >= 0) & (column - move < side)
        keep = jnp.concatenate([inside.astype(f32)] * (width // lane), axis=1)
        total = total + keep * sums_ref[tap_col, pl.ds(pad - move, pixels), :]
    return total


def tap_rows_out(sums_ref, tap_index, pixels, side, values):
    tap_row, tap_col = (tap_index // 3, tap_index % 3)
    rows = pl.ds(2 * side * tap_row, pixels)
    sums_ref[tap_col, rows, :] = sums_ref[tap_col, rows, :] + values


def tap_factors(offsets, tap_index, side):
    pixels = offsets.shape[0]
    tap_row, tap_col = (tap_index // 3, tap_index % 3)
    shape = (pixels, pixels)
    position = lax.broadcasted_iota(jnp.int32, (pixels, 1), 0)
    source = lax.broadcasted_iota(jnp.int32, (1, pixels), 1)
    row_at = (position // side + 2 * (tap_row - 1)).astype(f32) + offsets[:, 2 * tap_index : 2 * tap_index + 1]
    col_at = (position % side + 2 * (tap_col - 1)).astype(f32) + offsets[:, 2 * tap_index + 1 : 2 * tap_index + 2]
    dist_y = jnp.broadcast_to(row_at, shape) - (source // side).astype(f32)
    dist_x = jnp.broadcast_to(col_at, shape) - (source % side).astype(f32)
    bump_y = jnp.maximum(1.0 - dist_y * dist_y, 0.0)
    bump_x = jnp.maximum(1.0 - dist_x * dist_x, 0.0)
    return (dist_y, dist_x, bump_y, bump_x)


def first_body(sizes_ref, place_ref, images_ref, squeeze_ref, pre_ref, mask_ref, copies_ref, half_ref):
    pixels, width = pre_ref.shape
    side = 1 << ((pixels.bit_length() - 1) // 2)
    position = lax.broadcasted_iota(jnp.int32, (pixels, lane), 0)
    inside = (position // side < sizes_ref[0, 0]) & (position % side < sizes_ref[0, 1])
    mask = inside.astype(f32)
    mask_ref[...] = mask
    pre_ref[...] = dot_nn(images_ref[...], squeeze_ref[...])
    flush(pre_ref)

    def both(rows):
        values = pre_ref[rows, :]
        masked = values * wide_mask(mask_ref, rows, width)
        return (masked, masked * values)

    sums = two_sums(pixels, width, both)
    amount = jnp.sum(mask, axis=0, keepdims=True)
    write_copies(copies_ref, sums, jnp.broadcast_to(amount, (8, lane)))
    half = half_ref.shape[1]
    other = pl.multiple_of((1 - place_ref[0, 0]) * half, lane)
    half_ref[...] = images_ref[:, pl.ds(other, half)].astype(f32)


def activate(pre_ref, mask_ref, scale, shift, out_ref, base=0):
    pixels, width = pre_ref.shape

    def step(rows, carry):
        out = silu(pre_ref[rows, :] * scale + shift) * wide_mask(mask_ref, rows, width)
        target = pl.ds(rows.start + base, tile_rows)
        out_ref[target, :] = out.astype(bf16).astype(out_ref.dtype)
        return carry

    row_loop(pixels, step, 0)


def masked_sums(values_ref, mask_ref):
    pixels, width = values_ref.shape

    def both(rows):
        values = values_ref[rows, :]
        masked = values * wide_mask(mask_ref, rows, width)
        return (masked, masked * values)

    return two_sums(pixels, width, both)


def deform_body(
    total_ref, pre_ref, mask_ref, gain_ref, bias_ref, weights_ref, move_ref, spatial_ref,
    act_ref, wide_ref, columns_ref, offsets_ref, second_ref, copies_ref, stats_ref,
    count_ref, padded_ref, shifted_ref,
):
    pixels, width = pre_ref.shape
    side = 1 << ((pixels.bit_length() - 1) // 2)
    total = read_copies(total_ref)
    count = total[2 * width // lane : 2 * width // lane + 1, 0:1]
    count_ref[...] = jnp.broadcast_to(count, (8, lane))
    mean, var = moments(total, width, count)
    stats_ref[...] = jnp.concatenate([mean, var], axis=0)
    scale, shift = scale_shift(mean, var, gain_ref[:, :width], bias_ref[:, :width])
    padded_ref[...] = jnp.zeros_like(padded_ref)
    activate(pre_ref, mask_ref, scale, shift, padded_ref, 2 * side)
    wide_ref[...] = padded_ref[pl.ds(2 * side, pixels), :]
    flush(wide_ref)
    act_ref[...] = wide_ref[...].astype(bf16)
    build_taps(padded_ref, shifted_ref, pixels, side)
    flush(act_ref)
    offsets = move_ref[...]
    need(weights_ref)
    for tap_index in range(9):
        taps = tap_of(shifted_ref, tap_index, pixels, side)
        offsets = offsets + dot_nn(taps, weights_ref[tap_index])
    offsets_ref[...] = offsets
    flush(offsets_ref)
    need(spatial_ref)
    second_ref[...] = jnp.zeros_like(second_ref)
    for tap_index in range(9):
        dist_y, dist_x, bump_y, bump_x = tap_factors(offsets, tap_index, side)
        root = bump_y * bump_x
        columns = dot_nn((root * root).astype(bf16), act_ref[...]).astype(bf16)
        span = pl.ds(tap_index * width, width)
        columns_ref[:, span] = columns
        flush(columns_ref, tap_index)
        second_ref[...] = second_ref[...] + dot_nn(columns, spatial_ref[tap_index])
    flush(second_ref)
    write_copies(copies_ref, masked_sums(second_ref, mask_ref))


def columns_body(act_ref, offsets_ref, columns_ref, low_ref):
    pixels, width = act_ref.shape
    side = 1 << ((pixels.bit_length() - 1) // 2)
    low_ref[...] = act_ref[...].astype(bf16)
    offsets = offsets_ref[...]
    for tap_index in range(9):
        _, _, bump_y, bump_x = tap_factors(offsets, tap_index, side)
        root = bump_y * bump_x
        span = pl.ds(tap_index * width, width)
        columns_ref[:, span] = dot_nn((root * root).astype(bf16), low_ref[...]).astype(bf16)


def plain_body(
    total_ref, pre_ref, mask_ref, count_ref, gain_ref, bias_ref, spatial_ref,
    wide_ref, second_ref, copies_ref, stats_ref,
    padded_ref, shifted_ref,
):
    pixels, width = pre_ref.shape
    side = 1 << ((pixels.bit_length() - 1) // 2)
    total = read_copies(total_ref)
    mean, var = moments(total, width, count_ref[0:1, 0:1])
    stats_ref[...] = jnp.concatenate([mean, var], axis=0)
    scale, shift = scale_shift(mean, var, gain_ref[:, :width], bias_ref[:, :width])
    padded_ref[...] = jnp.zeros_like(padded_ref)
    activate(pre_ref, mask_ref, scale, shift, padded_ref, 2 * side)
    wide_ref[...] = padded_ref[pl.ds(2 * side, pixels), :]
    flush(wide_ref)
    build_taps(padded_ref, shifted_ref, pixels, side)
    need(spatial_ref)
    second_ref[...] = jnp.zeros_like(second_ref)
    for tap_index in range(9):
        taps = tap_of(shifted_ref, tap_index, pixels, side)
        second_ref[...] = second_ref[...] + dot_nn(taps, spatial_ref[tap_index])
    flush(second_ref)
    write_copies(copies_ref, masked_sums(second_ref, mask_ref))


def third_body(
    total_ref, pre_ref, mask_ref, count_ref, gain_ref, bias_ref, expand_ref,
    act_ref, wide_ref, third_ref, copies_ref, stats_ref,
):
    pixels, width = pre_ref.shape
    channels = third_ref.shape[1]
    total = read_copies(total_ref)
    mean, var = moments(total, width, count_ref[0:1, 0:1])
    stats_ref[...] = jnp.concatenate([mean, var], axis=0)
    scale, shift = scale_shift(
        mean, var, gain_ref[:, width : 2 * width], bias_ref[:, width : 2 * width]
    )
    activate(pre_ref, mask_ref, scale, shift, act_ref)
    wide_ref[...] = act_ref[...].astype(f32)
    flush(act_ref)
    flush(wide_ref)
    sums, squares = ([], [])
    for part, (start, size) in enumerate(spans_of(channels, 512)):
        need(expand_ref, part)
        block = dot_nn(act_ref[...], expand_ref[:, start : start + size])
        third_ref[:, start : start + size] = block
        flush(third_ref, part)
        sums.append(jnp.sum(block, axis=0, keepdims=True))
        squares.append(jnp.sum(block * block, axis=0, keepdims=True))
    flush(third_ref)
    write_copies(copies_ref, sums + squares)


def between_body(
    total_ref, pre_ref, images_ref, mask_ref, count_ref, place_ref, gain_ref, bias_ref, squeeze_ref,
    summed_ref, low_ref, half_ref, first_ref, copies_ref, stats_ref,
):
    pixels, channels = pre_ref.shape
    total = read_copies(total_ref)
    mean, var = moments(total, channels, count_ref[0:1, 0:1])
    stats_ref[...] = jnp.concatenate([mean, var], axis=0)
    begin = gain_ref.shape[1] - channels
    scale, shift = scale_shift(mean, var, gain_ref[:, begin:], bias_ref[:, begin:])
    for part, (start, size) in enumerate(spans_of(channels, 512)):
        span = pl.ds(start, size)
        need(pre_ref, part)
        need(images_ref, part)

        def step(rows, carry):
            summed = (
                pre_ref[rows, span] * scale[:, start : start + size]
                + shift[:, start : start + size]
                + images_ref[rows, span].astype(f32)
            )
            summed_ref[rows, span] = summed
            low_ref[rows, span] = (silu(summed) * wide_mask(mask_ref, rows, size)).astype(bf16)
            return carry

        row_loop(pixels, step, 0)
        flush(summed_ref, part)
        flush(low_ref, part)
    flush(summed_ref)
    flush(low_ref)
    need(squeeze_ref)
    sums, squares = ([], [])
    for start, size in spans_of(first_ref.shape[1], 256):
        block = dot_nn(low_ref[...], squeeze_ref[:, start : start + size])
        first_ref[:, start : start + size] = block
        sums.append(jnp.sum(block, axis=0, keepdims=True))
        squares.append(jnp.sum(block * block, axis=0, keepdims=True))
    flush(first_ref)
    write_copies(copies_ref, sums + squares)
    half = half_ref.shape[1]
    other = pl.multiple_of((1 - place_ref[0, 0]) * half, lane)
    half_ref[...] = low_ref[:, pl.ds(other, half)].astype(f32)


def turn_body(
    total_ref, pre_ref, before_ref, grad_ref, mask_ref, count_ref, gain_ref, bias_ref,
    image_ref, grad_sum_ref, copies_ref, stats_ref,
):
    pixels, channels = pre_ref.shape
    total = read_copies(total_ref)
    mean, var = moments(total, channels, count_ref[0:1, 0:1])
    stats_ref[...] = jnp.concatenate([mean, var], axis=0)
    begin = gain_ref.shape[1] - channels
    scale, shift = scale_shift(mean, var, gain_ref[:, begin:], bias_ref[:, begin:])
    inverse = lax.rsqrt(var + eps_norm)
    sums, prods = ([], [])
    for part, (start, size) in enumerate(spans_of(channels, 512)):
        span = pl.ds(start, size)
        cut = slice(start, start + size)
        for ref in (pre_ref, before_ref, grad_ref):
            need(ref, part)

        def both(rows):
            mask = wide_mask(mask_ref, rows, size)
            pre = pre_ref[rows, span]
            summed = pre * scale[:, cut] + shift[:, cut] + silu(before_ref[rows, span]) * mask
            gate = logistic(summed)
            image_ref[rows, span] = (summed * gate * mask).astype(bf16)
            slope = gate * (1.0 + summed * (1.0 - gate))
            grad = grad_ref[rows, span].astype(f32) * mask * slope
            grad_sum_ref[rows, span] = grad
            return (grad, grad * ((pre - mean[:, cut]) * inverse[:, cut]))

        total_grad, total_prod = two_sums(pixels, size, both)
        sums.append(total_grad)
        prods.append(total_prod)
        flush(image_ref, part)
        flush(grad_sum_ref, part)
    write_copies(copies_ref, sums + prods)


def low_gradient(rows, width, start, grad, pre, mask, coefs):
    cut = slice(start, start + width)
    scale, mean_grad, mean_prod, mean = (part[:, cut] for part in coefs[:4])
    return scale * (grad - mask * (mean_grad + (pre - mean) * mean_prod))


def back_third_body(
    total_ref, grad_sum_ref, pre_ref, stats_ref, second_ref, second_stats_ref, mask_ref, count_ref,
    place_ref, gain_ref, bias_ref, expand_ref,
    low_ref, half_ref, grad_ref, copies_ref, result_ref,
):
    pixels, channels = pre_ref.shape
    width = second_ref.shape[1]
    total = read_copies(total_ref)
    coefs = grad_rows(
        total, stats_ref[...], gain_ref[:, 2 * width :], count_ref[0:1, 0:1], channels
    )
    result_ref[...] = jnp.concatenate(coefs[4:6], axis=0)
    for part, (start, size) in enumerate(spans_of(channels, 512)):
        span = pl.ds(start, size)
        need(grad_sum_ref, part)
        need(pre_ref, part)

        def step(rows, carry):
            mask = wide_mask(mask_ref, rows, size)
            low_ref[rows, span] = low_gradient(
                rows, size, start, grad_sum_ref[rows, span], pre_ref[rows, span], mask, coefs
            ).astype(bf16)
            return carry

        row_loop(pixels, step, 0)
        flush(low_ref, part)
    half = half_ref.shape[1]
    other = pl.multiple_of((1 - place_ref[0, 0]) * half, lane)
    half_ref[...] = low_ref[:, pl.ds(other, half)].astype(f32)
    flush(low_ref)
    flush(half_ref)
    for ref in (expand_ref, second_ref, second_stats_ref):
        need(ref)
    for start, size in spans_of(width, 256):
        grad_ref[:, start : start + size] = dot_nt(low_ref[...], expand_ref[start : start + size, :])
    norm_two_slope(grad_ref, second_ref, second_stats_ref, mask_ref, gain_ref, bias_ref, width, copies_ref)


def norm_two_slope(grad_ref, pre_ref, stats_ref, mask_ref, gain_ref, bias_ref, begin, copies_ref):
    pixels, width = pre_ref.shape
    mean, var = (stats_ref[0:1, :], stats_ref[1:2, :])
    inverse = lax.rsqrt(var + eps_norm)
    scale, shift = scale_shift(
        mean, var, gain_ref[:, begin : begin + width], bias_ref[:, begin : begin + width]
    )

    def both(rows):
        pre = pre_ref[rows, :]
        slope = silu_slope(pre * scale + shift)
        grad = grad_ref[rows, :] * slope * wide_mask(mask_ref, rows, width)
        grad_ref[rows, :] = grad
        return (grad, grad * ((pre - mean) * inverse))

    write_copies(copies_ref, two_sums(pixels, width, both))


def low_second(total_ref, grad_ref, pre_ref, stats_ref, mask_ref, count_ref, gain, low_ref, result_ref):
    pixels, width = pre_ref.shape
    total = read_copies(total_ref)
    coefs = grad_rows(total, stats_ref[...], gain, count_ref[0:1, 0:1], width)
    result_ref[...] = jnp.concatenate(coefs[4:6], axis=0)

    def step(rows, carry):
        mask = wide_mask(mask_ref, rows, width)
        low_ref[rows, :] = low_gradient(
            rows, width, 0, grad_ref[rows, :], pre_ref[rows, :], mask, coefs
        ).astype(bf16)
        return carry

    row_loop(pixels, step, 0)


def back_plain_body(
    total_ref, grad_in_ref, second_ref, second_stats_ref, first_ref, first_stats_ref, mask_ref,
    count_ref, place_ref, gain_ref, bias_ref, spatial_ref,
    low_ref, half_ref, grad_ref, copies_ref, result_ref,
    sums_ref,
):
    pixels, width = second_ref.shape
    side = 1 << ((pixels.bit_length() - 1) // 2)
    low_second(
        total_ref, grad_in_ref, second_ref, second_stats_ref, mask_ref, count_ref,
        gain_ref[:, width : 2 * width], low_ref, result_ref,
    )
    half = half_ref.shape[1]
    other = pl.multiple_of((1 - place_ref[0, 0]) * half, lane)
    half_ref[...] = low_ref[:, pl.ds(other, half)].astype(f32)
    flush(low_ref)
    flush(half_ref)
    need(spatial_ref)
    sums_ref[...] = jnp.zeros_like(sums_ref)
    for tap_index in range(9):
        tap_rows_out(
            sums_ref, tap_index, pixels, side, dot_nt(low_ref[...], spatial_ref[tap_index])
        )
    grad_ref[...] = fold_columns(sums_ref, pixels, side)
    norm_two_slope(grad_ref, first_ref, first_stats_ref, mask_ref, gain_ref, bias_ref, 0, copies_ref)


def back_deform_body(
    total_ref, grad_in_ref, second_ref, second_stats_ref, first_ref, first_stats_ref, mask_ref,
    count_ref, place_ref, gain_ref, bias_ref, spatial_ref, act_ref, offsets_ref, weights_ref,
    low_ref, half_ref, grad_ref, copies_ref, result_ref, grad_offsets_ref,
    sums_ref, padded_ref, shifted_ref,
):
    pixels, width = second_ref.shape
    side = 1 << ((pixels.bit_length() - 1) // 2)
    low_second(
        total_ref, grad_in_ref, second_ref, second_stats_ref, mask_ref, count_ref,
        gain_ref[:, width : 2 * width], low_ref, result_ref,
    )
    half = half_ref.shape[1]
    other = pl.multiple_of((1 - place_ref[0, 0]) * half, lane)
    half_ref[...] = low_ref[:, pl.ds(other, half)].astype(f32)
    flush(low_ref)
    flush(half_ref)
    for ref in (first_ref, first_stats_ref, spatial_ref, act_ref, offsets_ref, weights_ref):
        need(ref)
    offsets = offsets_ref[...]
    outs = offsets.shape[1]
    channel = lax.broadcasted_iota(jnp.int32, (pixels, outs), 1)
    moved = jnp.zeros((pixels, outs), f32)
    grad_ref[...] = jnp.zeros_like(grad_ref)
    for tap_index in range(9):
        dist_y, dist_x, bump_y, bump_x = tap_factors(offsets, tap_index, side)
        weight_y, weight_x = (bump_y * bump_y, bump_x * bump_x)
        sampling = (weight_y * weight_x).astype(bf16)
        piece = dot_nt(low_ref[...], spatial_ref[tap_index]).astype(bf16)
        grad_ref[...] = grad_ref[...] + dot_tn(sampling, piece)
        product = -4.0 * dot_nt(piece, act_ref[...])
        along_y = jnp.sum(product * (dist_y * bump_y * weight_x), axis=1, keepdims=True)
        along_x = jnp.sum(product * (dist_x * bump_x * weight_y), axis=1, keepdims=True)
        moved = moved + jnp.where(channel == 2 * tap_index, along_y, 0.0)
        moved = moved + jnp.where(channel == 2 * tap_index + 1, along_x, 0.0)
    moved_low = moved.astype(bf16)
    padded_ref[...] = jnp.zeros_like(padded_ref)
    padded_ref[pl.ds(2 * side, pixels), :] = act_ref[...].astype(f32)
    build_taps(padded_ref, shifted_ref, pixels, side)
    sums_ref[...] = jnp.zeros_like(sums_ref)
    grad_offsets_ref[...] = jnp.zeros_like(grad_offsets_ref)
    for tap_index in range(9):
        taps = tap_of(shifted_ref, tap_index, pixels, side)
        first = tap_index * outs
        grad_offsets_ref[first : first + outs, :] = dot_tn(moved_low, taps)
        tap_rows_out(
            sums_ref, tap_index, pixels, side, dot_nt(moved_low, weights_ref[tap_index])
        )
    grad_ref[...] = grad_ref[...] + fold_columns(sums_ref, pixels, side)
    norm_two_slope(grad_ref, first_ref, first_stats_ref, mask_ref, gain_ref, bias_ref, 0, copies_ref)


def back_between_body(
    total_ref, grad_ref, first_ref, first_stats_ref, grad_sum_ref, summed_ref, pre_ref, stats_ref,
    mask_ref, count_ref, gain_ref, squeeze_ref,
    low_ref, wide_ref, next_ref, copies_ref, result_ref,
):
    pixels, width = first_ref.shape
    channels = pre_ref.shape[1]
    low_second(
        total_ref, grad_ref, first_ref, first_stats_ref, mask_ref, count_ref,
        gain_ref[:, :width], low_ref, result_ref,
    )
    wide_ref[...] = low_ref[...].astype(f32)
    flush(low_ref)
    flush(wide_ref)
    need(stats_ref)
    need(squeeze_ref)
    mean, var = (stats_ref[0:1, :], stats_ref[1:2, :])
    inverse = lax.rsqrt(var + eps_norm)
    sums, prods = ([], [])
    for part, (start, size) in enumerate(spans_of(channels, 512)):
        span = pl.ds(start, size)
        cut = slice(start, start + size)
        for ref in (grad_sum_ref, summed_ref, pre_ref):
            need(ref, part)
        next_ref[:, span] = dot_nt(low_ref[...], squeeze_ref[start : start + size, :])

        def both(rows):
            mask = wide_mask(mask_ref, rows, size)
            slope = silu_slope(summed_ref[rows, span])
            grad = (next_ref[rows, span] + grad_sum_ref[rows, span]) * mask * slope
            next_ref[rows, span] = grad
            return (grad, grad * ((pre_ref[rows, span] - mean[:, cut]) * inverse[:, cut]))

        total_grad, total_prod = two_sums(pixels, size, both)
        sums.append(total_grad)
        prods.append(total_prod)
        flush(next_ref, part)
    write_copies(copies_ref, sums + prods)


def last_low_body(
    total_ref, grad_ref, first_ref, first_stats_ref, mask_ref, count_ref, gain_ref,
    low_ref, wide_ref, result_ref,
):
    width = first_ref.shape[1]
    low_second(
        total_ref, grad_ref, first_ref, first_stats_ref, mask_ref, count_ref,
        gain_ref[:, :width], low_ref, result_ref,
    )
    wide_ref[...] = low_ref[...].astype(f32)


def last_body(low_ref, grad_sum_ref, squeeze_ref, image_ref, token_ref):
    token_ref[...] = jnp.zeros_like(token_ref)
    for start, size in spans_of(image_ref.shape[1], 256):
        block = dot_nt(low_ref[...], squeeze_ref[start : start + size, :])
        image_ref[:, start : start + size] = (
            block + grad_sum_ref[:, start : start + size]
        ).astype(bf16)


def sum_copies_body(copies_ref, out_ref):
    total = jnp.sum(copies_ref[...], axis=0)

    def one_copy(step, carry):
        out_ref[step] = total
        return carry

    lax.fori_loop(0, out_ref.shape[0], one_copy, 0)


def offsets_body(sums_ref, out_ref, token_ref):
    token_ref[...] = jnp.zeros_like(token_ref)
    outs = out_ref.shape[1]
    for tap in range(out_ref.shape[0]):
        out_ref[tap] = sums_ref[tap * outs : (tap + 1) * outs, :]


block_cols = 256


def split_chunks(scratch_ref, keep_ref, send_ref, own, place, spot):
    for index in range(keep_ref.shape[0]):
        low = index & ((1 << place) - 1)
        base = ((index >> place) << (place + 1)) | low
        keep_ref[index, spot] = scratch_ref[base + own * (1 << place)]
        send_ref[index, spot] = scratch_ref[base + (1 - own) * (1 << place)]


def weights_body(kinds, firsts, spans, own_place_ref, *refs):
    groups = [refs[4 * place : 4 * place + 4] for place in range(len(kinds))]
    rest = refs[4 * len(kinds) :]
    results = 2 * len(spans) if firsts else 1
    outs, token_ref = (rest[:results], rest[results])
    chunks_ref, scratch = (rest[results + 1], list(rest[results + 2 :]))
    token_ref[...] = jnp.zeros_like(token_ref)
    count, depth, _ = chunks_ref.shape
    makers = []
    for kind, (rows_ref, rows_other_ref, cols_ref, cols_other_ref) in zip(kinds, groups):
        for ref in (rows_ref, rows_other_ref, cols_ref, cols_other_ref):
            need(ref)
        pixels, half = cols_other_ref.shape
        side = 1 << ((pixels.bit_length() - 1) // 2)
        both_cols = scratch.pop(0)
        start_own = pl.multiple_of(own_place_ref[0, 0] * half, lane)
        both_cols[pl.ds(0, pixels), :] = cols_ref[:, pl.ds(start_own, half)]
        both_cols[pl.ds(pixels, pixels), :] = cols_other_ref[...].astype(bf16)
        if kind == "rows":
            both_rows = scratch.pop(0)
            both_rows[pl.ds(0, pixels), :] = rows_ref[...]
            both_rows[pl.ds(pixels, pixels), :] = rows_other_ref[...].astype(bf16)
            for start in range(0, half, block_cols):
                makers.append(
                    lambda rows=both_rows, cols=both_cols, start=start: dot_tn(
                        rows[...], cols[:, start : start + block_cols]
                    )
                )
        elif kind == "plain":
            padded, taps = (scratch.pop(0), (scratch.pop(0), scratch.pop(0)))
            for source, shifted in zip((rows_ref, rows_other_ref), taps):
                padded[...] = jnp.zeros_like(padded)
                padded[pl.ds(2 * side, pixels), :] = source[...]
                build_taps(padded, shifted, pixels, side)
            for tap in range(9):
                makers.append(
                    lambda taps=taps, cols=both_cols, tap=tap, pixels=pixels, side=side: dot_tn(
                        tap_of(taps[0], tap, pixels, side), cols[pl.ds(0, pixels), :]
                    )
                    + dot_tn(tap_of(taps[1], tap, pixels, side), cols[pl.ds(pixels, pixels), :])
                )
        else:
            width = cols_ref.shape[1]
            for tap in range(9):
                span = slice(tap * width, (tap + 1) * width)
                makers.append(
                    lambda one=rows_ref, two=rows_other_ref, cols=both_cols, span=span, pixels=pixels: dot_tn(
                        one[:, span], cols[pl.ds(0, pixels), :]
                    )
                    + dot_tn(two[:, span], cols[pl.ds(pixels, pixels), :])
                )
    if not firsts:
        for part, maker in enumerate(makers):
            outs[0][:, part] = maker().reshape(count, depth, block_cols)
        return
    for stream, (start, stop) in enumerate(spans):
        bit = firsts[stream]
        own = own_place_ref[0, bit]
        for part in range(start, stop):
            chunks_ref[...] = makers[part]().reshape(count, depth, block_cols)
            split_chunks(
                chunks_ref, outs[2 * stream], outs[2 * stream + 1], own, bit - 1, part - start
            )
        flush(outs[2 * stream + 1])
        flush(outs[2 * stream])


def advance_body(groups, own_place_ref, *refs):
    streams = sum(count for count, _ in groups)
    kept, came = (refs[:streams], refs[streams : 2 * streams])
    outs = list(refs[2 * streams :])
    token_ref = outs.pop()
    token_ref[...] = jnp.zeros_like(token_ref)
    at, used, start = (0, 0, 0)
    for count, spot in groups:
        members = list(range(at, at + count))
        at += count
        for stream in members:
            need(kept[stream])
            need(came[stream])
        if spot is None:
            for stream in members:
                stop = start + kept[stream].shape[1]
                outs[-1][start:stop] = kept[stream][0] + came[stream][0]
                start = stop
            continue
        bit, place = spot
        own = own_place_ref[0, bit]
        for target_ref, side in ((outs[used + 1], 1 - own), (outs[used], own)):
            first = 0
            for stream in members:
                stop = first + kept[stream].shape[1]
                for index in range(target_ref.shape[0]):
                    low = index & ((1 << place) - 1)
                    base = ((index >> place) << (place + 1)) | low
                    chunk = base + side * (1 << place)
                    target_ref[index, first:stop] = kept[stream][chunk] + came[stream][chunk]
                first = stop
            flush(target_ref)
        used += 2


def assemble_body(kinds, labels, summed, own_place_ref, own_ref, pair_ref, side_ref, both_ref, *targets):
    targets[-1][...] = jnp.zeros_like(targets[-1])
    targets = targets[:-1]
    rows, cols = own_ref.shape[-2:]
    pair, line = (own_place_ref[0, 0], own_place_ref[0, 1])
    for row_at, col_at in ((0, 0), (0, 1), (1, 0), (1, 1)):
        if summed and row_at:
            continue
        same_row, same_col = (line == row_at, pair == col_at)
        row_span = slice(row_at * rows, (row_at + 1) * rows)
        for part, (place, step) in enumerate(labels):
            near = jnp.where(same_col, own_ref[part], pair_ref[part])
            far = jnp.where(same_col, side_ref[part], both_ref[part])
            value = near + far if summed else jnp.where(same_row, near, far)
            target = targets[place]
            if kinds[place] == "rows":
                parts = target.shape[1] // 2 // cols
                at = (col_at * parts + step) * cols
                target[row_span, at : at + cols] = value
            else:
                target[step, row_span, col_at * cols : (col_at + 1) * cols] = value
    for target in targets:
        flush(target)


def gate_body(*refs):
    pass


def gate(arrays, after):
    hbm = pl.BlockSpec(memory_space=pltpu.HBM)
    return pl.pallas_call(
        gate_body,
        out_shape=tuple(shape_of(part.shape) for part in arrays),
        in_specs=[hbm] * len(arrays) + [pl.BlockSpec(memory_space=pl.ANY)] * len(after),
        out_specs=(hbm,) * len(arrays),
        input_output_aliases={place: place for place in range(len(arrays))},
    )(*arrays, *after)


class Comm:
    def __init__(self, wide_size, narrow_size):
        self.total = wide_size * narrow_size
        self.bits = self.total.bit_length() - 1
        self.low = narrow_size.bit_length() - 1
        self.index = lax.axis_index("wide") * narrow_size + lax.axis_index("narrow")
        self.places = jnp.stack([self.bit(place) for place in range(self.bits)])[None, :]

    def bit(self, place):
        return (self.index >> place) & 1

    def swap_over(self, values, flips):
        pairs = [(source, source ^ flips) for source in range(self.total)]
        return lax.ppermute(values, axes, pairs)

    def swap(self, values, place):
        return self.swap_over(values, 1 << place)

    def sync(self, copies):
        return Near(lax.all_to_all(copies, axes, 0, 0, tiled=True))

    def order(self, letters):
        named = {"y": 1, "x": self.low, "a": self.low + 1, "b": self.low + 2}
        return [named[letter] for letter in letters] + list(range(self.low + 3, self.bits))


token = (8, lane)


class Group:
    def __init__(self, comm, total, plan):
        self.comm = comm
        self.orders = [comm.order(letters) for letters, _ in plan]
        self.left = [
            [place for place in range(1, comm.bits) if place != order[0]] for order in self.orders
        ]
        shares = [share for _, share in plan]
        ends = [total * sum(shares[: at + 1]) // sum(shares) for at in range(len(plan))]
        self.bounds = tuple(zip([0] + ends[:-1], ends))
        self.total = total
        self.arrays = {}
        self.labels = []
        self.kinds = ()
        self.shapes = []
        self.at = 1

    def add(self, kind, group, after=()):
        comm = self.comm
        pixels, rows = group[0].shape
        if kind == "given":
            rows = group[2].shape[1]
        chunks = 1 << (comm.bits - 1 if self.orders else comm.bits - comm.low)
        depth = rows // chunks
        half = getattr(group[3], "value", group[3]).shape[1]
        side = 1 << ((pixels.bit_length() - 1) // 2)
        scratch = [pltpu.VMEM((chunks, depth, block_cols), f32), pltpu.VMEM((2 * pixels, half), bf16)]
        wide_depth = rows >> (comm.bits - comm.low)
        self.shapes.append((wide_depth, 2 * half) if kind == "rows" else (9, wide_depth, 2 * half))
        if kind == "rows":
            scratch.append(pltpu.VMEM((2 * pixels, rows), bf16))
        if kind == "plain":
            scratch.append(pltpu.VMEM((pixels + 4 * side, rows), f32))
            scratch += [pltpu.VMEM((3, pixels + 4 * side, rows), bf16)] * 2
        count = half // block_cols if kind == "rows" else 9
        begin = len(self.labels)
        self.labels += [(len(self.kinds), step) for step in range(count)]
        self.kinds += (kind,)
        keys, spans, outs, pieces, begun = ([], [], [], {}, {})
        if not self.orders:
            if self.arrays:
                begun[0] = self.arrays[0, 0]
            pieces[0] = (begin, count)
            outs.append(shape_of((chunks, self.total, depth, block_cols)))
        for stream, (start, stop) in enumerate(self.bounds):
            low, high = (max(start, begin), min(stop, begin + count))
            if low >= high:
                continue
            spans.append((low - begin, high - begin))
            keys.append(stream)
            for which in range(2):
                if (stream, which) in self.arrays:
                    begun[len(outs)] = self.arrays[stream, which]
                pieces[len(outs)] = (low - start, high - low)
                outs.append(shape_of((chunks // 2, stop - start, depth, block_cols)))
        args = (comm.places,) + tuple(group)
        made = call(
            functools.partial(
                weights_body, (kind,), tuple(self.orders[stream][0] for stream in keys), tuple(spans)
            ),
            outs + [shape_of(token)], args, (0,), scratch, after, tuple(range(1, len(args))),
            pieces=pieces, begun=begun,
        )
        if not self.orders:
            self.arrays[0, 0] = made[0]
        for number, stream in enumerate(keys):
            self.arrays[stream, 0] = made[2 * number]
            self.arrays[stream, 1] = made[2 * number + 1]
        return made[-1]

    def offload(self):
        self.share = lax.psum_scatter(self.arrays[0, 0], "wide", scatter_dimension=0, tiled=True)

    def collect(self, after):
        (share,) = gate((self.share.reshape(self.share.shape[1:]),), after)
        self.join(share)

    def join(self, share):
        beside = self.comm.swap(share, 1)
        self.quarters = [share, self.comm.swap(share, 0), beside, self.comm.swap(beside, 0)]

    def start(self, after=()):
        sent = [self.arrays[stream, 1] for stream in range(len(self.orders))]
        sent = gate(sent, after) if after else sent
        self.streams = [
            [(self.arrays[stream, 0], self.comm.swap(sent[stream], order[0]))]
            for stream, order in enumerate(self.orders)
        ]

    def advance(self, after=()):
        comm = self.comm
        if len({tuple(order[self.at :]) for order in self.orders}) == 1:
            self.orders, self.left = (self.orders[:1], self.left[:1])
            self.streams = [sum(self.streams, [])]
        groups, outs = ([], [])
        last = self.at == len(self.orders[0])
        total = 0
        for order, left, members in zip(self.orders, self.left, self.streams):
            spot = None
            parts = sum(kept.shape[1] for kept, _ in members)
            shape = members[0][0].shape
            total += parts
            if not last:
                bit = order[self.at]
                spot = (bit, left.index(bit))
                left.remove(bit)
                outs += [shape_of((shape[0] // 2, parts) + shape[2:])] * 2
            groups.append((len(members), spot))
        if last:
            outs = [shape_of((total,) + shape[2:])]
        flat = [pair for members in self.streams for pair in members]
        *pieces, mark = call(
            functools.partial(advance_body, tuple(groups)),
            outs + [shape_of(token)],
            (comm.places, *(kept for kept, _ in flat), *(Near(came) for _, came in flat)),
            (0,), (), after, tuple(range(1, 1 + 2 * len(flat))),
        )
        if last:
            self.join(pieces[0])
        else:
            self.streams = [
                [(pieces[2 * place], comm.swap(pieces[2 * place + 1], order[self.at]))]
                for place, order in enumerate(self.orders)
            ]
        self.at += 1
        return mark

    def ended(self):
        return self.at > len(self.orders[0])

    def finish(self, after=()):
        while self.orders and not self.ended():
            self.advance(after)
        kinds, shapes = (self.kinds, self.shapes)
        outs = [shape_of(shape) for shape in shapes]
        *results, self.token = call(
            functools.partial(assemble_body, kinds, tuple(self.labels), not self.orders),
            outs + [shape_of(token)], (self.comm.places, self.quarters[0], *(Near(part) for part in self.quarters[1:])), (0,), (), after,
        )
        return results


def per_device(
    wide_size, narrow_size, images, image_sizes, offset_shift, squeeze_one, offsets_one, spatial_one,
    expand_one, squeeze_two, spatial_two, expand_two, norm_gain_one, norm_bias_one, norm_gain_two,
    norm_bias_two, run_mean_one, run_var_one, run_mean_two, run_var_two, grad_output,
):
    comm = Comm(wide_size, narrow_size)
    side, channels = (images.shape[1], images.shape[3])
    pixels = side * side
    width = squeeze_one.shape[1]
    outs = offsets_one.shape[2]
    total = comm.total
    small = (total, 2 * width // lane, lane)
    quarters = channels // 512
    large = (total, 2 * channels // lane, lane)
    flat = images.reshape(pixels, channels)
    grad_out = grad_output.reshape(pixels, channels)
    gain_one, bias_one = (norm_gain_one[None, :], norm_bias_one[None, :])
    gain_two, bias_two = (norm_gain_two[None, :], norm_bias_two[None, :])
    field = shape_of((pixels, width))
    field_low = shape_of((pixels, width), bf16)
    plane = shape_of((pixels, channels))
    plane_low = shape_of((pixels, channels), bf16)
    half_plane = shape_of((pixels, channels // 2))
    half_field = shape_of((pixels, width // 2))
    stats_small, stats_large = (shape_of((2, width)), shape_of((2, channels)))
    padded = pltpu.VMEM((pixels + 4 * side, width), f32)
    shifted = pltpu.VMEM((3, pixels + 4 * side, width), bf16)
    tap_sums = pltpu.VMEM((3, pixels + 4 * side, width), f32)

    first_one, mask, copies, images_half = call(
        first_body,
        (field, shape_of((pixels, lane)), shape_of((total, 2 * width // lane + 8, lane)), half_plane),
        (image_sizes, comm.places, flat, squeeze_one),
        (0, 1),
    )
    images_half = comm.swap(images_half, 0)
    copies = comm.sync(copies)
    (act_one, act_wide, columns, offsets, second_one, copies, first_stats_one, count) = call(
        deform_body,
        (
            field_low, field, shape_of((pixels, 9 * width), bf16),
            shape_of((pixels, outs)), field, shape_of(small), stats_small, shape_of((8, lane)),
        ),
        (
            copies, first_one, mask, gain_one, bias_one, offsets_one,
            offset_shift.astype(f32)[None, :], spatial_one,
        ),
        (),
        (padded, shifted),
        (),
        (5, 7), blocks_out={2: 9},
    )
    act_other, offsets_other = (comm.swap(act_wide, 0), comm.swap(offsets, 0))
    copies = comm.sync(copies)
    act_second_one, act_second_wide_one, third_one, copies, second_stats_one = call(
        third_body,
        (field_low, field, plane, shape_of(large), stats_small),
        (copies, second_one, mask, count, gain_one, bias_one, expand_one),
        blocks={6: quarters}, blocks_out={2: quarters},
    )
    (columns_other,) = call(
        columns_body, (shape_of((pixels, 9 * width), bf16),),
        (Near(act_other), Near(offsets_other)), (), (pltpu.VMEM((pixels, width), bf16),), (second_stats_one,),
    )
    act_second_wide_one = comm.swap(act_second_wide_one, 0)
    copies = comm.sync(copies)
    summed_one, low_two, low_half, first_two, copies, third_stats_one = call(
        between_body,
        (plane, plane_low, half_plane, field, shape_of(small), stats_large),
        (copies, third_one, flat, mask, count, comm.places, gain_one, bias_one, squeeze_two),
        (5,), (), (columns_other,), (8,),
        blocks={1: quarters, 2: quarters}, blocks_out={0: quarters, 1: quarters},
    )
    low_half = comm.swap(low_half, 0)
    copies = comm.sync(copies)
    act_wide_two, second_two, copies, first_stats_two = call(
        plain_body,
        (field, field, shape_of(small), stats_small),
        (copies, first_two, mask, count, gain_two, bias_two, spatial_two),
        (),
        (padded, shifted), late=(6,),
    )
    act_wide_two_other = comm.swap(act_wide_two, 0)
    copies = comm.sync(copies)
    act_second_two, act_second_wide_two, third_two, copies, second_stats_two = call(
        third_body,
        (field_low, field, plane, shape_of(large), stats_small),
        (copies, second_two, mask, count, gain_two, bias_two, expand_two),
        blocks={6: quarters}, blocks_out={2: quarters},
    )
    act_second_wide_two = comm.swap(act_second_wide_two, 0)
    copies = comm.sync(copies)
    output_images, grad_sum_two, copies, third_stats_two = call(
        turn_body,
        (plane_low, plane, shape_of(large), stats_large),
        (copies, third_two, summed_one, grad_out, mask, count, gain_two, bias_two),
        blocks={1: quarters, 2: quarters, 3: quarters}, blocks_out={0: quarters, 1: quarters},
    )
    copies = comm.sync(copies)
    low_third_two, third_half, grad_second_two, copies, third_result_two = call(
        back_third_body,
        (plane_low, half_plane, field, shape_of(small), stats_large),
        (
            copies, grad_sum_two, third_two, third_stats_two, second_two, second_stats_two, mask, count,
            comm.places, gain_two, bias_two, expand_two,
        ),
        (8,), late=(4, 5, 11), blocks={1: quarters, 2: quarters}, blocks_out={0: quarters},
    )
    third_half = comm.swap(third_half, 0)
    copies = comm.sync(copies)
    blocks = channels // 2 // block_cols
    plan = (("xyab", 6), ("yaxb", 6), ("axyb", 5))
    group_two = Group(comm, 2 * blocks + 9, plan)
    group_one = Group(comm, 2 * blocks + 9, (("xayb", 7), ("yxab", 7), ("ayxb", 3)))
    done = group_two.add("rows", (act_second_two, act_second_wide_two, low_third_two, Near(third_half)))
    low_second_two, second_half, grad_first_two, copies, second_result_two = call(
        back_plain_body,
        (field_low, half_field, field, shape_of(small), stats_small),
        (
            copies, grad_second_two, second_two, second_stats_two, first_two, first_stats_two, mask,
            count, comm.places, gain_two, bias_two, spatial_two,
        ),
        (8,),
        (tap_sums,),
        (done,),
        (11,),
    )
    second_half = comm.swap(second_half, 0)
    copies = comm.sync(copies)
    done = group_two.add("plain", (act_wide_two, act_wide_two_other, low_second_two, Near(second_half)))
    low_first_two, low_first_wide, grad_sum_one, copies, first_result_two = call(
        back_between_body,
        (field_low, field, plane, shape_of(large), stats_small),
        (
            copies, grad_first_two, first_two, first_stats_two, grad_sum_two, summed_one, third_one,
            third_stats_one, mask, count, gain_two, squeeze_two,
        ),
        (),
        (),
        (done,),
        (4, 5, 6, 7, 11),
        blocks={4: quarters, 5: quarters, 6: quarters}, blocks_out={2: quarters},
    )
    low_first_wide = comm.swap(low_first_wide, 0)
    copies = comm.sync(copies)
    done = group_two.add("rows", (low_first_two, Near(low_first_wide), low_two, low_half))
    low_third_one, third_half, grad_second_one, copies, third_result_one = call(
        back_third_body,
        (plane_low, half_plane, field, shape_of(small), stats_large),
        (
            copies, grad_sum_one, third_one, third_stats_one, second_one, second_stats_one, mask, count,
            comm.places, gain_one, bias_one, expand_one,
        ),
        (8,),
        (),
        (done,),
        (4, 5, 11),
        blocks={1: quarters, 2: quarters}, blocks_out={0: quarters},
    )
    third_half = comm.swap(third_half, 0)
    copies = comm.sync(copies)
    done = group_one.add("rows", (act_second_one, act_second_wide_one, low_third_one, Near(third_half)))
    group_two.start((copies.value, done))
    slots = -(-9 * outs // total)
    slots = -(-slots // 8) * 8
    low_second_one, second_half, grad_first_one, copies, second_result_one, grad_offsets = call(
        back_deform_body,
        (
            field_low, half_field, field, shape_of(small), stats_small, shape_of((total * slots, width)),
        ),
        (
            copies, grad_second_one, second_one, second_stats_one, first_one, first_stats_one, mask,
            count, comm.places, gain_one, bias_one, spatial_one, act_one, offsets, offsets_one,
        ),
        (8,),
        (tap_sums, padded, shifted),
        (done,),
        (4, 5, 11, 12, 13, 14),
    )
    second_half = comm.swap(second_half, 0)
    copies = comm.sync(copies)
    done = group_one.add("given", (columns, columns_other, low_second_one, Near(second_half)))
    done = group_two.advance((done,))
    low_first_one, low_first_wide, first_result_one = call(
        last_low_body,
        (field_low, field, stats_small),
        (copies, grad_first_one, first_one, first_stats_one, mask, count, gain_one),
        (), (), (done,),
    )
    low_first_wide = comm.swap(low_first_wide, 0)
    grad_offsets = comm.sync(grad_offsets.reshape(total, slots, width))
    done = group_one.add(
        "rows", (low_first_one, Near(low_first_wide), flat, images_half), (first_result_one, done)
    )
    done = group_two.advance((done,))
    grad_images, done = call(
        last_body,
        (plane_low, shape_of(token)),
        (low_first_one, grad_sum_one, squeeze_one),
        (), (), (done,),
    )
    done = group_two.advance((done, grad_offsets.value))
    group_one.start((done,))
    (grad_offsets,) = call(
        sum_copies_body, (shape_of((total, slots, width)),), (grad_offsets,), (), (),
        (done,),
    )
    grad_offsets = comm.sync(grad_offsets).value
    done = group_two.advance((done,))
    done = group_one.advance((done,))
    grad_offsets, done = call(
        offsets_body, (shape_of((9, outs, width)), shape_of(token)),
        (grad_offsets.reshape(total * slots, width),), (), (), (done,),
    )
    done = group_one.advance((done,))
    done = group_one.advance((done,))
    grad_expand_two, grad_spatial_two, grad_squeeze_two = group_two.finish((done,))
    grad_expand_one, grad_spatial_one, grad_squeeze_one = group_one.finish((group_two.token,))

    def laid(parts, row):
        return jnp.concatenate([part[row] for part in parts])

    results_one = (first_result_one, second_result_one, third_result_one)
    results_two = (first_result_two, second_result_two, third_result_two)
    stats_one = (first_stats_one, second_stats_one, third_stats_one)
    stats_two = (first_stats_two, second_stats_two, third_stats_two)
    pixel_count = count[0, 0]
    unbias = pixel_count / (pixel_count - 1.0)
    fresh = 1.0 - keep_rate
    return (
        output_images.reshape(images.shape),
        grad_images.reshape(images.shape),
        grad_squeeze_one.T,
        grad_offsets.transpose(0, 2, 1),
        grad_spatial_one,
        grad_expand_one,
        grad_squeeze_two.T,
        grad_spatial_two,
        grad_expand_two,
        laid(results_one, 1),
        laid(results_one, 0),
        laid(results_two, 1),
        laid(results_two, 0),
        keep_rate * run_mean_one + fresh * laid(stats_one, 0),
        keep_rate * run_var_one + fresh * laid(stats_one, 1) * unbias,
        keep_rate * run_mean_two + fresh * laid(stats_two, 0),
        keep_rate * run_var_two + fresh * laid(stats_two, 1) * unbias,
    )


def solution(mesh):
    images_spec = P(axes, None, None, None)
    whole = P()
    return jax.shard_map(
        functools.partial(per_device, mesh.shape["wide"], mesh.shape["narrow"]),
        mesh=mesh,
        in_specs=(images_spec, P(axes, None)) + (whole,) * 16 + (images_spec,),
        out_specs=(
            images_spec,
            images_spec,
            P(None, "wide"),
            whole,
            P(None, "wide", None),
            P("wide", None),
            P(None, "wide"),
            P(None, "wide", None),
            P("wide", None),
        )
        + (whole,) * 8,
        check_vma=False,
    )
```

```python
import functools

import jax
import jax.numpy as jnp
from jax import lax
from jax.experimental import pallas as pl
from jax.experimental.pallas import tpu as pltpu
from jax.sharding import PartitionSpec as P

eps_norm = 1e-05
keep_rate = 0.6
vmem_bytes = 52 * 1024 * 1024
lane = 128
tile_rows = 16
row_unroll = 2
axes = ("wide", "narrow")
f32 = jnp.float32
bf16 = jnp.bfloat16


def shape_of(shape, kind=f32):
    return jax.ShapeDtypeStruct(shape, kind)


copies_of = {}


def need(ref, part=None):
    entries = copies_of.get(id(ref), [])
    for entry in entries if part is None else entries[part : part + 1]:
        if entry[1]:
            entry[1] = False
            entry[0].wait()
    return ref


def flush(ref, part=None):
    entries = copies_of.get(id(ref), [])
    for entry in entries if part is None else entries[part : part + 1]:
        if entry[1]:
            entry[1] = False
            entry[0].start()


def column_copies(source, target, flags, first, count):
    if count == 1:
        return [[pltpu.make_async_copy(source, target, flags.at[first]), True]]
    width = source.shape[1] // count
    spans = [pl.ds(width * at, width) for at in range(count)]
    return [
        [pltpu.make_async_copy(source.at[:, span], target.at[:, span], flags.at[first + at]), True]
        for at, span in enumerate(spans)
    ]


class Near:
    def __init__(self, value):
        self.value = value


def call(body, outs, args, smem=(), scratch=(), after=(), late=(), stay_out=(), pieces=None, begun=None, blocks=None, blocks_out=None):
    stay = tuple(place for place, arg in enumerate(args) if isinstance(arg, Near))
    args = tuple(arg.value if isinstance(arg, Near) else arg for arg in args)
    pieces = pieces or {}
    begun = begun or {}
    blocks = blocks or {}
    blocks_out = blocks_out or {}
    hbm = pl.BlockSpec(memory_space=pltpu.HBM)
    vmem = pl.BlockSpec(memory_space=pltpu.VMEM)
    specs = [
        pl.BlockSpec(memory_space=pltpu.SMEM) if place in smem else vmem if place in stay else hbm
        for place in range(len(args))
    ] + [pl.BlockSpec(memory_space=pl.ANY)] * len(after) + [hbm] * len(begun)
    moved = [place for place in range(len(args)) if place not in smem and place not in stay]
    used, extra, made = (len(args), len(after) + len(begun), len(outs))
    sent = [slot for slot in range(made) if slot not in stay_out]

    def kernel(*refs):
        given = list(refs[:used])
        results = list(refs[used + extra : used + extra + made])
        rest = refs[used + extra + made :]
        in_slots, out_slots = (rest[: len(moved)], rest[len(moved) : len(moved) + len(sent)])
        in_flags, out_flags = rest[len(moved) + len(sent) : len(moved) + len(sent) + 2]
        copies_of.clear()
        first = 0
        for slot, place in enumerate(moved):
            count = blocks.get(place, 1)
            entries = column_copies(given[place], in_slots[slot], in_flags, first, count)
            first += count
            for entry in entries:
                entry[0].start()
            copies_of[id(in_slots[slot])] = entries
            given[place] = in_slots[slot]
        for place in moved:
            if place not in late and place not in blocks:
                need(given[place])
        first = 0
        for slot, place in enumerate(sent):
            count = blocks_out.get(place, 1)
            target = results[place].at[:, pl.ds(*pieces[place])] if place in pieces else results[place]
            copies_of[id(out_slots[slot])] = column_copies(out_slots[slot], target, out_flags, first, count)
            first += count
            results[place] = out_slots[slot]
        body(*given, *results, *rest[len(moved) + len(sent) + 2 :])
        for place in moved:
            need(given[place])
        for slot in out_slots:
            flush(slot)
        for slot in out_slots:
            for entry in copies_of[id(slot)]:
                entry[0].wait()
        copies_of.clear()

    slots = [pltpu.VMEM(args[place].shape, args[place].dtype) for place in moved]
    for place in sent:
        shape = outs[place].shape
        if place in pieces:
            shape = (shape[0], pieces[place][1]) + shape[2:]
        slots.append(pltpu.VMEM(shape, outs[place].dtype))
    in_count = sum(blocks.get(place, 1) for place in moved)
    out_count = sum(blocks_out.get(place, 1) for place in sent)
    flags = [pltpu.SemaphoreType.DMA((max(in_count, 1),)), pltpu.SemaphoreType.DMA((max(out_count, 1),))]
    return pl.pallas_call(
        kernel,
        input_output_aliases={used + len(after) + at: place for at, place in enumerate(begun)},
        out_shape=tuple(outs),
        in_specs=specs,
        out_specs=tuple(vmem if place in stay_out else hbm for place in range(made)),
        scratch_shapes=slots + flags + list(scratch),
        compiler_params=pltpu.CompilerParams(vmem_limit_bytes=vmem_bytes),
    )(*args, *after, *begun.values())


def dot_nn(first_op, second_op):
    return lax.dot_general(
        first_op, second_op, (((1,), (0,)), ((), ())), preferred_element_type=f32
    )


def dot_nt(first_op, second_op):
    return lax.dot_general(
        first_op, second_op, (((1,), (1,)), ((), ())), preferred_element_type=f32
    )


def dot_tn(first_op, second_op):
    return lax.dot_general(
        first_op, second_op, (((0,), (0,)), ((), ())), preferred_element_type=f32
    )


def logistic(values):
    return 0.5 * jnp.tanh(0.5 * values) + 0.5


def silu(values):
    return values * logistic(values)


def silu_slope(values):
    gate = logistic(values)
    return gate * (1.0 + values * (1.0 - gate))


def flat_row(rows, start, width):
    first = start // lane
    return jnp.concatenate(
        [rows[first + step : first + step + 1, :] for step in range(width // lane)], axis=1
    )


def fold_row(row):
    return [row[:, step * lane : (step + 1) * lane] for step in range(row.shape[1] // lane)]


def write_copies(copies_ref, rows, extra=None):
    packed = jnp.concatenate([piece for row in rows for piece in fold_row(row)], axis=0)
    if extra is not None:
        packed = jnp.concatenate([packed, extra], axis=0)

    def one_copy(step, carry):
        copies_ref[step] = packed
        return carry

    lax.fori_loop(0, copies_ref.shape[0], one_copy, 0)


def read_copies(copies_ref):
    return jnp.sum(copies_ref[...], axis=0)


def wide_mask(mask_ref, rows, width):
    return jnp.concatenate([mask_ref[rows, :]] * (width // lane), axis=1)


def eight_rows(values):
    folded = values[:8]
    for start in range(8, values.shape[0], 8):
        folded = folded + values[start : start + 8]
    return folded


def row_loop(pixels, body, carry):
    def step(index, state):
        return body(pl.ds(pl.multiple_of(index * tile_rows, tile_rows), tile_rows), state)

    return lax.fori_loop(0, pixels // tile_rows, step, carry, unroll=row_unroll)


def two_sums(pixels, width, body):
    zero = jnp.zeros((8, width), f32)

    def step(rows, state):
        first, second = body(rows)
        return (state[0] + eight_rows(first), state[1] + eight_rows(second))

    first, second = row_loop(pixels, step, (zero, zero))
    return (jnp.sum(first, axis=0, keepdims=True), jnp.sum(second, axis=0, keepdims=True))


def moments(total, width, count):
    mean = flat_row(total, 0, width) / count
    var = flat_row(total, width, width) / count - mean * mean
    return (mean, var)


def scale_shift(mean, var, gain, bias):
    inverse = lax.rsqrt(var + eps_norm)
    scale = gain * inverse
    return (scale, bias - mean * scale)


def spans_of(width, block):
    return [(start, min(block, width - start)) for start in range(0, width, block)]


def grad_rows(total, stats, gain, count, width):
    mean, var = (stats[0:1], stats[1:2])
    inverse = lax.rsqrt(var + eps_norm)
    sum_grad = flat_row(total, 0, width)
    sum_prod = flat_row(total, width, width)
    return (
        gain * inverse,
        sum_grad / count,
        inverse * sum_prod / count,
        mean,
        sum_grad,
        sum_prod,
    )


def build_taps(act_ref, shifted_ref, pixels, side):
    pad = 2 * side
    width = act_ref.shape[1]
    column = lax.broadcasted_iota(jnp.int32, (pixels, lane), 0) % side
    for tap_col in range(3):
        move = 2 * (tap_col - 1)
        moved = act_ref[pl.ds(pad + move, pixels), :]
        if move:
            inside = (column + move >= 0) & (column + move < side)
            keep = jnp.concatenate([inside.astype(f32)] * (width // lane), axis=1)
            moved = moved * keep
        shifted_ref[tap_col, pl.ds(0, pad), :] = jnp.zeros((pad, width), bf16)
        shifted_ref[tap_col, pl.ds(pad + pixels, pad), :] = jnp.zeros((pad, width), bf16)
        shifted_ref[tap_col, pl.ds(pad, pixels), :] = moved.astype(bf16)


def tap_of(shifted_ref, tap_index, pixels, side):
    tap_row, tap_col = (tap_index // 3, tap_index % 3)
    return shifted_ref[tap_col, pl.ds(2 * side * tap_row, pixels), :]


def fold_columns(sums_ref, pixels, side):
    pad = 2 * side
    width = sums_ref.shape[2]
    column = lax.broadcasted_iota(jnp.int32, (pixels, lane), 0) % side
    total = sums_ref[1, pl.ds(pad, pixels), :]
    for tap_col in (0, 2):
        move = 2 * (tap_col - 1)
        inside = (column - move >= 0) & (column - move < side)
        keep = jnp.concatenate([inside.astype(f32)] * (width // lane), axis=1)
        total = total + keep * sums_ref[tap_col, pl.ds(pad - move, pixels), :]
    return total


def tap_rows_out(sums_ref, tap_index, pixels, side, values):
    tap_row, tap_col = (tap_index // 3, tap_index % 3)
    rows = pl.ds(2 * side * tap_row, pixels)
    sums_ref[tap_col, rows, :] = sums_ref[tap_col, rows, :] + values


def tap_factors(offsets, tap_index, side):
    pixels = offsets.shape[0]
    tap_row, tap_col = (tap_index // 3, tap_index % 3)
    shape = (pixels, pixels)
    position = lax.broadcasted_iota(jnp.int32, (pixels, 1), 0)
    source = lax.broadcasted_iota(jnp.int32, (1, pixels), 1)
    row_at = (position // side + 2 * (tap_row - 1)).astype(f32) + offsets[:, 2 * tap_index : 2 * tap_index + 1]
    col_at = (position % side + 2 * (tap_col - 1)).astype(f32) + offsets[:, 2 * tap_index + 1 : 2 * tap_index + 2]
    dist_y = jnp.broadcast_to(row_at, shape) - (source // side).astype(f32)
    dist_x = jnp.broadcast_to(col_at, shape) - (source % side).astype(f32)
    bump_y = jnp.maximum(1.0 - dist_y * dist_y, 0.0)
    bump_x = jnp.maximum(1.0 - dist_x * dist_x, 0.0)
    return (dist_y, dist_x, bump_y, bump_x)


def first_body(sizes_ref, place_ref, images_ref, squeeze_ref, pre_ref, mask_ref, copies_ref, half_ref):
    pixels, width = pre_ref.shape
    side = 1 << ((pixels.bit_length() - 1) // 2)
    position = lax.broadcasted_iota(jnp.int32, (pixels, lane), 0)
    inside = (position // side < sizes_ref[0, 0]) & (position % side < sizes_ref[0, 1])
    mask = inside.astype(f32)
    mask_ref[...] = mask
    pre_ref[...] = dot_nn(images_ref[...], squeeze_ref[...])
    flush(pre_ref)

    def both(rows):
        values = pre_ref[rows, :]
        masked = values * wide_mask(mask_ref, rows, width)
        return (masked, masked * values)

    sums = two_sums(pixels, width, both)
    amount = jnp.sum(mask, axis=0, keepdims=True)
    write_copies(copies_ref, sums, jnp.broadcast_to(amount, (8, lane)))
    half = half_ref.shape[1]
    other = pl.multiple_of((1 - place_ref[0, 0]) * half, lane)
    half_ref[...] = images_ref[:, pl.ds(other, half)].astype(f32)


def activate(pre_ref, mask_ref, scale, shift, out_ref, base=0):
    pixels, width = pre_ref.shape

    def step(rows, carry):
        out = silu(pre_ref[rows, :] * scale + shift) * wide_mask(mask_ref, rows, width)
        target = pl.ds(rows.start + base, tile_rows)
        out_ref[target, :] = out.astype(bf16).astype(out_ref.dtype)
        return carry

    row_loop(pixels, step, 0)


def masked_sums(values_ref, mask_ref):
    pixels, width = values_ref.shape

    def both(rows):
        values = values_ref[rows, :]
        masked = values * wide_mask(mask_ref, rows, width)
        return (masked, masked * values)

    return two_sums(pixels, width, both)


def deform_body(
    total_ref, pre_ref, mask_ref, gain_ref, bias_ref, weights_ref, move_ref, spatial_ref,
    act_ref, wide_ref, columns_ref, offsets_ref, second_ref, copies_ref, stats_ref,
    count_ref, padded_ref, shifted_ref,
):
    pixels, width = pre_ref.shape
    side = 1 << ((pixels.bit_length() - 1) // 2)
    total = read_copies(total_ref)
    count = total[2 * width // lane : 2 * width // lane + 1, 0:1]
    count_ref[...] = jnp.broadcast_to(count, (8, lane))
    mean, var = moments(total, width, count)
    stats_ref[...] = jnp.concatenate([mean, var], axis=0)
    scale, shift = scale_shift(mean, var, gain_ref[:, :width], bias_ref[:, :width])
    padded_ref[...] = jnp.zeros_like(padded_ref)
    activate(pre_ref, mask_ref, scale, shift, padded_ref, 2 * side)
    wide_ref[...] = padded_ref[pl.ds(2 * side, pixels), :]
    flush(wide_ref)
    act_ref[...] = wide_ref[...].astype(bf16)
    build_taps(padded_ref, shifted_ref, pixels, side)
    flush(act_ref)
    offsets = move_ref[...]
    need(weights_ref)
    for tap_index in range(9):
        taps = tap_of(shifted_ref, tap_index, pixels, side)
        offsets = offsets + dot_nn(taps, weights_ref[tap_index])
    offsets_ref[...] = offsets
    flush(offsets_ref)
    need(spatial_ref)
    second_ref[...] = jnp.zeros_like(second_ref)
    for tap_index in range(9):
        dist_y, dist_x, bump_y, bump_x = tap_factors(offsets, tap_index, side)
        root = bump_y * bump_x
        columns = dot_nn((root * root).astype(bf16), act_ref[...]).astype(bf16)
        span = pl.ds(tap_index * width, width)
        columns_ref[:, span] = columns
        flush(columns_ref, tap_index)
        second_ref[...] = second_ref[...] + dot_nn(columns, spatial_ref[tap_index])
    flush(second_ref)
    write_copies(copies_ref, masked_sums(second_ref, mask_ref))


def columns_body(act_ref, offsets_ref, columns_ref, low_ref):
    pixels, width = act_ref.shape
    side = 1 << ((pixels.bit_length() - 1) // 2)
    low_ref[...] = act_ref[...].astype(bf16)
    offsets = offsets_ref[...]
    for tap_index in range(9):
        _, _, bump_y, bump_x = tap_factors(offsets, tap_index, side)
        root = bump_y * bump_x
        span = pl.ds(tap_index * width, width)
        columns_ref[:, span] = dot_nn((root * root).astype(bf16), low_ref[...]).astype(bf16)


def plain_body(
    total_ref, pre_ref, mask_ref, count_ref, gain_ref, bias_ref, spatial_ref,
    wide_ref, second_ref, copies_ref, stats_ref,
    padded_ref, shifted_ref,
):
    pixels, width = pre_ref.shape
    side = 1 << ((pixels.bit_length() - 1) // 2)
    total = read_copies(total_ref)
    mean, var = moments(total, width, count_ref[0:1, 0:1])
    stats_ref[...] = jnp.concatenate([mean, var], axis=0)
    scale, shift = scale_shift(mean, var, gain_ref[:, :width], bias_ref[:, :width])
    padded_ref[...] = jnp.zeros_like(padded_ref)
    activate(pre_ref, mask_ref, scale, shift, padded_ref, 2 * side)
    wide_ref[...] = padded_ref[pl.ds(2 * side, pixels), :]
    flush(wide_ref)
    build_taps(padded_ref, shifted_ref, pixels, side)
    need(spatial_ref)
    second_ref[...] = jnp.zeros_like(second_ref)
    for tap_index in range(9):
        taps = tap_of(shifted_ref, tap_index, pixels, side)
        second_ref[...] = second_ref[...] + dot_nn(taps, spatial_ref[tap_index])
    flush(second_ref)
    write_copies(copies_ref, masked_sums(second_ref, mask_ref))


def third_body(
    total_ref, pre_ref, mask_ref, count_ref, gain_ref, bias_ref, expand_ref,
    act_ref, wide_ref, third_ref, copies_ref, stats_ref,
):
    pixels, width = pre_ref.shape
    channels = third_ref.shape[1]
    total = read_copies(total_ref)
    mean, var = moments(total, width, count_ref[0:1, 0:1])
    stats_ref[...] = jnp.concatenate([mean, var], axis=0)
    scale, shift = scale_shift(
        mean, var, gain_ref[:, width : 2 * width], bias_ref[:, width : 2 * width]
    )
    activate(pre_ref, mask_ref, scale, shift, act_ref)
    wide_ref[...] = act_ref[...].astype(f32)
    flush(act_ref)
    flush(wide_ref)
    sums, squares = ([], [])
    for part, (start, size) in enumerate(spans_of(channels, 512)):
        need(expand_ref, part)
        block = dot_nn(act_ref[...], expand_ref[:, start : start + size])
        third_ref[:, start : start + size] = block
        flush(third_ref, part)
        sums.append(jnp.sum(block, axis=0, keepdims=True))
        squares.append(jnp.sum(block * block, axis=0, keepdims=True))
    flush(third_ref)
    write_copies(copies_ref, sums + squares)


def between_body(
    total_ref, pre_ref, images_ref, mask_ref, count_ref, place_ref, gain_ref, bias_ref, squeeze_ref,
    summed_ref, low_ref, half_ref, first_ref, copies_ref, stats_ref,
):
    pixels, channels = pre_ref.shape
    total = read_copies(total_ref)
    mean, var = moments(total, channels, count_ref[0:1, 0:1])
    stats_ref[...] = jnp.concatenate([mean, var], axis=0)
    begin = gain_ref.shape[1] - channels
    scale, shift = scale_shift(mean, var, gain_ref[:, begin:], bias_ref[:, begin:])
    for part, (start, size) in enumerate(spans_of(channels, 512)):
        span = pl.ds(start, size)
        need(pre_ref, part)
        need(images_ref, part)

        def step(rows, carry):
            summed = (
                pre_ref[rows, span] * scale[:, start : start + size]
                + shift[:, start : start + size]
                + images_ref[rows, span].astype(f32)
            )
            summed_ref[rows, span] = summed
            low_ref[rows, span] = (silu(summed) * wide_mask(mask_ref, rows, size)).astype(bf16)
            return carry

        row_loop(pixels, step, 0)
        flush(summed_ref, part)
        flush(low_ref, part)
    flush(summed_ref)
    flush(low_ref)
    need(squeeze_ref)
    sums, squares = ([], [])
    for start, size in spans_of(first_ref.shape[1], 256):
        block = dot_nn(low_ref[...], squeeze_ref[:, start : start + size])
        first_ref[:, start : start + size] = block
        sums.append(jnp.sum(block, axis=0, keepdims=True))
        squares.append(jnp.sum(block * block, axis=0, keepdims=True))
    flush(first_ref)
    write_copies(copies_ref, sums + squares)
    half = half_ref.shape[1]
    other = pl.multiple_of((1 - place_ref[0, 0]) * half, lane)
    half_ref[...] = low_ref[:, pl.ds(other, half)].astype(f32)


def turn_body(
    total_ref, pre_ref, before_ref, grad_ref, mask_ref, count_ref, gain_ref, bias_ref,
    image_ref, grad_sum_ref, copies_ref, stats_ref,
):
    pixels, channels = pre_ref.shape
    total = read_copies(total_ref)
    mean, var = moments(total, channels, count_ref[0:1, 0:1])
    stats_ref[...] = jnp.concatenate([mean, var], axis=0)
    begin = gain_ref.shape[1] - channels
    scale, shift = scale_shift(mean, var, gain_ref[:, begin:], bias_ref[:, begin:])
    inverse = lax.rsqrt(var + eps_norm)
    sums, prods = ([], [])
    for part, (start, size) in enumerate(spans_of(channels, 512)):
        span = pl.ds(start, size)
        cut = slice(start, start + size)
        for ref in (pre_ref, before_ref, grad_ref):
            need(ref, part)

        def both(rows):
            mask = wide_mask(mask_ref, rows, size)
            pre = pre_ref[rows, span]
            summed = pre * scale[:, cut] + shift[:, cut] + silu(before_ref[rows, span]) * mask
            gate = logistic(summed)
            image_ref[rows, span] = (summed * gate * mask).astype(bf16)
            slope = gate * (1.0 + summed * (1.0 - gate))
            grad = grad_ref[rows, span].astype(f32) * mask * slope
            grad_sum_ref[rows, span] = grad
            return (grad, grad * ((pre - mean[:, cut]) * inverse[:, cut]))

        total_grad, total_prod = two_sums(pixels, size, both)
        sums.append(total_grad)
        prods.append(total_prod)
        flush(image_ref, part)
        flush(grad_sum_ref, part)
    write_copies(copies_ref, sums + prods)


def low_gradient(rows, width, start, grad, pre, mask, coefs):
    cut = slice(start, start + width)
    scale, mean_grad, mean_prod, mean = (part[:, cut] for part in coefs[:4])
    return scale * (grad - mask * (mean_grad + (pre - mean) * mean_prod))


def back_third_body(
    total_ref, grad_sum_ref, pre_ref, stats_ref, second_ref, second_stats_ref, mask_ref, count_ref,
    place_ref, gain_ref, bias_ref, expand_ref,
    low_ref, half_ref, grad_ref, copies_ref, result_ref,
):
    pixels, channels = pre_ref.shape
    width = second_ref.shape[1]
    total = read_copies(total_ref)
    coefs = grad_rows(
        total, stats_ref[...], gain_ref[:, 2 * width :], count_ref[0:1, 0:1], channels
    )
    result_ref[...] = jnp.concatenate(coefs[4:6], axis=0)
    for part, (start, size) in enumerate(spans_of(channels, 512)):
        span = pl.ds(start, size)
        need(grad_sum_ref, part)
        need(pre_ref, part)

        def step(rows, carry):
            mask = wide_mask(mask_ref, rows, size)
            low_ref[rows, span] = low_gradient(
                rows, size, start, grad_sum_ref[rows, span], pre_ref[rows, span], mask, coefs
            ).astype(bf16)
            return carry

        row_loop(pixels, step, 0)
        flush(low_ref, part)
    half = half_ref.shape[1]
    other = pl.multiple_of((1 - place_ref[0, 0]) * half, lane)
    half_ref[...] = low_ref[:, pl.ds(other, half)].astype(f32)
    flush(low_ref)
    flush(half_ref)
    for ref in (expand_ref, second_ref, second_stats_ref):
        need(ref)
    for start, size in spans_of(width, 256):
        grad_ref[:, start : start + size] = dot_nt(low_ref[...], expand_ref[start : start + size, :])
    norm_two_slope(grad_ref, second_ref, second_stats_ref, mask_ref, gain_ref, bias_ref, width, copies_ref)


def norm_two_slope(grad_ref, pre_ref, stats_ref, mask_ref, gain_ref, bias_ref, begin, copies_ref):
    pixels, width = pre_ref.shape
    mean, var = (stats_ref[0:1, :], stats_ref[1:2, :])
    inverse = lax.rsqrt(var + eps_norm)
    scale, shift = scale_shift(
        mean, var, gain_ref[:, begin : begin + width], bias_ref[:, begin : begin + width]
    )

    def both(rows):
        pre = pre_ref[rows, :]
        slope = silu_slope(pre * scale + shift)
        grad = grad_ref[rows, :] * slope * wide_mask(mask_ref, rows, width)
        grad_ref[rows, :] = grad
        return (grad, grad * ((pre - mean) * inverse))

    write_copies(copies_ref, two_sums(pixels, width, both))


def low_second(total_ref, grad_ref, pre_ref, stats_ref, mask_ref, count_ref, gain, low_ref, result_ref):
    pixels, width = pre_ref.shape
    total = read_copies(total_ref)
    coefs = grad_rows(total, stats_ref[...], gain, count_ref[0:1, 0:1], width)
    result_ref[...] = jnp.concatenate(coefs[4:6], axis=0)

    def step(rows, carry):
        mask = wide_mask(mask_ref, rows, width)
        low_ref[rows, :] = low_gradient(
            rows, width, 0, grad_ref[rows, :], pre_ref[rows, :], mask, coefs
        ).astype(bf16)
        return carry

    row_loop(pixels, step, 0)


def back_plain_body(
    total_ref, grad_in_ref, second_ref, second_stats_ref, first_ref, first_stats_ref, mask_ref,
    count_ref, place_ref, gain_ref, bias_ref, spatial_ref,
    low_ref, half_ref, grad_ref, copies_ref, result_ref,
    sums_ref,
):
    pixels, width = second_ref.shape
    side = 1 << ((pixels.bit_length() - 1) // 2)
    low_second(
        total_ref, grad_in_ref, second_ref, second_stats_ref, mask_ref, count_ref,
        gain_ref[:, width : 2 * width], low_ref, result_ref,
    )
    half = half_ref.shape[1]
    other = pl.multiple_of((1 - place_ref[0, 0]) * half, lane)
    half_ref[...] = low_ref[:, pl.ds(other, half)].astype(f32)
    flush(low_ref)
    flush(half_ref)
    need(spatial_ref)
    sums_ref[...] = jnp.zeros_like(sums_ref)
    for tap_index in range(9):
        tap_rows_out(
            sums_ref, tap_index, pixels, side, dot_nt(low_ref[...], spatial_ref[tap_index])
        )
    grad_ref[...] = fold_columns(sums_ref, pixels, side)
    norm_two_slope(grad_ref, first_ref, first_stats_ref, mask_ref, gain_ref, bias_ref, 0, copies_ref)


def back_deform_body(
    total_ref, grad_in_ref, second_ref, second_stats_ref, first_ref, first_stats_ref, mask_ref,
    count_ref, place_ref, gain_ref, bias_ref, spatial_ref, act_ref, offsets_ref, weights_ref,
    low_ref, half_ref, grad_ref, copies_ref, result_ref, grad_offsets_ref,
    sums_ref, padded_ref, shifted_ref,
):
    pixels, width = second_ref.shape
    side = 1 << ((pixels.bit_length() - 1) // 2)
    low_second(
        total_ref, grad_in_ref, second_ref, second_stats_ref, mask_ref, count_ref,
        gain_ref[:, width : 2 * width], low_ref, result_ref,
    )
    half = half_ref.shape[1]
    other = pl.multiple_of((1 - place_ref[0, 0]) * half, lane)
    half_ref[...] = low_ref[:, pl.ds(other, half)].astype(f32)
    flush(low_ref)
    flush(half_ref)
    for ref in (first_ref, first_stats_ref, spatial_ref, act_ref, offsets_ref, weights_ref):
        need(ref)
    offsets = offsets_ref[...]
    outs = offsets.shape[1]
    channel = lax.broadcasted_iota(jnp.int32, (pixels, outs), 1)
    moved = jnp.zeros((pixels, outs), f32)
    grad_ref[...] = jnp.zeros_like(grad_ref)
    for tap_index in range(9):
        dist_y, dist_x, bump_y, bump_x = tap_factors(offsets, tap_index, side)
        weight_y, weight_x = (bump_y * bump_y, bump_x * bump_x)
        sampling = (weight_y * weight_x).astype(bf16)
        piece = dot_nt(low_ref[...], spatial_ref[tap_index]).astype(bf16)
        grad_ref[...] = grad_ref[...] + dot_tn(sampling, piece)
        product = -4.0 * dot_nt(piece, act_ref[...])
        along_y = jnp.sum(product * (dist_y * bump_y * weight_x), axis=1, keepdims=True)
        along_x = jnp.sum(product * (dist_x * bump_x * weight_y), axis=1, keepdims=True)
        moved = moved + jnp.where(channel == 2 * tap_index, along_y, 0.0)
        moved = moved + jnp.where(channel == 2 * tap_index + 1, along_x, 0.0)
    moved_low = moved.astype(bf16)
    padded_ref[...] = jnp.zeros_like(padded_ref)
    padded_ref[pl.ds(2 * side, pixels), :] = act_ref[...].astype(f32)
    build_taps(padded_ref, shifted_ref, pixels, side)
    sums_ref[...] = jnp.zeros_like(sums_ref)
    grad_offsets_ref[...] = jnp.zeros_like(grad_offsets_ref)
    for tap_index in range(9):
        taps = tap_of(shifted_ref, tap_index, pixels, side)
        first = tap_index * outs
        grad_offsets_ref[first : first + outs, :] = dot_tn(moved_low, taps)
        tap_rows_out(
            sums_ref, tap_index, pixels, side, dot_nt(moved_low, weights_ref[tap_index])
        )
    grad_ref[...] = grad_ref[...] + fold_columns(sums_ref, pixels, side)
    norm_two_slope(grad_ref, first_ref, first_stats_ref, mask_ref, gain_ref, bias_ref, 0, copies_ref)


def back_between_body(
    total_ref, grad_ref, first_ref, first_stats_ref, grad_sum_ref, summed_ref, pre_ref, stats_ref,
    mask_ref, count_ref, gain_ref, squeeze_ref,
    low_ref, wide_ref, next_ref, copies_ref, result_ref,
):
    pixels, width = first_ref.shape
    channels = pre_ref.shape[1]
    low_second(
        total_ref, grad_ref, first_ref, first_stats_ref, mask_ref, count_ref,
        gain_ref[:, :width], low_ref, result_ref,
    )
    wide_ref[...] = low_ref[...].astype(f32)
    flush(low_ref)
    flush(wide_ref)
    need(stats_ref)
    need(squeeze_ref)
    mean, var = (stats_ref[0:1, :], stats_ref[1:2, :])
    inverse = lax.rsqrt(var + eps_norm)
    sums, prods = ([], [])
    for part, (start, size) in enumerate(spans_of(channels, 512)):
        span = pl.ds(start, size)
        cut = slice(start, start + size)
        for ref in (grad_sum_ref, summed_ref, pre_ref):
            need(ref, part)
        next_ref[:, span] = dot_nt(low_ref[...], squeeze_ref[start : start + size, :])

        def both(rows):
            mask = wide_mask(mask_ref, rows, size)
            slope = silu_slope(summed_ref[rows, span])
            grad = (next_ref[rows, span] + grad_sum_ref[rows, span]) * mask * slope
            next_ref[rows, span] = grad
            return (grad, grad * ((pre_ref[rows, span] - mean[:, cut]) * inverse[:, cut]))

        total_grad, total_prod = two_sums(pixels, size, both)
        sums.append(total_grad)
        prods.append(total_prod)
        flush(next_ref, part)
    write_copies(copies_ref, sums + prods)


def last_low_body(
    total_ref, grad_ref, first_ref, first_stats_ref, mask_ref, count_ref, gain_ref,
    low_ref, wide_ref, result_ref,
):
    width = first_ref.shape[1]
    low_second(
        total_ref, grad_ref, first_ref, first_stats_ref, mask_ref, count_ref,
        gain_ref[:, :width], low_ref, result_ref,
    )
    wide_ref[...] = low_ref[...].astype(f32)


def last_body(low_ref, grad_sum_ref, squeeze_ref, image_ref, token_ref):
    token_ref[...] = jnp.zeros_like(token_ref)
    for start, size in spans_of(image_ref.shape[1], 256):
        block = dot_nt(low_ref[...], squeeze_ref[start : start + size, :])
        image_ref[:, start : start + size] = (
            block + grad_sum_ref[:, start : start + size]
        ).astype(bf16)


def sum_copies_body(copies_ref, out_ref):
    total = jnp.sum(copies_ref[...], axis=0)

    def one_copy(step, carry):
        out_ref[step] = total
        return carry

    lax.fori_loop(0, out_ref.shape[0], one_copy, 0)


def offsets_body(sums_ref, out_ref, token_ref):
    token_ref[...] = jnp.zeros_like(token_ref)
    outs = out_ref.shape[1]
    for tap in range(out_ref.shape[0]):
        out_ref[tap] = sums_ref[tap * outs : (tap + 1) * outs, :]


block_cols = 256


def split_chunks(scratch_ref, keep_ref, send_ref, own, place, spot):
    for index in range(keep_ref.shape[0]):
        low = index & ((1 << place) - 1)
        base = ((index >> place) << (place + 1)) | low
        keep_ref[index, spot] = scratch_ref[base + own * (1 << place)]
        send_ref[index, spot] = scratch_ref[base + (1 - own) * (1 << place)]


def weights_body(kinds, firsts, spans, own_place_ref, *refs):
    groups = [refs[4 * place : 4 * place + 4] for place in range(len(kinds))]
    rest = refs[4 * len(kinds) :]
    results = 2 * len(spans) if firsts else 1
    outs, token_ref = (rest[:results], rest[results])
    chunks_ref, scratch = (rest[results + 1], list(rest[results + 2 :]))
    token_ref[...] = jnp.zeros_like(token_ref)
    count, depth, _ = chunks_ref.shape
    makers = []
    for kind, (rows_ref, rows_other_ref, cols_ref, cols_other_ref) in zip(kinds, groups):
        for ref in (rows_ref, rows_other_ref, cols_ref, cols_other_ref):
            need(ref)
        pixels, half = cols_other_ref.shape
        side = 1 << ((pixels.bit_length() - 1) // 2)
        both_cols = scratch.pop(0)
        start_own = pl.multiple_of(own_place_ref[0, 0] * half, lane)
        both_cols[pl.ds(0, pixels), :] = cols_ref[:, pl.ds(start_own, half)]
        both_cols[pl.ds(pixels, pixels), :] = cols_other_ref[...].astype(bf16)
        if kind == "rows":
            both_rows = scratch.pop(0)
            both_rows[pl.ds(0, pixels), :] = rows_ref[...]
            both_rows[pl.ds(pixels, pixels), :] = rows_other_ref[...].astype(bf16)
            for start in range(0, half, block_cols):
                makers.append(
                    lambda rows=both_rows, cols=both_cols, start=start: dot_tn(
                        rows[...], cols[:, start : start + block_cols]
                    )
                )
        elif kind == "plain":
            padded, taps = (scratch.pop(0), (scratch.pop(0), scratch.pop(0)))
            for source, shifted in zip((rows_ref, rows_other_ref), taps):
                padded[...] = jnp.zeros_like(padded)
                padded[pl.ds(2 * side, pixels), :] = source[...]
                build_taps(padded, shifted, pixels, side)
            for tap in range(9):
                makers.append(
                    lambda taps=taps, cols=both_cols, tap=tap, pixels=pixels, side=side: dot_tn(
                        tap_of(taps[0], tap, pixels, side), cols[pl.ds(0, pixels), :]
                    )
                    + dot_tn(tap_of(taps[1], tap, pixels, side), cols[pl.ds(pixels, pixels), :])
                )
        else:
            width = cols_ref.shape[1]
            for tap in range(9):
                span = slice(tap * width, (tap + 1) * width)
                makers.append(
                    lambda one=rows_ref, two=rows_other_ref, cols=both_cols, span=span, pixels=pixels: dot_tn(
                        one[:, span], cols[pl.ds(0, pixels), :]
                    )
                    + dot_tn(two[:, span], cols[pl.ds(pixels, pixels), :])
                )
    if not firsts:
        for part, maker in enumerate(makers):
            outs[0][:, part] = maker().reshape(count, depth, block_cols)
        return
    for stream, (start, stop) in enumerate(spans):
        bit = firsts[stream]
        own = own_place_ref[0, bit]
        for part in range(start, stop):
            chunks_ref[...] = makers[part]().reshape(count, depth, block_cols)
            split_chunks(
                chunks_ref, outs[2 * stream], outs[2 * stream + 1], own, bit - 1, part - start
            )
        flush(outs[2 * stream + 1])
        flush(outs[2 * stream])


def advance_body(groups, own_place_ref, *refs):
    streams = sum(count for count, _ in groups)
    kept, came = (refs[:streams], refs[streams : 2 * streams])
    outs = list(refs[2 * streams :])
    token_ref = outs.pop()
    token_ref[...] = jnp.zeros_like(token_ref)
    at, used, start = (0, 0, 0)
    for count, spot in groups:
        members = list(range(at, at + count))
        at += count
        for stream in members:
            need(kept[stream])
            need(came[stream])
        if spot is None:
            for stream in members:
                stop = start + kept[stream].shape[1]
                outs[-1][start:stop] = kept[stream][0] + came[stream][0]
                start = stop
            continue
        bit, place = spot
        own = own_place_ref[0, bit]
        for target_ref, side in ((outs[used + 1], 1 - own), (outs[used], own)):
            first = 0
            for stream in members:
                stop = first + kept[stream].shape[1]
                for index in range(target_ref.shape[0]):
                    low = index & ((1 << place) - 1)
                    base = ((index >> place) << (place + 1)) | low
                    chunk = base + side * (1 << place)
                    target_ref[index, first:stop] = kept[stream][chunk] + came[stream][chunk]
                first = stop
            flush(target_ref)
        used += 2


def assemble_body(kinds, labels, summed, own_place_ref, own_ref, pair_ref, side_ref, both_ref, *targets):
    targets[-1][...] = jnp.zeros_like(targets[-1])
    targets = targets[:-1]
    rows, cols = own_ref.shape[-2:]
    pair, line = (own_place_ref[0, 0], own_place_ref[0, 1])
    for row_at, col_at in ((0, 0), (0, 1), (1, 0), (1, 1)):
        if summed and row_at:
            continue
        same_row, same_col = (line == row_at, pair == col_at)
        row_span = slice(row_at * rows, (row_at + 1) * rows)
        for part, (place, step) in enumerate(labels):
            near = jnp.where(same_col, own_ref[part], pair_ref[part])
            far = jnp.where(same_col, side_ref[part], both_ref[part])
            value = near + far if summed else jnp.where(same_row, near, far)
            target = targets[place]
            if kinds[place] == "rows":
                parts = target.shape[1] // 2 // cols
                at = (col_at * parts + step) * cols
                target[row_span, at : at + cols] = value
            else:
                target[step, row_span, col_at * cols : (col_at + 1) * cols] = value
    for target in targets:
        flush(target)


def gate_body(*refs):
    pass


def gate(arrays, after):
    hbm = pl.BlockSpec(memory_space=pltpu.HBM)
    return pl.pallas_call(
        gate_body,
        out_shape=tuple(shape_of(part.shape) for part in arrays),
        in_specs=[hbm] * len(arrays) + [pl.BlockSpec(memory_space=pl.ANY)] * len(after),
        out_specs=(hbm,) * len(arrays),
        input_output_aliases={place: place for place in range(len(arrays))},
    )(*arrays, *after)


class Comm:
    def __init__(self, wide_size, narrow_size):
        self.total = wide_size * narrow_size
        self.bits = self.total.bit_length() - 1
        self.low = narrow_size.bit_length() - 1
        self.index = lax.axis_index("wide") * narrow_size + lax.axis_index("narrow")
        self.places = jnp.stack([self.bit(place) for place in range(self.bits)])[None, :]

    def bit(self, place):
        return (self.index >> place) & 1

    def swap_over(self, values, flips):
        pairs = [(source, source ^ flips) for source in range(self.total)]
        return lax.ppermute(values, axes, pairs)

    def swap(self, values, place):
        return self.swap_over(values, 1 << place)

    def sync(self, copies):
        return Near(lax.all_to_all(copies, axes, 0, 0, tiled=True))

    def order(self, letters):
        named = {"y": 1, "x": self.low, "a": self.low + 1, "b": self.low + 2}
        return [named[letter] for letter in letters] + list(range(self.low + 3, self.bits))


token = (8, lane)


class Group:
    def __init__(self, comm, total, plan):
        self.comm = comm
        self.orders = [comm.order(letters) for letters, _ in plan]
        self.left = [
            [place for place in range(1, comm.bits) if place != order[0]] for order in self.orders
        ]
        shares = [share for _, share in plan]
        ends = [total * sum(shares[: at + 1]) // sum(shares) for at in range(len(plan))]
        self.bounds = tuple(zip([0] + ends[:-1], ends))
        self.total = total
        self.arrays = {}
        self.labels = []
        self.kinds = ()
        self.shapes = []
        self.at = 1

    def add(self, kind, group, after=()):
        comm = self.comm
        pixels, rows = group[0].shape
        if kind == "given":
            rows = group[2].shape[1]
        chunks = 1 << (comm.bits - 1 if self.orders else comm.bits - comm.low)
        depth = rows // chunks
        half = getattr(group[3], "value", group[3]).shape[1]
        side = 1 << ((pixels.bit_length() - 1) // 2)
        scratch = [pltpu.VMEM((chunks, depth, block_cols), f32), pltpu.VMEM((2 * pixels, half), bf16)]
        wide_depth = rows >> (comm.bits - comm.low)
        self.shapes.append((wide_depth, 2 * half) if kind == "rows" else (9, wide_depth, 2 * half))
        if kind == "rows":
            scratch.append(pltpu.VMEM((2 * pixels, rows), bf16))
        if kind == "plain":
            scratch.append(pltpu.VMEM((pixels + 4 * side, rows), f32))
            scratch += [pltpu.VMEM((3, pixels + 4 * side, rows), bf16)] * 2
        count = half // block_cols if kind == "rows" else 9
        begin = len(self.labels)
        self.labels += [(len(self.kinds), step) for step in range(count)]
        self.kinds += (kind,)
        keys, spans, outs, pieces, begun = ([], [], [], {}, {})
        if not self.orders:
            if self.arrays:
                begun[0] = self.arrays[0, 0]
            pieces[0] = (begin, count)
            outs.append(shape_of((chunks, self.total, depth, block_cols)))
        for stream, (start, stop) in enumerate(self.bounds):
            low, high = (max(start, begin), min(stop, begin + count))
            if low >= high:
                continue
            spans.append((low - begin, high - begin))
            keys.append(stream)
            for which in range(2):
                if (stream, which) in self.arrays:
                    begun[len(outs)] = self.arrays[stream, which]
                pieces[len(outs)] = (low - start, high - low)
                outs.append(shape_of((chunks // 2, stop - start, depth, block_cols)))
        args = (comm.places,) + tuple(group)
        made = call(
            functools.partial(
                weights_body, (kind,), tuple(self.orders[stream][0] for stream in keys), tuple(spans)
            ),
            outs + [shape_of(token)], args, (0,), scratch, after, tuple(range(1, len(args))),
            pieces=pieces, begun=begun,
        )
        if not self.orders:
            self.arrays[0, 0] = made[0]
        for number, stream in enumerate(keys):
            self.arrays[stream, 0] = made[2 * number]
            self.arrays[stream, 1] = made[2 * number + 1]
        return made[-1]

    def offload(self):
        self.share = lax.psum_scatter(self.arrays[0, 0], "wide", scatter_dimension=0, tiled=True)

    def collect(self, after):
        (share,) = gate((self.share.reshape(self.share.shape[1:]),), after)
        self.join(share)

    def join(self, share):
        beside = self.comm.swap(share, 1)
        self.quarters = [share, self.comm.swap(share, 0), beside, self.comm.swap(beside, 0)]

    def start(self, after=()):
        sent = [self.arrays[stream, 1] for stream in range(len(self.orders))]
        sent = gate(sent, after) if after else sent
        self.streams = [
            [(self.arrays[stream, 0], self.comm.swap(sent[stream], order[0]))]
            for stream, order in enumerate(self.orders)
        ]

    def advance(self, after=()):
        comm = self.comm
        if len({tuple(order[self.at :]) for order in self.orders}) == 1:
            self.orders, self.left = (self.orders[:1], self.left[:1])
            self.streams = [sum(self.streams, [])]
        groups, outs = ([], [])
        last = self.at == len(self.orders[0])
        total = 0
        for order, left, members in zip(self.orders, self.left, self.streams):
            spot = None
            parts = sum(kept.shape[1] for kept, _ in members)
            shape = members[0][0].shape
            total += parts
            if not last:
                bit = order[self.at]
                spot = (bit, left.index(bit))
                left.remove(bit)
                outs += [shape_of((shape[0] // 2, parts) + shape[2:])] * 2
            groups.append((len(members), spot))
        if last:
            outs = [shape_of((total,) + shape[2:])]
        flat = [pair for members in self.streams for pair in members]
        *pieces, mark = call(
            functools.partial(advance_body, tuple(groups)),
            outs + [shape_of(token)],
            (comm.places, *(kept for kept, _ in flat), *(Near(came) for _, came in flat)),
            (0,), (), after, tuple(range(1, 1 + 2 * len(flat))),
        )
        if last:
            self.join(pieces[0])
        else:
            self.streams = [
                [(pieces[2 * place], comm.swap(pieces[2 * place + 1], order[self.at]))]
                for place, order in enumerate(self.orders)
            ]
        self.at += 1
        return mark

    def ended(self):
        return self.at > len(self.orders[0])

    def finish(self, after=()):
        while self.orders and not self.ended():
            self.advance(after)
        kinds, shapes = (self.kinds, self.shapes)
        outs = [shape_of(shape) for shape in shapes]
        *results, self.token = call(
            functools.partial(assemble_body, kinds, tuple(self.labels), not self.orders),
            outs + [shape_of(token)], (self.comm.places, self.quarters[0], *(Near(part) for part in self.quarters[1:])), (0,), (), after,
        )
        return results


def per_device(
    wide_size, narrow_size, images, image_sizes, offset_shift, squeeze_one, offsets_one, spatial_one,
    expand_one, squeeze_two, spatial_two, expand_two, norm_gain_one, norm_bias_one, norm_gain_two,
    norm_bias_two, run_mean_one, run_var_one, run_mean_two, run_var_two, grad_output,
):
    comm = Comm(wide_size, narrow_size)
    side, channels = (images.shape[1], images.shape[3])
    pixels = side * side
    width = squeeze_one.shape[1]
    outs = offsets_one.shape[2]
    total = comm.total
    small = (total, 2 * width // lane, lane)
    quarters = channels // 512
    large = (total, 2 * channels // lane, lane)
    flat = images.reshape(pixels, channels)
    grad_out = grad_output.reshape(pixels, channels)
    gain_one, bias_one = (norm_gain_one[None, :], norm_bias_one[None, :])
    gain_two, bias_two = (norm_gain_two[None, :], norm_bias_two[None, :])
    field = shape_of((pixels, width))
    field_low = shape_of((pixels, width), bf16)
    plane = shape_of((pixels, channels))
    plane_low = shape_of((pixels, channels), bf16)
    half_plane = shape_of((pixels, channels // 2))
    half_field = shape_of((pixels, width // 2))
    stats_small, stats_large = (shape_of((2, width)), shape_of((2, channels)))
    padded = pltpu.VMEM((pixels + 4 * side, width), f32)
    shifted = pltpu.VMEM((3, pixels + 4 * side, width), bf16)
    tap_sums = pltpu.VMEM((3, pixels + 4 * side, width), f32)

    first_one, mask, copies, images_half = call(
        first_body,
        (field, shape_of((pixels, lane)), shape_of((total, 2 * width // lane + 8, lane)), half_plane),
        (image_sizes, comm.places, flat, squeeze_one),
        (0, 1),
    )
    images_half = comm.swap(images_half, 0)
    copies = comm.sync(copies)
    (act_one, act_wide, columns, offsets, second_one, copies, first_stats_one, count) = call(
        deform_body,
        (
            field_low, field, shape_of((pixels, 9 * width), bf16),
            shape_of((pixels, outs)), field, shape_of(small), stats_small, shape_of((8, lane)),
        ),
        (
            copies, first_one, mask, gain_one, bias_one, offsets_one,
            offset_shift.astype(f32)[None, :], spatial_one,
        ),
        (),
        (padded, shifted),
        (),
        (5, 7), blocks_out={2: 9},
    )
    act_other, offsets_other = (comm.swap(act_wide, 0), comm.swap(offsets, 0))
    copies = comm.sync(copies)
    act_second_one, act_second_wide_one, third_one, copies, second_stats_one = call(
        third_body,
        (field_low, field, plane, shape_of(large), stats_small),
        (copies, second_one, mask, count, gain_one, bias_one, expand_one),
        blocks={6: quarters}, blocks_out={2: quarters},
    )
    (columns_other,) = call(
        columns_body, (shape_of((pixels, 9 * width), bf16),),
        (Near(act_other), Near(offsets_other)), (), (pltpu.VMEM((pixels, width), bf16),), (second_stats_one,),
    )
    act_second_wide_one = comm.swap(act_second_wide_one, 0)
    copies = comm.sync(copies)
    summed_one, low_two, low_half, first_two, copies, third_stats_one = call(
        between_body,
        (plane, plane_low, half_plane, field, shape_of(small), stats_large),
        (copies, third_one, flat, mask, count, comm.places, gain_one, bias_one, squeeze_two),
        (5,), (), (columns_other,), (8,),
        blocks={1: quarters, 2: quarters}, blocks_out={0: quarters, 1: quarters},
    )
    low_half = comm.swap(low_half, 0)
    copies = comm.sync(copies)
    act_wide_two, second_two, copies, first_stats_two = call(
        plain_body,
        (field, field, shape_of(small), stats_small),
        (copies, first_two, mask, count, gain_two, bias_two, spatial_two),
        (),
        (padded, shifted), late=(6,),
    )
    act_wide_two_other = comm.swap(act_wide_two, 0)
    copies = comm.sync(copies)
    act_second_two, act_second_wide_two, third_two, copies, second_stats_two = call(
        third_body,
        (field_low, field, plane, shape_of(large), stats_small),
        (copies, second_two, mask, count, gain_two, bias_two, expand_two),
        blocks={6: quarters}, blocks_out={2: quarters},
    )
    act_second_wide_two = comm.swap(act_second_wide_two, 0)
    copies = comm.sync(copies)
    output_images, grad_sum_two, copies, third_stats_two = call(
        turn_body,
        (plane_low, plane, shape_of(large), stats_large),
        (copies, third_two, summed_one, grad_out, mask, count, gain_two, bias_two),
        blocks={1: quarters, 2: quarters, 3: quarters}, blocks_out={0: quarters, 1: quarters},
    )
    copies = comm.sync(copies)
    low_third_two, third_half, grad_second_two, copies, third_result_two = call(
        back_third_body,
        (plane_low, half_plane, field, shape_of(small), stats_large),
        (
            copies, grad_sum_two, third_two, third_stats_two, second_two, second_stats_two, mask, count,
            comm.places, gain_two, bias_two, expand_two,
        ),
        (8,), late=(4, 5, 11), blocks={1: quarters, 2: quarters}, blocks_out={0: quarters},
    )
    third_half = comm.swap(third_half, 0)
    copies = comm.sync(copies)
    blocks = channels // 2 // block_cols
    plan = (("xayb", 6), ("yxab", 6), ("ayxb", 5))
    group_two = Group(comm, 2 * blocks + 9, plan)
    group_one = Group(comm, 2 * blocks + 9, (("xayb", 7), ("yxab", 7), ("ayxb", 3)))
    done = group_two.add("rows", (act_second_two, act_second_wide_two, low_third_two, Near(third_half)))
    low_second_two, second_half, grad_first_two, copies, second_result_two = call(
        back_plain_body,
        (field_low, half_field, field, shape_of(small), stats_small),
        (
            copies, grad_second_two, second_two, second_stats_two, first_two, first_stats_two, mask,
            count, comm.places, gain_two, bias_two, spatial_two,
        ),
        (8,),
        (tap_sums,),
        (done,),
        (11,),
    )
    second_half = comm.swap(second_half, 0)
    copies = comm.sync(copies)
    done = group_two.add("plain", (act_wide_two, act_wide_two_other, low_second_two, Near(second_half)))
    low_first_two, low_first_wide, grad_sum_one, copies, first_result_two = call(
        back_between_body,
        (field_low, field, plane, shape_of(large), stats_small),
        (
            copies, grad_first_two, first_two, first_stats_two, grad_sum_two, summed_one, third_one,
            third_stats_one, mask, count, gain_two, squeeze_two,
        ),
        (),
        (),
        (done,),
        (4, 5, 6, 7, 11),
        blocks={4: quarters, 5: quarters, 6: quarters}, blocks_out={2: quarters},
    )
    low_first_wide = comm.swap(low_first_wide, 0)
    copies = comm.sync(copies)
    done = group_two.add("rows", (low_first_two, Near(low_first_wide), low_two, low_half))
    low_third_one, third_half, grad_second_one, copies, third_result_one = call(
        back_third_body,
        (plane_low, half_plane, field, shape_of(small), stats_large),
        (
            copies, grad_sum_one, third_one, third_stats_one, second_one, second_stats_one, mask, count,
            comm.places, gain_one, bias_one, expand_one,
        ),
        (8,),
        (),
        (done,),
        (4, 5, 11),
        blocks={1: quarters, 2: quarters}, blocks_out={0: quarters},
    )
    third_half = comm.swap(third_half, 0)
    copies = comm.sync(copies)
    done = group_one.add("rows", (act_second_one, act_second_wide_one, low_third_one, Near(third_half)))
    group_two.start((copies.value, done))
    slots = -(-9 * outs // total)
    slots = -(-slots // 8) * 8
    low_second_one, second_half, grad_first_one, copies, second_result_one, grad_offsets = call(
        back_deform_body,
        (
            field_low, half_field, field, shape_of(small), stats_small, shape_of((total * slots, width)),
        ),
        (
            copies, grad_second_one, second_one, second_stats_one, first_one, first_stats_one, mask,
            count, comm.places, gain_one, bias_one, spatial_one, act_one, offsets, offsets_one,
        ),
        (8,),
        (tap_sums, padded, shifted),
        (done,),
        (4, 5, 11, 12, 13, 14),
    )
    second_half = comm.swap(second_half, 0)
    copies = comm.sync(copies)
    done = group_one.add("given", (columns, columns_other, low_second_one, Near(second_half)))
    done = group_two.advance((done,))
    low_first_one, low_first_wide, first_result_one = call(
        last_low_body,
        (field_low, field, stats_small),
        (copies, grad_first_one, first_one, first_stats_one, mask, count, gain_one),
        (), (), (done,),
    )
    low_first_wide = comm.swap(low_first_wide, 0)
    grad_offsets = comm.sync(grad_offsets.reshape(total, slots, width))
    done = group_one.add(
        "rows", (low_first_one, Near(low_first_wide), flat, images_half), (first_result_one, done)
    )
    done = group_two.advance((done,))
    grad_images, done = call(
        last_body,
        (plane_low, shape_of(token)),
        (low_first_one, grad_sum_one, squeeze_one),
        (), (), (done,),
    )
    done = group_two.advance((done, grad_offsets.value))
    group_one.start((done,))
    (grad_offsets,) = call(
        sum_copies_body, (shape_of((total, slots, width)),), (grad_offsets,), (), (),
        (done,),
    )
    grad_offsets = comm.sync(grad_offsets).value
    done = group_two.advance((done,))
    done = group_one.advance((done,))
    grad_offsets, done = call(
        offsets_body, (shape_of((9, outs, width)), shape_of(token)),
        (grad_offsets.reshape(total * slots, width),), (), (), (done,),
    )
    done = group_one.advance((done,))
    done = group_one.advance((done,))
    grad_expand_two, grad_spatial_two, grad_squeeze_two = group_two.finish((done,))
    grad_expand_one, grad_spatial_one, grad_squeeze_one = group_one.finish((group_two.token,))

    def laid(parts, row):
        return jnp.concatenate([part[row] for part in parts])

    results_one = (first_result_one, second_result_one, third_result_one)
    results_two = (first_result_two, second_result_two, third_result_two)
    stats_one = (first_stats_one, second_stats_one, third_stats_one)
    stats_two = (first_stats_two, second_stats_two, third_stats_two)
    pixel_count = count[0, 0]
    unbias = pixel_count / (pixel_count - 1.0)
    fresh = 1.0 - keep_rate
    return (
        output_images.reshape(images.shape),
        grad_images.reshape(images.shape),
        grad_squeeze_one.T,
        grad_offsets.transpose(0, 2, 1),
        grad_spatial_one,
        grad_expand_one,
        grad_squeeze_two.T,
        grad_spatial_two,
        grad_expand_two,
        laid(results_one, 1),
        laid(results_one, 0),
        laid(results_two, 1),
        laid(results_two, 0),
        keep_rate * run_mean_one + fresh * laid(stats_one, 0),
        keep_rate * run_var_one + fresh * laid(stats_one, 1) * unbias,
        keep_rate * run_mean_two + fresh * laid(stats_two, 0),
        keep_rate * run_var_two + fresh * laid(stats_two, 1) * unbias,
    )


def solution(mesh):
    images_spec = P(axes, None, None, None)
    whole = P()
    return jax.shard_map(
        functools.partial(per_device, mesh.shape["wide"], mesh.shape["narrow"]),
        mesh=mesh,
        in_specs=(images_spec, P(axes, None)) + (whole,) * 16 + (images_spec,),
        out_specs=(
            images_spec,
            images_spec,
            P(None, "wide"),
            whole,
            P(None, "wide", None),
            P("wide", None),
            P(None, "wide"),
            P(None, "wide", None),
            P("wide", None),
        )
        + (whole,) * 8,
        check_vma=False,
    )
```
